32 devices in a mesh: seq: 8 (over y, x, core), feat: 4 (over z).
Axes of the slice: x: 2, y: 2, z: 4, core: 2. Of those that a mesh axis runs over, the one named last changes fastest.
Arguments:
- tokens: bfloat16 [2, 6144, 2048], P(None, 'seq'), may hold values from -6 to 6
- cotangent: bfloat16 [2, 6144, 2048], P(None, 'seq'), may hold values from -6 to 6
- lengths: int32 [2, 3], replicated, may hold values from 96 to 5760, as said below
- w_query: bfloat16 [2048, 256], P('seq', 'feat'), may hold values from -0.125 to 0.125
- w_key: bfloat16 [2048, 256], P('seq', 'feat'), may hold values from -0.125 to 0.125
- w_value: bfloat16 [2048, 2048], P('seq', 'feat'), may hold values from -0.125 to 0.125
- w_output: bfloat16 [2048, 2048], P('seq', 'feat'), may hold values from -6 to 6
- w_gate: bfloat16 [2048, 5504], P('seq', 'feat'), may hold values from -0.125 to 0.125
- w_up: bfloat16 [2048, 5504], P('seq', 'feat'), may hold values from -0.125 to 0.125
- w_down: bfloat16 [5504, 2048], P('feat', 'seq'), may hold values from -0.078125 to 0.078125
- gain_mixer: bfloat16 [2048], P('seq'), may hold values from 0.099609375 to 1.8984375
- gain_mlp: bfloat16 [2048], P('seq'), may hold values from 0.099609375 to 1.8984375
Outputs:
- mixed: bfloat16 [2, 6144, 2048], P(None, 'seq', 'feat')
- input_grad: float32 [2, 6144, 2048], P(None, 'seq')
- grad_query: float32 [2048, 256], P('seq', 'feat')
- grad_key: float32 [2048, 256], P('seq', 'feat')
- grad_value: float32 [2048, 2048], P('seq', 'feat')
- grad_output: float32 [2048, 2048], P('seq', 'feat')
- grad_gate: float32 [2048, 5504], P('seq', 'feat')
- grad_up: float32 [2048, 5504], P('seq', 'feat')
- grad_down: float32 [5504, 2048], P('feat', 'seq')
- grad_gain_mixer: float32 [2048], P('seq')
- grad_gain_mlp: float32 [2048], P('seq')
The draws below stay inside these ranges and needn't reach their ends.
Inputs may be any that keep to these rules, and one draw needn't show every extreme that they name: `lengths`: in each micro-batch the first document lies within the first 768 slots, the second reaches into the last 768 slots, and the slots after the three documents are padding, at least one and fewer than 768.
All inputs are finite; a program needn't handle non-finite values.
Results may differ from the reference program's by a relative error of at most 0.03.
Values may be sent and summed in bfloat16 or wider, within the bound.
No kernel may reach another device: no remote copies, remote signals or barrier semaphores. Data moves between devices by JAX's collectives and lax.ppermute only.
A program may use at most 256 MiB of HBM per device.

```python
import jax
import jax.numpy as jnp
import numpy as np
from jax import lax

D = 2048
HEADS = 16
HEAD_V = 128
QK = 16
FF = 5504
FEATS = 288
MB = 2
TOK_DEV = 768
TOK_MB = 6144


def draw_lengths(key, part):
    key = jax.random.fold_in(key, 7)
    first_key, third_key, padding_key = jax.random.split(key, 3)
    first_len = jax.random.randint(first_key, (MB,), TOK_DEV // 4, 3 * TOK_DEV // 4)
    third_len = jax.random.randint(third_key, (MB,), TOK_DEV // 8, 3 * TOK_DEV // 8)
    padding = jax.random.randint(padding_key, (MB,), TOK_DEV // 8, 3 * TOK_DEV // 8)
    second_len = TOK_MB - first_len - third_len - padding
    return jnp.stack([first_len, second_len, third_len], axis=1).astype(jnp.int32)


def shard_levels(own_key, dims, cuts, smallest, largest):
    factor_of, own = 1.0, jax.random.fold_in(own_key, 6)
    for dim, blocks in cuts:
        heights = jnp.exp(jax.random.uniform(jax.random.fold_in(own, dim), (blocks,), jnp.float32, smallest / len(cuts), largest / len(cuts)))
        factor_of = factor_of * jnp.repeat(heights, dims[dim] // blocks).reshape([-1 if axis == dim else 1 for axis in range(len(dims))])
    return factor_of


def scatter_about(own_key, dims, width, reach, pieces=(), held_as=jnp.bfloat16):
    gain = shard_levels(own_key, dims, pieces, -0.22, 0.18) if pieces else 1.0
    values = jax.random.normal(own_key, dims, jnp.float32) * width * gain
    return jnp.minimum(jnp.maximum(values, -reach), reach).astype(held_as)


def setup_inputs(seed: int = 0) -> dict:
    splits = jax.random.split(jax.random.key(seed), 13)
    return {
        "tokens": scatter_about(splits[0], (MB, TOK_MB, D), 1.0, 6.0, ((1, 8),)),
        "cotangent": scatter_about(splits[1], (MB, TOK_MB, D), 1.0, 6.0, ((1, 8),)),
        "lengths": draw_lengths(jax.random.fold_in(splits[12], 71), 0),
        "w_query": scatter_about(splits[3], (D, HEADS * QK), D ** -0.5, 0.125, ((0, 8), (1, 4))),
        "w_key": scatter_about(splits[4], (D, HEADS * QK), D ** -0.5, 0.125, ((0, 8), (1, 4))),
        "w_value": scatter_about(splits[5], (D, HEADS * HEAD_V), D ** -0.5, 0.125, ((0, 8), (1, 4))),
        "w_output": scatter_about(splits[6], (HEADS * HEAD_V, D), 1 ** -0.5, 6.0, ((0, 8), (1, 4))),
        "w_gate": scatter_about(splits[7], (D, FF), D ** -0.5, 0.125, ((0, 8), (1, 4))),
        "w_up": scatter_about(splits[8], (D, FF), D ** -0.5, 0.125, ((0, 8), (1, 4))),
        "w_down": scatter_about(splits[9], (FF, D), FF ** -0.5, 0.078125, ((0, 4), (1, 8))),
        "gain_mixer": jnp.clip(1.0 + 0.18 * jax.random.normal(splits[10], (D,), jnp.float32), 0.099609375, 1.8984375).astype(jnp.bfloat16),
        "gain_mlp": jnp.clip(1.0 + 0.18 * jax.random.normal(splits[11], (D,), jnp.float32), 0.099609375, 1.8984375).astype(jnp.bfloat16),
    }


EPS = 1e-05
HIGH = lax.Precision.HIGHEST

@jax.custom_vjp
def low(v):
    return lax.optimization_barrier(v.astype(jnp.bfloat16)).astype(jnp.float32)

@jax.custom_vjp
def low_back(v):
    return v

def low_keep(v):
    return (low(v), None)

def low_pass(kept, grad):
    return (grad,)

def back_keep(v):
    return (v, None)

def back_low(kept, grad):
    return (low(grad),)
low.defvjp(low_keep, low_pass)
low_back.defvjp(back_keep, back_low)

def feature_tables():
    left_list = [0] + list(range(1, QK + 1)) + [left_idx + 1 for left_idx in range(QK) for right_idx in range(QK)]
    right_list = [0] * (QK + 1) + [right_idx + 1 for left_idx in range(QK) for right_idx in range(QK)]
    scale_list = [1.0] * (QK + 1) + [0.7071067811865476] * (QK * QK)
    padding = FEATS - len(left_list)
    left_list = left_list + [0] * padding
    right_list = right_list + [0] * padding
    scale_list = scale_list + [0.0] * padding
    pick_left = (np.arange(QK + 1)[:, None] == np.array(left_list)[None, :]).astype(np.float32)
    pick_right = (np.arange(QK + 1)[:, None] == np.array(right_list)[None, :]).astype(np.float32)
    return (pick_left, pick_right, np.array(scale_list, np.float32))

def feature_map(heads_in):
    pick_left, pick_right, scale_row = feature_tables()
    ftype = heads_in.dtype
    extended = jnp.concatenate([jnp.ones(heads_in.shape[:-1] + (1,), ftype), 0.5 * heads_in], axis=-1)
    left_part = jnp.einsum('thi,ij->thj', extended, jnp.asarray(pick_left, ftype), precision=HIGH)
    right_part = jnp.einsum('thi,ij->thj', extended, jnp.asarray(pick_right, ftype), precision=HIGH)
    return jnp.asarray(scale_row, ftype) * left_part * right_part

def micro_batch(params, tokens_f, lengths_row):
    w_query, w_key, w_value, w_output, w_gate, w_up, w_down, gain_mixer, gain_mlp = params
    ftype = tokens_f.dtype
    blocks = TOK_MB // TOK_DEV
    positions = jnp.arange(TOK_MB, dtype=jnp.int32)
    bounds = jnp.cumsum(lengths_row).astype(jnp.int32)
    segment = lax.optimization_barrier(jnp.sum((positions[:, None] >= bounds[None, :]).astype(jnp.int32), axis=1))
    valid = segment < 3
    block_first = (jnp.arange(blocks, dtype=jnp.int32) * TOK_DEV).astype(jnp.int32)
    before = lax.optimization_barrier(jnp.sum((block_first[:, None] - 1 >= bounds[None, :]).astype(jnp.int32), axis=1))
    before = jnp.where(block_first == 0, -1, before).astype(jnp.int32)
    inv_one = lax.rsqrt(lax.optimization_barrier(jnp.mean(tokens_f * tokens_f, axis=-1, keepdims=True)) + EPS)
    normed = low(tokens_f * inv_one * gain_mixer)
    query = low_back(low(jnp.dot(normed, w_query, precision=HIGH)))
    keys = low_back(low(jnp.dot(normed, w_key, precision=HIGH)))
    values = low_back(low(jnp.dot(normed, w_value, precision=HIGH)))
    feat_q = low(feature_map(query.reshape(TOK_MB, HEADS, QK)))
    feat_k = low(feature_map(keys.reshape(TOK_MB, HEADS, QK)))
    values_h = values.reshape(TOK_MB, HEADS, HEAD_V)

    def block_step(carry, inputs):
        state, state_sum = carry
        block_q, block_k, block_v, block_seg, block_valid, prev_seg = inputs
        order = jnp.arange(TOK_DEV)
        mask = (order[None, :] <= order[:, None]) & (block_seg[None, :] == block_seg[:, None]) & block_valid[None, :]
        scores = jnp.einsum('thf,shf->hts', block_q, block_k, precision=HIGH) * mask.astype(ftype)[None]
        scores = low_back(low(scores))
        use = (block_valid & (block_seg == prev_seg)).astype(ftype)
        tail = (block_valid & (block_seg == block_seg[-1])).astype(ftype)
        flag = (block_seg[-1] != prev_seg).astype(ftype)
        numer = jnp.einsum('hts,shc->thc', scores, block_v, precision=HIGH)
        numer = numer + use[:, None, None] * jnp.einsum('thf,hfc->thc', block_q, low(state), precision=HIGH)
        denom = lax.optimization_barrier(jnp.sum(scores, axis=2)).T + use[:, None] * jnp.einsum('thf,hf->th', block_q, state_sum, precision=HIGH)
        tail_k = block_k * tail[:, None, None]
        local_state = low_back(jnp.einsum('shf,shc->hfc', tail_k, block_v, precision=HIGH))
        local_sum = lax.optimization_barrier(jnp.sum(tail_k, axis=0))
        new_state = local_state + (1.0 - flag) * state
        new_sum = local_sum + (1.0 - flag) * state_sum
        return ((new_state, new_sum), (numer, denom))
    inputs = (feat_q.reshape(blocks, TOK_DEV, HEADS, FEATS), feat_k.reshape(blocks, TOK_DEV, HEADS, FEATS), values_h.reshape(blocks, TOK_DEV, HEADS, HEAD_V), segment.reshape(blocks, TOK_DEV), valid.reshape(blocks, TOK_DEV), before)
    start_carry = (jnp.zeros((HEADS, FEATS, HEAD_V), ftype), jnp.zeros((HEADS, FEATS), ftype))
    ignored, (numer, denom) = lax.scan(jax.checkpoint(block_step), start_carry, inputs)
    numer = low_back(numer.reshape(TOK_MB, HEADS, HEAD_V))
    denom = denom.reshape(TOK_MB, HEADS) + (1.0 - valid.astype(ftype))[:, None]
    mixer_in = low(numer / denom[:, :, None]).reshape(TOK_MB, HEADS * HEAD_V)
    branch = low_back(low(jnp.dot(mixer_in, w_output, precision=HIGH)))
    hidden_state = tokens_f + branch
    inv_two = lax.rsqrt(lax.optimization_barrier(jnp.mean(hidden_state * hidden_state, axis=-1, keepdims=True)) + EPS)
    normed_two = low(hidden_state * inv_two * gain_mlp)
    gate = low_back(jnp.dot(normed_two, w_gate, precision=HIGH))
    upward = low_back(jnp.dot(normed_two, w_up, precision=HIGH))
    hidden = low(jax.nn.silu(gate) * upward)
    return hidden_state + jnp.dot(hidden, w_down, precision=HIGH)

def forward(params, tokens_f, lengths):
    return jnp.stack([micro_batch(params, tokens_f[batch_number], lengths[batch_number]) for batch_number in range(MB)])

def reference(tokens, cotangent, lengths, w_query, w_key, w_value, w_output, w_gate, w_up, w_down, gain_mixer, gain_mlp):
    params = tuple((each_weight.astype(jnp.float32) for each_weight in (w_query, w_key, w_value, w_output, w_gate, w_up, w_down, gain_mixer, gain_mlp)))
    tokens_f = tokens.astype(jnp.float32)
    mixed, pullback = jax.vjp(lambda weights_in, tokens_in: forward(weights_in, tokens_in, lengths), params, tokens_f)
    grads, input_grad = pullback(cotangent.astype(jnp.float32))
    return (mixed.astype(jnp.bfloat16), input_grad, grads[0], grads[1], grads[2], grads[3], grads[4], grads[5], grads[6], grads[7], grads[8])
```

```python
import jax
import jax.numpy as jnp
import numpy as np
from jax import lax
from jax.sharding import PartitionSpec as P

HEADS = 16
HEAD_V = 128
QK = 16
NFEAT = 160
CORES = 2
EPS = 1e-05
BF = jnp.bfloat16
F32 = jnp.float32


def feature_tables():
    left, right, scale = [-1], [-1], [1.0]
    for i in range(QK):
        left.append(i), right.append(-1), scale.append(1.0)
    for i in range(QK):
        for j in range(i, QK):
            left.append(i), right.append(j), scale.append(1.0 if i < j else 0.7071067811865476)
    padding = NFEAT - len(left)
    left, right, scale = left + [-2] * padding, right + [-2] * padding, scale + [0.0] * padding
    table = []
    for side in (left, right):
        side = np.array(side)
        table.append((0.5 * (np.arange(QK)[:, None] == side[None, :])).astype(np.float32))
        table.append((side == -1).astype(np.float32))
    return (*table, np.array(scale, np.float32))


def dot(a, b, ca=1, cb=0):
    return lax.dot_general(a, b, (((ca,), (cb,)), ((), ())), preferred_element_type=F32)


def ein(spec, *args):
    return jnp.einsum(spec, *args, preferred_element_type=F32)


def on_device(
    tokens,
    cotangent,
    lengths,
    w_query,
    w_key,
    w_value,
    w_output,
    w_gate,
    w_up,
    w_down,
    gain_mixer,
    gain_mlp,
):
    micro, block, width = tokens.shape
    seq_count, feat_count = lax.axis_size("seq"), lax.axis_size("feat")
    seq_rank, feat_rank = lax.axis_index("seq"), lax.axis_index("feat")
    group = feat_count // micro
    ranks = CORES * group
    chips = seq_count // CORES
    chip, core = seq_rank // CORES, seq_rank % CORES
    batch, part = feat_rank // group, feat_rank % group
    rank = core * group + part
    rows = CORES * block
    piece = width // ranks
    heads = HEADS // ranks

    def move(value, target):
        pairs = []
        for s in range(seq_count):
            for f in range(feat_count):
                there = target(s // CORES, s % CORES, f // group, f % group)
                if there is not None:
                    c2, k2, m2, l2 = there
                    pairs.append(
                        (s * feat_count + f, (c2 * CORES + k2) * feat_count + m2 * group + l2)
                    )
        return lax.ppermute(value, ("seq", "feat"), pairs)

    def to_core(value):
        return move(value, lambda c, k, m, l: (c, 1 - k, m, l))

    def to_part(value, d):
        return move(value, lambda c, k, m, l: (c, k, m, l ^ d))

    def to_chip(value, mask):
        return move(value, lambda c, k, m, l: (c ^ mask, k, m, l))

    def shift_chip(value, d):
        return move(value, lambda c, k, m, l: (c + d, k, m, l) if 0 <= c + d < chips else None)

    def spread(value):
        return (
            move(value, lambda c, k, m, l: (c, m, k, l)),
            move(value, lambda c, k, m, l: (c, m, 1 - k, l)),
        )

    def unspread(same, other):
        return (
            move(same, lambda c, k, m, l: (c, m, k, l)),
            move(other, lambda c, k, m, l: (c, 1 - m, k, l)),
        )

    def ordered(first_if_zero, second_if_zero, bit, axis):
        return jnp.where(
            bit == 0,
            jnp.concatenate([first_if_zero, second_if_zero], axis),
            jnp.concatenate([second_if_zero, first_if_zero], axis),
        )

    def gather_chips(value):
        size = value.shape[0]
        bits = [1 << i for i in range(chips.bit_length() - 1)]
        full = jnp.zeros((size * seq_count, value.shape[1]), value.dtype)
        for own, order, k in zip(spread(value), (bits, bits[::-1]), (batch, 1 - batch)):
            held = {0: own}
            for bit in order:
                for mask in list(held):
                    held[mask | bit] = to_chip(held[mask], bit)
            for mask, got in held.items():
                at = ((chip ^ mask) * CORES + k) * size
                full = lax.dynamic_update_slice_in_dim(full, got, at, 0)
        return full

    chip_groups = [[c * CORES + k for c in range(chips)] for k in range(CORES)]

    def gather_chips_bulk(value, axis):
        same, other = spread(value)
        return lax.all_gather(
            ordered(same, other, batch, axis),
            "seq",
            axis=axis,
            tiled=True,
            axis_index_groups=chip_groups,
        )

    def scatter_chips(value, axis):
        mine = lax.psum_scatter(
            value.astype(BF),
            "seq",
            scatter_dimension=axis,
            tiled=True,
            axis_index_groups=chip_groups,
        )
        size = mine.shape[axis] // CORES
        same = lax.dynamic_slice_in_dim(mine, batch * size, size, axis)
        other = lax.dynamic_slice_in_dim(mine, (1 - batch) * size, size, axis)
        a, b = unspread(same, other)
        return a.astype(F32) + b.astype(F32)

    def gather_ranks(own):
        found = []
        for d in range(group):
            here = own if d == 0 else to_part(own, d)
            found.append((core * group + (part ^ d), here))
            found.append(((1 - core) * group + (part ^ d), to_core(here)))
        return found

    def reduce_ranks(partial):
        arrived = []
        for d in range(group - 1, -1, -1):
            away = to_core(partial((1 - core) * group + (part ^ d)).astype(BF))
            total = partial(core * group + (part ^ d)) + away.astype(F32)
            arrived.append(to_part(total.astype(BF), d).astype(F32) if d else total)
        return sum(arrived[:-1], arrived[-1])

    def sum_ranks(value):
        for d in [1 << i for i in range(group.bit_length() - 1)]:
            value = value + to_part(value, d)
        return value + to_core(value)

    def row_piece(value, r):
        return lax.dynamic_slice_in_dim(value, r * piece, piece, 0)

    def column_piece(value, r):
        return lax.dynamic_slice_in_dim(value, r * piece, piece, 1)

    qkv_full = gather_chips(jnp.concatenate([w_query, w_key, w_value], 1))
    qk_width, v_width = heads * QK, heads * HEAD_V
    gains = lax.all_gather(jnp.stack([gain_mixer, gain_mlp]), "seq", axis=1, tiled=True)
    gains = gains.astype(F32)
    mixer_gain, mlp_gain = gains[0], gains[1]
    output_full = gather_chips(w_output)
    gate_full = gather_chips_bulk(w_gate, 0)
    up_full = gather_chips_bulk(w_up, 0)
    down_full = gather_chips_bulk(w_down, 1)

    def chip_tokens(value):
        own = lax.dynamic_index_in_dim(value, batch, 0, False)
        return ordered(own, to_core(own), core, 0)

    tokens_c = chip_tokens(tokens)
    grad_out = chip_tokens(cotangent)

    bounds = jnp.cumsum(lax.dynamic_index_in_dim(lengths, batch, 0, False))

    def segment_of(p):
        return jnp.sum((p[..., None] >= bounds).astype(jnp.int32), axis=-1)

    start = chip * rows
    segment = segment_of(start + jnp.arange(rows, dtype=jnp.int32))
    valid = segment < 3
    valid_f = valid.astype(F32)
    edges = segment_of(start - 1 + block * jnp.arange(CORES + 1, dtype=jnp.int32))
    edges = jnp.where((jnp.arange(CORES + 1) == 0) & (start == 0), -1, edges)
    before, last = jnp.repeat(edges[:-1], block), jnp.repeat(edges[1:], block)
    use = (valid & (segment == before)).astype(F32)
    tail = (valid & (segment == last)).astype(F32)
    keep = (edges[1:] == edges[:-1]).astype(F32)
    segment_b, valid_b = segment.reshape(CORES, block), valid.reshape(CORES, block)
    order = jnp.arange(block)
    mask = (
        (order[None, None, :] <= order[None, :, None])
        & (segment_b[:, None, :] == segment_b[:, :, None])
        & valid_b[:, None, :]
    )[:, None]

    tokens_f = tokens_c.astype(F32)
    inv_one = lax.rsqrt(jnp.mean(tokens_f * tokens_f, axis=-1, keepdims=True) + EPS)
    normed = (tokens_f * inv_one * mixer_gain).astype(BF)
    qkv = dot(normed, qkv_full).astype(BF)

    def by_head(value, size):
        return value.reshape(CORES, block, heads, size).transpose(0, 2, 1, 3)

    def from_head(value):
        return value.transpose(0, 2, 1, 3).reshape(rows, -1)

    query = by_head(qkv[:, :qk_width], QK)
    keys = by_head(qkv[:, qk_width : 2 * qk_width], QK)
    values = by_head(qkv[:, 2 * qk_width :], HEAD_V)
    pick_l, one_l, pick_r, one_r, scale = feature_tables()
    pick_l, pick_r = jnp.asarray(pick_l, BF), jnp.asarray(pick_r, BF)

    def sides(x):
        return ein("bhti,ij->bhtj", x, pick_l) + one_l, ein("bhti,ij->bhtj", x, pick_r) + one_r

    def features(x):
        left, right = sides(x)
        return (left * right * scale).astype(BF)

    def features_back(x, grad):
        left, right = sides(x)
        grad = grad * scale
        return ein("bhtj,ij->bhti", (grad * right).astype(BF), pick_l) + ein(
            "bhtj,ij->bhti", (grad * left).astype(BF), pick_r
        )

    feat_q, feat_k = features(query), features(keys)
    use_b, tail_b = use.reshape(CORES, 1, block, 1), tail.reshape(CORES, 1, block, 1)
    tail_k = feat_k * tail_b.astype(BF)
    local_state = ein("bhsf,bhsc->bhfc", tail_k, values)
    local_sum = jnp.sum(tail_k, axis=2, dtype=F32)

    def pack(state, total):
        total = jnp.pad(total, ((0, 0), (0, -NFEAT % HEAD_V))).reshape(-1, HEAD_V)
        return jnp.concatenate([state.reshape(-1, HEAD_V), total], 0).astype(BF)

    def unpack(flat):
        flat = flat.astype(F32)
        cut = heads * NFEAT
        return (
            flat[:cut].reshape(heads, NFEAT, HEAD_V),
            flat[cut:].reshape(heads, -1)[:, :NFEAT],
        )

    def scan_blocks(state, total, blocks_order, step):
        at_end = (state[blocks_order[0]], total[blocks_order[0]])
        for i in blocks_order[1:]:
            carry_keep = keep[i]
            at_end = (
                state[i] + carry_keep * at_end[0],
                total[i] + carry_keep * at_end[1],
            )
        message = pack(*at_end)
        run = None
        for d in range(1, chips):
            got = unpack(shift_chip(message, step * d))
            other = chip - step * d
            if step > 0:
                same = edges[0] == segment_of((other + 1) * rows - 1)
            else:
                same = edges[CORES] == segment_of(other * rows - 1)
            weight = (same & (other >= 0) & (other < chips)).astype(F32)
            term = (weight * got[0], weight * got[1])
            run = term if run is None else (run[0] + term[0], run[1] + term[1])
        found = {}
        for i in blocks_order:
            found[i] = run
            run = (state[i] + keep[i] * run[0], total[i] + keep[i] * run[1])
        return tuple(jnp.stack([found[i][j] for i in range(CORES)]) for j in range(2))

    state, total = scan_blocks(local_state, local_sum, list(range(CORES)), 1)
    state_b = state.astype(BF)
    total_high = total.astype(BF)
    total_low = (total - total_high.astype(F32)).astype(BF)
    total_two = jnp.stack([total_high, total_low], -1)

    products = ein("bhti,bhsi->bhts", query, keys) * 0.25
    scores = jnp.where(mask, 1.0 + products + 0.5 * products * products, 0.0).astype(BF)
    numer = ein("bhts,bhsc->bhtc", scores, values)
    numer = numer + use_b * ein("bhtf,bhfc->bhtc", feat_q, state_b)
    denom = jnp.sum(scores, axis=3, dtype=F32)[..., None]
    denom = denom + use_b * jnp.sum(
        ein("bhtf,bhfe->bhte", feat_q, total_two), axis=3, keepdims=True
    )
    safe = denom + (1.0 - valid_f.reshape(CORES, 1, block, 1))
    mixer_own = from_head((numer / safe).astype(BF))

    mixer_parts = gather_ranks(mixer_own)
    branch_own = sum(dot(got, row_piece(output_full, r)) for r, got in mixer_parts).astype(BF)
    branch = jnp.zeros((rows, width), BF)
    for r, got in gather_ranks(branch_own):
        branch = lax.dynamic_update_slice_in_dim(branch, got, r * piece, 1)
    hidden_state = tokens_f + branch.astype(F32)
    inv_two = lax.rsqrt(jnp.mean(hidden_state * hidden_state, axis=-1, keepdims=True) + EPS)
    normed_two = (hidden_state * inv_two * mlp_gain).astype(BF)

    grad_hidden = dot(grad_out, down_full, 1, 1).astype(BF).astype(F32)
    gate = dot(normed_two, gate_full).astype(BF).astype(F32)
    upward = dot(normed_two, up_full).astype(BF).astype(F32)
    logistic = jax.nn.sigmoid(gate)
    activated = gate * logistic
    hidden = (activated * upward).astype(BF)
    grad_gate_f = grad_hidden * upward * logistic * (1.0 + gate * (1.0 - logistic))
    grad_up_f = grad_hidden * activated
    grad_gate_b, grad_up_b = grad_gate_f.astype(BF), grad_up_f.astype(BF)
    inner_two = sum_ranks(jnp.sum(grad_gate_f * gate + grad_up_f * upward, axis=1)) / width
    normed_grad = reduce_ranks(
        lambda r: dot(grad_gate_b, row_piece(gate_full, r), 1, 1)
        + dot(grad_up_b, row_piece(up_full, r), 1, 1)
    )
    tokens_own = column_piece(tokens_c, rank).astype(F32)
    hidden_own = tokens_own + branch_own.astype(F32)
    scaled_two = hidden_own * inv_two
    mlp_gain_own = lax.dynamic_slice_in_dim(mlp_gain, rank * piece, piece, 0)
    hidden_grad = column_piece(grad_out, rank).astype(F32) + inv_two * (
        normed_grad * mlp_gain_own - scaled_two * inner_two[:, None]
    )
    grad_gain_mlp = jnp.sum(normed_grad * scaled_two, axis=0)
    branch_grad = hidden_grad.astype(BF)

    mixer_grad = reduce_ranks(lambda r: dot(branch_grad, row_piece(output_full, r), 1, 1))
    mixer_grad = by_head(mixer_grad, HEAD_V)
    mixer_f = by_head(mixer_own, HEAD_V).astype(F32)
    grad_numer = (mixer_grad / safe).astype(BF)
    grad_denom = -jnp.sum(mixer_grad * mixer_f, axis=3, keepdims=True) / safe
    use_q = feat_q * use_b.astype(BF)
    grad_state = ein("bhtf,bhtc->bhfc", use_q, grad_numer)
    grad_sum = jnp.sum(use_q.astype(F32) * grad_denom, axis=2)
    carried, carried_sum = scan_blocks(grad_state, grad_sum, list(range(CORES))[::-1], -1)
    carried_b = carried.astype(BF)
    grad_scores = jnp.where(
        mask, ein("bhtc,bhsc->bhts", grad_numer, values) + grad_denom, 0.0
    ).astype(BF)
    grad_products = (grad_scores.astype(F32) * (0.25 + 0.25 * products)).astype(BF)
    grad_fq = use_b * (
        ein("bhtc,bhfc->bhtf", grad_numer, state_b) + grad_denom * total[:, :, None, :]
    )
    grad_fk = tail_b * (
        ein("bhsc,bhfc->bhsf", values, carried_b) + carried_sum[:, :, None, :]
    )
    grad_query = ein("bhts,bhsi->bhti", grad_products, keys) + features_back(query, grad_fq)
    grad_keys = ein("bhts,bhti->bhsi", grad_products, query) + features_back(keys, grad_fk)
    grad_values = ein("bhts,bhtc->bhsc", scores, grad_numer) + tail_b * ein(
        "bhsf,bhfc->bhsc", feat_k, carried_b
    )
    grad_qkv = jnp.concatenate(
        [from_head(g.astype(BF)) for g in (grad_query, grad_keys, grad_values)], 1
    )
    inner_one = jnp.sum(grad_qkv.astype(F32) * qkv.astype(F32), axis=1)
    inner_one = sum_ranks(inner_one) / width
    input_normed = reduce_ranks(lambda r: dot(grad_qkv, row_piece(qkv_full, r), 1, 1))
    scaled_one = tokens_own * inv_one
    mixer_gain_own = lax.dynamic_slice_in_dim(mixer_gain, rank * piece, piece, 0)
    grad_gain_mixer = jnp.sum(input_normed * scaled_one, axis=0)
    input_own = (
        hidden_grad
        + inv_one * (input_normed * mixer_gain_own - scaled_one * inner_one[:, None])
    ).astype(BF)

    def half(value, k):
        return lax.dynamic_slice_in_dim(value, k * block, block, 0)

    input_pair = ordered(
        half(input_own, core)[None], to_core(half(input_own, 1 - core))[None], core, 0
    )
    input_grad = lax.all_gather(input_pair, "feat", axis=0)
    input_grad = input_grad.reshape(micro, group, CORES, block, piece)
    input_grad = input_grad.transpose(0, 3, 2, 1, 4).reshape(micro, block, width).astype(F32)

    mlp_own = reduce_ranks(lambda r: dot(hidden, column_piece(down_full, r)))
    mixed_own = (hidden_own + mlp_own).astype(BF)
    same, other = unspread(half(mixed_own, batch), half(mixed_own, 1 - batch))
    mixed = ordered(same[None], other[None], core, 0)

    grad_gate = scatter_chips(dot(normed_two, grad_gate_b, 0, 0), 0)
    grad_up = scatter_chips(dot(normed_two, grad_up_b, 0, 0), 0)
    grad_down = scatter_chips(dot(hidden, grad_out, 0, 0), 1)
    grad_output = jnp.zeros((width, piece), BF)
    for r, got in mixer_parts:
        grad_output = lax.dynamic_update_slice_in_dim(
            grad_output, dot(got, branch_grad, 0, 0).astype(BF), r * piece, 0
        )
    grad_output = scatter_chips(grad_output, 0)
    grad_qkv_w = scatter_chips(dot(normed, grad_qkv, 0, 0), 0)

    gain_grads = lax.dynamic_update_slice_in_dim(
        jnp.zeros((2, width), F32), jnp.stack([grad_gain_mixer, grad_gain_mlp]), rank * piece, 1
    )
    gain_grads = lax.psum(gain_grads, ("seq", "feat"))
    shard = width // seq_count
    gain_grads = lax.dynamic_slice_in_dim(gain_grads, seq_rank * shard, shard, 1)
    return (
        mixed,
        input_grad,
        grad_qkv_w[:, :qk_width],
        grad_qkv_w[:, qk_width : 2 * qk_width],
        grad_qkv_w[:, 2 * qk_width :],
        grad_output,
        grad_gate,
        grad_up,
        grad_down,
        gain_grads[0],
        gain_grads[1],
    )


def solution(mesh):
    in_specs = (
        P(None, "seq", None),
        P(None, "seq", None),
        P(),
        P("seq", "feat"),
        P("seq", "feat"),
        P("seq", "feat"),
        P("seq", "feat"),
        P("seq", "feat"),
        P("seq", "feat"),
        P("feat", "seq"),
        P("seq"),
        P("seq"),
    )
    out_specs = (
        P(None, "seq", "feat"),
        P(None, "seq", None),
        P("seq", "feat"),
        P("seq", "feat"),
        P("seq", "feat"),
        P("seq", "feat"),
        P("seq", "feat"),
        P("seq", "feat"),
        P("feat", "seq"),
        P("seq"),
        P("seq"),
    )
    return jax.shard_map(
        on_device, mesh=mesh, in_specs=in_specs, out_specs=out_specs, check_vma=False
    )
```

```python
import functools

import jax
import jax.numpy as jnp
import numpy as np
from jax import lax
from jax.experimental import pallas as pl
from jax.experimental.pallas import tpu as pltpu
from jax.sharding import PartitionSpec as P

HEADS = 16
HEAD_V = 128
QK = 16
NFEAT = 160
CORES = 2
EPS = 1e-05
BF = jnp.bfloat16
F32 = jnp.float32


LANES = 256
TILE = 256


def feature_tables(heads):
    left, right, scale = [-1], [-1], [1.0]
    for i in range(QK):
        left.append(i), right.append(-1), scale.append(1.0)
    for i in range(QK):
        for j in range(i, QK):
            left.append(i), right.append(j), scale.append(1.0 if i < j else 0.7071067811865476)
    padding = LANES - len(left)
    left, right, scale = left + [-2] * padding, right + [-2] * padding, scale + [0.0] * padding
    both = np.array(left + right)
    pick = np.zeros((heads * QK, heads, 2 * LANES), np.float32)
    for h in range(heads):
        pick[h * QK : (h + 1) * QK, h] = 0.5 * (np.arange(QK)[:, None] == both[None, :])
    ones = (both == -1).astype(np.float32)[None]
    own = np.zeros((8, heads * QK), np.float32)
    for h in range(heads):
        own[h, h * QK : (h + 1) * QK] = 0.25
    return (
        jnp.asarray(pick.reshape(heads * QK, -1), BF),
        jnp.asarray(ones),
        jnp.asarray(np.array(scale, np.float32)[None]),
        jnp.asarray(own, BF),
    )


def nt(a, b):
    return lax.dot_general(a, b, (((1,), (1,)), ((), ())), preferred_element_type=F32)


def tn(a, b):
    return lax.dot_general(a, b, (((0,), (0,)), ((), ())), preferred_element_type=F32)


def nn(a, b):
    return lax.dot_general(a, b, (((1,), (0,)), ((), ())), preferred_element_type=F32)


class Marks:
    def __init__(self, marks, b, block):
        t = lax.broadcasted_iota(jnp.int32, (block, 1), 0)
        first, second, third = marks[b, 0], marks[b, 1], marks[b, 2]
        low = jnp.where(t >= first, first, 0)
        low = jnp.where(t >= second, second, low)
        self.low = jnp.where(t >= third, block, low)
        self.padding = jnp.where(t >= third, 1.0, 0.0).astype(F32)
        self.use = jnp.where(t < marks[b, 3], 1.0, 0.0).astype(F32)
        self.tail = jnp.where(t >= marks[b, 4], 1.0, 0.0).astype(F32)

    def mask(self, at, count):
        t = lax.broadcasted_iota(jnp.int32, (TILE, count), 0) + at
        s = lax.broadcasted_iota(jnp.int32, (TILE, count), 1)
        return (s <= t) & (s >= self.low[at : at + TILE])


def sides(x, pick, ones, h):
    both = nn(x, pick[:, 2 * LANES * h : 2 * LANES * (h + 1)]) + ones
    return both[:, :LANES], both[:, LANES:]


def head_cols(ref, h):
    return ref[:, HEAD_V * h : HEAD_V * (h + 1)]


def output_grads(do_ref, o_ref, den_ref, h):
    do, o, den = head_cols(do_ref, h), head_cols(o_ref, h).astype(F32), head_cols(den_ref, h)
    do = do.astype(F32)
    inverse = 1.0 / den
    dnum = (do * inverse).astype(BF)
    dden = -jnp.sum(do * o, axis=1, keepdims=True) * inverse
    return dnum, dden


def state_kernel(marks, k_ref, v_ref, pick, ones, scale, out_ref, *, heads, block):
    m = Marks(marks, pl.program_id(0), block)
    k = k_ref[...]
    for h in range(heads):
        left, right = sides(k, pick, ones[...], h)
        feat = (left * right * (scale[...] * m.tail)).astype(BF)
        v = head_cols(v_ref, h)
        out_ref[0, h] = tn(feat, jnp.concatenate([v, jnp.ones_like(v)], 1))[:NFEAT]


def grad_state_kernel(
    marks, q_ref, do_ref, o_ref, den_ref, pick, ones, scale, out_ref, *, heads, block
):
    m = Marks(marks, pl.program_id(0), block)
    q = q_ref[...]
    for h in range(heads):
        left, right = sides(q, pick, ones[...], h)
        feat = (left * right * (scale[...] * m.use)).astype(BF)
        dnum, dden = output_grads(do_ref, o_ref, den_ref, h)
        out_ref[0, h] = tn(feat, jnp.concatenate([dnum, dden.astype(BF)], 1))[:NFEAT]


def mixer_kernel(
    marks, q_ref, k_ref, v_ref, s_ref, pick, ones, scale, own, o_ref, den_ref, *, heads, block
):
    m = Marks(marks, pl.program_id(0), block)
    q, k = q_ref[...], k_ref[...]
    for h in range(heads):
        q_own = q * own[h : h + 1, :]
        left, right = sides(q, pick, ones[...], h)
        feat = (left * right * scale[...]).astype(BF)
        before = nn(feat, s_ref[0, h]) * m.use
        v = head_cols(v_ref, h)
        v_one = jnp.concatenate([v, jnp.ones_like(v)], 1)
        for at in range(0, block, TILE):
            count = at + TILE
            prod = nt(q_own[at:count], k[:count])
            score = 1.0 + prod + 0.5 * prod * prod
            score = jnp.where(m.mask(at, count), score, 0.0).astype(BF)
            both = nn(score, v_one[:count]) + before[at:count]
            den = both[:, HEAD_V:] + m.padding[at:count]
            here = (slice(at, count), slice(HEAD_V * h, HEAD_V * (h + 1)))
            o_ref[here] = (both[:, :HEAD_V] / den).astype(BF)
            den_ref[here] = den


def mixer_back_kernel(
    marks,
    q_ref,
    k_ref,
    v_ref,
    do_ref,
    o_ref,
    den_ref,
    s_ref,
    g_ref,
    pick,
    ones,
    scale,
    own,
    dq_ref,
    dk_ref,
    dv_ref,
    dq,
    dk,
    dv,
    *,
    heads,
    block,
):
    m = Marks(marks, pl.program_id(0), block)
    q, k = q_ref[...], k_ref[...]
    first_lane = lax.broadcasted_iota(jnp.int32, (block, HEAD_V), 1) == 0
    dq[...] = jnp.zeros_like(dq)
    dk[...] = jnp.zeros_like(dk)
    for h in range(heads):
        table = pick[:, 2 * LANES * h : 2 * LANES * (h + 1)]
        q_own, k_own = q * own[h : h + 1, :], k * own[h : h + 1, :]
        v = head_cols(v_ref, h)
        dnum, dden = output_grads(do_ref, o_ref, den_ref, h)
        state, carried = s_ref[0, h], g_ref[0, h]

        left, right = sides(q, pick, ones[...], h)
        wide = jnp.concatenate([dnum, jnp.where(first_lane, dden, 0.0).astype(BF)], 1)
        dfeat = nt(wide, state) * (scale[...] * m.use)
        pulled = jnp.concatenate([(dfeat * right).astype(BF), (dfeat * left).astype(BF)], 1)
        dq[...] += nt(pulled, table)

        left, right = sides(k, pick, ones[...], h)
        wide = jnp.concatenate([v, jnp.where(first_lane, 1.0, 0.0).astype(BF)], 1)
        dfeat = nt(wide, carried) * (scale[...] * m.tail)
        pulled = jnp.concatenate([(dfeat * right).astype(BF), (dfeat * left).astype(BF)], 1)
        dk[...] += nt(pulled, table)
        feat = (left * right * (scale[...] * m.tail)).astype(BF)
        dv[...] = nn(feat, carried[:, :HEAD_V])

        for at in range(0, block, TILE):
            count = at + TILE
            prod = nt(q_own[at:count], k[:count])
            one = 1.0 + prod
            mask = m.mask(at, count)
            score = jnp.where(mask, one + 0.5 * prod * prod, 0.0).astype(BF)
            dscore = nt(dnum[at:count], v[:count]) + dden[at:count, :1]
            dprod = jnp.where(mask, dscore * one, 0.0).astype(BF)
            dq[at:count] += nn(dprod, k_own[:count])
            dk[:count] += tn(dprod, q_own[at:count])
            dv[:count] += tn(score, dnum[at:count])
        dv_ref[:, HEAD_V * h : HEAD_V * (h + 1)] = dv[...].astype(BF)
    dq_ref[...] = dq[...].astype(BF)
    dk_ref[...] = dk[...].astype(BF)


def mixer_calls(heads, block, blocks):
    tables = feature_tables(heads)
    narrow = pl.BlockSpec((block, heads * QK), lambda b, marks: (b, 0))
    wide = pl.BlockSpec((block, heads * HEAD_V), lambda b, marks: (b, 0))
    local = pl.BlockSpec((1, heads, NFEAT, 2 * HEAD_V), lambda b, marks: (b, 0, 0, 0))
    state = pl.BlockSpec((1, heads, LANES, 2 * HEAD_V), lambda b, marks: (b, 0, 0, 0))
    fixed = [pl.BlockSpec(t.shape, lambda b, marks: (0, 0)) for t in tables]
    rows = block * blocks

    def call(kernel, specs, used, outs, scratch, cost):
        def run(marks, *args):
            return pl.pallas_call(
                functools.partial(kernel, heads=heads, block=block),
                grid_spec=pltpu.PrefetchScalarGridSpec(
                    num_scalar_prefetch=1,
                    grid=(blocks,),
                    in_specs=specs + fixed[:used],
                    out_specs=[o[0] for o in outs],
                    scratch_shapes=scratch,
                ),
                out_shape=[jax.ShapeDtypeStruct(*o[1:]) for o in outs],
                cost_estimate=pl.CostEstimate(
                    flops=cost * rows * heads, bytes_accessed=rows * heads * 1500, transcendentals=0
                ),
                compiler_params=pltpu.CompilerParams(vmem_limit_bytes=48 * 2**20),
            )(marks, *args, *tables[:used])

        return run

    local_out = (local, (blocks, heads, NFEAT, 2 * HEAD_V), F32)
    wide_b, wide_f = (wide, (rows, heads * HEAD_V), BF), (wide, (rows, heads * HEAD_V), F32)
    narrow_b = (narrow, (rows, heads * QK), BF)
    scratch = [
        pltpu.VMEM((block, heads * QK), F32),
        pltpu.VMEM((block, heads * QK), F32),
        pltpu.VMEM((block, HEAD_V), F32),
    ]
    return (
        call(state_kernel, [narrow, wide], 3, [local_out], [], 500000),
        call(mixer_kernel, [narrow, narrow, wide, state], 4, [wide_b, wide_f], [], 1000000),
        call(grad_state_kernel, [narrow, wide, wide, wide], 3, [local_out], [], 500000),
        call(
            mixer_back_kernel,
            [narrow, narrow, wide, wide, wide, wide, state, state],
            4,
            [narrow_b, narrow_b, wide_b],
            scratch,
            2500000,
        ),
    )


def dot(a, b, ca=1, cb=0):
    return lax.dot_general(a, b, (((ca,), (cb,)), ((), ())), preferred_element_type=F32)


def after(value, *others):
    return lax.optimization_barrier((value, *others))[0]


def place_kernel(offsets, *refs, axis):
    *pieces, out, sems = refs
    copies = []
    for i, piece in enumerate(pieces):
        size = piece.shape[axis]
        span = pl.ds(pl.multiple_of(offsets[i], size), size)
        target = out.at[span] if axis == 0 else out.at[:, span]
        copies.append(pltpu.make_async_copy(piece, target, sems.at[i]))
    for copy in copies:
        copy.start()
    for copy in copies:
        copy.wait()


def place(pieces, offsets, axis):
    shape = list(pieces[0].shape)
    shape[axis] = sum(p.shape[axis] for p in pieces)
    size = int(np.prod(shape)) * pieces[0].dtype.itemsize
    return pl.pallas_call(
        functools.partial(place_kernel, axis=axis),
        grid_spec=pltpu.PrefetchScalarGridSpec(
            num_scalar_prefetch=1,
            grid=(),
            in_specs=[pl.BlockSpec(memory_space=pl.ANY)] * len(pieces),
            out_specs=pl.BlockSpec(memory_space=pl.ANY),
            scratch_shapes=[pltpu.SemaphoreType.DMA((len(pieces),))],
        ),
        out_shape=jax.ShapeDtypeStruct(tuple(shape), pieces[0].dtype),
        cost_estimate=pl.CostEstimate(flops=0, bytes_accessed=2 * size, transcendentals=0),
    )(jnp.stack(offsets).astype(jnp.int32), *pieces)


def widen_kernel(where, *refs, group):
    *shares, out = refs
    count, core = (len(shares) + 1) // 2, where[1]
    piece = shares[0].shape[2]
    for d in range(count):
        plane = lax.rem(where[0] + count - d, count)
        batch, part = plane // group, lax.rem(plane, group)
        for j in range(CORES):
            got = shares[d][j].astype(F32)
            if d:
                got = got + shares[2 * count - 1 - d][j].astype(F32)
            k = core if j == 0 else 1 - core
            at = pl.multiple_of((k * group + part) * piece, piece)
            out[batch, :, pl.ds(at, piece)] = got


def widen(shares, feat_rank, core, micro, group, width):
    _, block, piece = shares[0].shape
    tile = 128
    return pl.pallas_call(
        functools.partial(widen_kernel, group=group),
        grid_spec=pltpu.PrefetchScalarGridSpec(
            num_scalar_prefetch=1,
            grid=(block // tile,),
            in_specs=[pl.BlockSpec((CORES, tile, piece), lambda i, w: (0, i, 0))] * len(shares),
            out_specs=pl.BlockSpec((micro, tile, width), lambda i, w: (0, i, 0)),
        ),
        out_shape=jax.ShapeDtypeStruct((micro, block, width), F32),
        compiler_params=pltpu.CompilerParams(vmem_limit_bytes=48 * 2**20),
    )(jnp.stack([feat_rank, core]).astype(jnp.int32), *shares)


def on_device(
    tokens,
    cotangent,
    lengths,
    w_query,
    w_key,
    w_value,
    w_output,
    w_gate,
    w_up,
    w_down,
    gain_mixer,
    gain_mlp,
):
    micro, block, width = tokens.shape
    seq_count, feat_count = lax.axis_size("seq"), lax.axis_size("feat")
    seq_rank, feat_rank = lax.axis_index("seq"), lax.axis_index("feat")
    group = feat_count // micro
    ranks = CORES * group
    chips = seq_count // CORES
    chip, core = seq_rank // CORES, seq_rank % CORES
    batch, part = feat_rank // group, feat_rank % group
    rank = core * group + part
    rows = CORES * block
    piece = width // ranks
    heads = HEADS // ranks

    def move(value, target):
        pairs = []
        for s in range(seq_count):
            for f in range(feat_count):
                there = target(s // CORES, s % CORES, f // group, f % group)
                if there is not None:
                    c2, k2, m2, l2 = there
                    pairs.append(
                        (s * feat_count + f, (c2 * CORES + k2) * feat_count + m2 * group + l2)
                    )
        return lax.ppermute(value, ("seq", "feat"), pairs)

    def to_core(value):
        return move(value, lambda c, k, m, l: (c, 1 - k, m, l))

    def to_part(value, d):
        return move(value, lambda c, k, m, l: (c, k, m, l ^ d))

    def to_chip(value, mask):
        return move(value, lambda c, k, m, l: (c ^ mask, k, m, l))

    def shift_chip(value, d):
        return move(value, lambda c, k, m, l: (c + d, k, m, l) if 0 <= c + d < chips else None)

    def spread(value):
        return (
            move(value, lambda c, k, m, l: (c, m, k, l)),
            move(value, lambda c, k, m, l: (c, m, 1 - k, l)),
        )

    def unspread(same, other):
        return (
            move(same, lambda c, k, m, l: (c, m, k, l)),
            move(other, lambda c, k, m, l: (c, 1 - m, k, l)),
        )

    def ordered(first_if_zero, second_if_zero, bit, axis):
        return jnp.where(
            bit == 0,
            jnp.concatenate([first_if_zero, second_if_zero], axis),
            jnp.concatenate([second_if_zero, first_if_zero], axis),
        )

    def gather_chips(value, axis=0, needs=()):
        size = value.shape[axis]
        bits = [1 << i for i in range(chips.bit_length() - 1)]
        pieces, offsets = [], []
        owns = spread(after(value, *needs) if needs else value)
        for own, order, k in zip(owns, (bits, bits[::-1]), (batch, 1 - batch)):
            held = {0: own}
            for bit in order:
                for mask in list(held):
                    held[mask | bit] = to_chip(held[mask], bit)
            for mask, got in held.items():
                pieces.append(got)
                offsets.append(((chip ^ mask) * CORES + k) * size)
        return place(pieces, offsets, axis), owns

    chip_groups = [[c * CORES + k for c in range(chips)] for k in range(CORES)]

    def scatter_chips(value, axis):
        mine = lax.psum_scatter(
            value.astype(BF),
            "seq",
            scatter_dimension=axis,
            tiled=True,
            axis_index_groups=chip_groups,
        )
        size = mine.shape[axis] // CORES
        same = lax.dynamic_slice_in_dim(mine, batch * size, size, axis)
        other = lax.dynamic_slice_in_dim(mine, (1 - batch) * size, size, axis)
        a, b = unspread(same, other)
        return a.astype(F32) + b.astype(F32)

    def gather_ranks(own):
        found = []
        for d in range(group):
            here = own if d == 0 else to_part(own, d)
            found.append((core * group + (part ^ d), here))
            found.append(((1 - core) * group + (part ^ d), to_core(here)))
        return found

    def reduce_ranks(partial, needs=()):
        arrived = []
        for d in range(group - 1, -1, -1):
            away = to_core(partial((1 - core) * group + (part ^ d)).astype(BF))
            total = partial(core * group + (part ^ d)) + away.astype(F32)
            if d:
                total = total.astype(BF)
                total = after(total, *needs) if needs else total
                total = to_part(total, d).astype(F32)
            arrived.append(total)
        return sum(arrived[:-1], arrived[-1])

    def sum_ranks(value):
        for d in [1 << i for i in range(group.bit_length() - 1)]:
            value = value + to_part(value, d)
        return value + to_core(value)

    def row_piece(value, r):
        return lax.dynamic_slice_in_dim(value, r * piece, piece, 0)

    def column_piece(value, r):
        return lax.dynamic_slice_in_dim(value, r * piece, piece, 1)

    def chip_tokens(value):
        own = lax.dynamic_index_in_dim(value, batch, 0, False)
        return place([own, to_core(own)], [core * block, (1 - core) * block], 0)

    tokens_c = chip_tokens(tokens)
    grad_out = chip_tokens(cotangent)

    qk_width, v_width = heads * QK, heads * HEAD_V
    qkv_full, first = gather_chips(jnp.concatenate([w_query, w_key, w_value], 1))
    gains = lax.all_gather(jnp.stack([gain_mixer, gain_mlp]), "seq", axis=1, tiled=True)
    gains = gains.astype(F32)
    mixer_gain, mlp_gain = gains[0], gains[1]
    output_full, first = gather_chips(w_output, 0, first)
    gate_full, first = gather_chips(w_gate, 0, first)
    up_full, first = gather_chips(w_up, 0, first)
    down_full, first = gather_chips(w_down, 1, first)

    bounds = jnp.cumsum(lax.dynamic_index_in_dim(lengths, batch, 0, False))

    def segment_of(p):
        return jnp.sum((p[..., None] >= bounds).astype(jnp.int32), axis=-1)

    start = chip * rows
    base = start + block * jnp.arange(CORES + 1, dtype=jnp.int32)
    edges = jnp.where(base == 0, -1, segment_of(base - 1))
    keep = (edges[1:] == edges[:-1]).astype(F32)
    base = base[:-1]
    ends = jnp.concatenate([jnp.zeros((1,), jnp.int32), bounds])
    open_end = jnp.where((edges[:-1] < 0) | (edges[:-1] > 2), 0, ends[edges[:-1] + 1] - base)
    tail_start = jnp.where(edges[1:] > 2, block, ends[edges[1:]] - base)
    marks = jnp.concatenate(
        [bounds[None, :] - base[:, None], open_end[:, None], tail_start[:, None]], 1
    ).astype(jnp.int32)

    tokens_f = tokens_c.astype(F32)
    inv_one = lax.rsqrt(jnp.mean(tokens_f * tokens_f, axis=-1, keepdims=True) + EPS)
    normed = (tokens_f * inv_one * mixer_gain).astype(BF)
    qkv = dot(normed, qkv_full).astype(BF)

    query, keys = qkv[:, :qk_width], qkv[:, qk_width : 2 * qk_width]
    values = qkv[:, 2 * qk_width :]
    local_states, mixer, grad_states, mixer_back = mixer_calls(heads, block, CORES)

    def pack(state, total):
        total = jnp.pad(total, ((0, 0), (0, -NFEAT % HEAD_V))).reshape(-1, HEAD_V)
        return jnp.concatenate([state.reshape(-1, HEAD_V), total], 0).astype(BF)

    def unpack(flat):
        flat = flat.astype(F32)
        cut = heads * NFEAT
        return (
            flat[:cut].reshape(heads, NFEAT, HEAD_V),
            flat[cut:].reshape(heads, -1)[:, :NFEAT],
        )

    def scan_blocks(both, blocks_order, step):
        state, total = both[..., :HEAD_V], both[..., HEAD_V]
        at_end = (state[blocks_order[0]], total[blocks_order[0]])
        for i in blocks_order[1:]:
            carry_keep = keep[i]
            at_end = (
                state[i] + carry_keep * at_end[0],
                total[i] + carry_keep * at_end[1],
            )
        message = pack(*at_end)
        run = None
        for d in range(1, chips):
            got = unpack(shift_chip(message, step * d))
            other = chip - step * d
            if step > 0:
                same = edges[0] == segment_of((other + 1) * rows - 1)
            else:
                same = edges[CORES] == segment_of(other * rows - 1)
            weight = (same & (other >= 0) & (other < chips)).astype(F32)
            term = (weight * got[0], weight * got[1])
            run = term if run is None else (run[0] + term[0], run[1] + term[1])
        found = {}
        for i in blocks_order:
            found[i] = run
            run = (state[i] + keep[i] * run[0], total[i] + keep[i] * run[1])
        state, total = (jnp.stack([found[i][j] for i in range(CORES)]) for j in range(2))
        total = jnp.broadcast_to(total[..., None], state.shape)
        both = jnp.concatenate([state, total], -1).astype(BF)
        return jnp.pad(both, ((0, 0), (0, 0), (0, LANES - NFEAT), (0, 0)))

    (local,) = local_states(marks, keys, values)
    states = scan_blocks(local, list(range(CORES)), 1)
    mixer_own, denom = mixer(marks, query, keys, values, states)

    mixer_parts = gather_ranks(mixer_own)
    branch_own = sum(dot(got, row_piece(output_full, r)) for r, got in mixer_parts).astype(BF)
    branch_parts = gather_ranks(branch_own)
    branch = place([got for _, got in branch_parts], [r * piece for r, _ in branch_parts], 1)
    hidden_state = tokens_f + branch.astype(F32)
    inv_two = lax.rsqrt(jnp.mean(hidden_state * hidden_state, axis=-1, keepdims=True) + EPS)
    normed_two = (hidden_state * inv_two * mlp_gain).astype(BF)

    grad_hidden = dot(grad_out, down_full, 1, 1).astype(BF).astype(F32)
    gate = dot(normed_two, gate_full).astype(BF).astype(F32)
    upward = dot(normed_two, up_full).astype(BF).astype(F32)
    logistic = jax.nn.sigmoid(gate)
    activated = gate * logistic
    hidden = (activated * upward).astype(BF)
    grad_gate_f = grad_hidden * upward * logistic * (1.0 + gate * (1.0 - logistic))
    grad_up_f = grad_hidden * activated
    grad_gate_b, grad_up_b = grad_gate_f.astype(BF), grad_up_f.astype(BF)
    inner_two = sum_ranks(jnp.sum(grad_gate_f * gate + grad_up_f * upward, axis=1)) / width
    normed_grad = reduce_ranks(
        lambda r: dot(grad_gate_b, row_piece(gate_full, r), 1, 1)
        + dot(grad_up_b, row_piece(up_full, r), 1, 1),
        (inner_two,),
    )
    tokens_own = column_piece(tokens_c, rank).astype(F32)
    hidden_own = tokens_own + branch_own.astype(F32)
    scaled_two = hidden_own * inv_two
    mlp_gain_own = lax.dynamic_slice_in_dim(mlp_gain, rank * piece, piece, 0)
    hidden_grad = column_piece(grad_out, rank).astype(F32) + inv_two * (
        normed_grad * mlp_gain_own - scaled_two * inner_two[:, None]
    )
    grad_gain_mlp = jnp.sum(normed_grad * scaled_two, axis=0)
    branch_grad = hidden_grad.astype(BF)

    mixer_grad = reduce_ranks(lambda r: dot(branch_grad, row_piece(output_full, r), 1, 1))
    (grad_local,) = grad_states(marks, query, mixer_grad, mixer_own, denom)
    carried = scan_blocks(grad_local, list(range(CORES))[::-1], -1)
    grad_qkv = jnp.concatenate(
        mixer_back(
            marks, query, keys, values, mixer_grad, mixer_own, denom, states, carried
        ),
        1,
    )
    inner_one = jnp.sum(grad_qkv.astype(F32) * qkv.astype(F32), axis=1)
    inner_one = sum_ranks(inner_one) / width
    input_normed = reduce_ranks(
        lambda r: dot(grad_qkv, row_piece(qkv_full, r), 1, 1), (inner_one,)
    )
    scaled_one = tokens_own * inv_one
    mixer_gain_own = lax.dynamic_slice_in_dim(mixer_gain, rank * piece, piece, 0)
    grad_gain_mixer = jnp.sum(input_normed * scaled_one, axis=0)
    input_own = (
        hidden_grad
        + inv_one * (input_normed * mixer_gain_own - scaled_one * inner_one[:, None])
    ).astype(BF)

    def half(value, k):
        return lax.dynamic_slice_in_dim(value, k * block, block, 0)

    gain_grads = lax.dynamic_update_slice_in_dim(
        jnp.zeros((2, width), F32), jnp.stack([grad_gain_mixer, grad_gain_mlp]), rank * piece, 1
    )
    planes = [
        move(gain_grads, lambda c, k, m, l: (c, k, *divmod((m * group + l) ^ d, group)))
        for d in range(1, feat_count)
    ]
    input_own = after(input_own, gain_grads)
    input_pair = jnp.stack([half(input_own, core), to_core(half(input_own, 1 - core))])

    def step_plane(value, step, first):
        def target(c, k, m, l):
            here = m * group + l
            behind = here if step > 0 else feat_count - 1 - here
            if behind < first or behind == feat_count - 1:
                return None
            return (c, k, *divmod(here + step, group))

        return move(value, target)

    ups, downs = [input_pair], [input_pair]
    for d in range(feat_count - 1):
        ups.append(step_plane(ups[-1], 1, d))
        downs.append(step_plane(downs[-1], -1, d))
    input_grad = widen(ups + downs[1:], feat_rank, core, micro, group, width)

    gain_grads = sum(planes, gain_grads)
    gain_grads = gain_grads + to_core(gain_grads)
    for bit in [1 << i for i in range(chips.bit_length() - 1)]:
        gain_grads = gain_grads + to_chip(gain_grads, bit)
    shard = width // seq_count
    gain_grads = lax.dynamic_slice_in_dim(gain_grads, seq_rank * shard, shard, 1)

    mlp_own = reduce_ranks(lambda r: dot(hidden, column_piece(down_full, r)), (mixer_grad,))
    mixed_own = (hidden_own + mlp_own).astype(BF)
    same, other = unspread(half(mixed_own, batch), half(mixed_own, 1 - batch))
    mixed = ordered(same[None], other[None], core, 0)

    grad_gate = scatter_chips(dot(normed_two, grad_gate_b, 0, 0), 0)
    grad_up = scatter_chips(dot(normed_two, grad_up_b, 0, 0), 0)
    grad_down = scatter_chips(dot(hidden, grad_out, 0, 0), 1)
    grad_output = place(
        [dot(got, branch_grad, 0, 0).astype(BF) for _, got in mixer_parts],
        [r * piece for r, _ in mixer_parts],
        0,
    )
    grad_output = scatter_chips(grad_output, 0)
    grad_qkv_w = scatter_chips(dot(normed, grad_qkv, 0, 0), 0)

    return (
        mixed,
        input_grad,
        grad_qkv_w[:, :qk_width],
        grad_qkv_w[:, qk_width : 2 * qk_width],
        grad_qkv_w[:, 2 * qk_width :],
        grad_output,
        grad_gate,
        grad_up,
        grad_down,
        gain_grads[0],
        gain_grads[1],
    )


def solution(mesh):
    in_specs = (
        P(None, "seq", None),
        P(None, "seq", None),
        P(),
        P("seq", "feat"),
        P("seq", "feat"),
        P("seq", "feat"),
        P("seq", "feat"),
        P("seq", "feat"),
        P("seq", "feat"),
        P("feat", "seq"),
        P("seq"),
        P("seq"),
    )
    out_specs = (
        P(None, "seq", "feat"),
        P(None, "seq", None),
        P("seq", "feat"),
        P("seq", "feat"),
        P("seq", "feat"),
        P("seq", "feat"),
        P("seq", "feat"),
        P("seq", "feat"),
        P("feat", "seq"),
        P("seq"),
        P("seq"),
    )
    return jax.shard_map(
        on_device, mesh=mesh, in_specs=in_specs, out_specs=out_specs, check_vma=False
    )
```

```python
import functools

import jax
import jax.numpy as jnp
import numpy as np
from jax import lax
from jax.experimental import pallas as pl
from jax.experimental.pallas import tpu as pltpu
from jax.sharding import PartitionSpec as P

HEADS = 16
HEAD_V = 128
QK = 16
NFEAT = 160
CORES = 2
EPS = 1e-05
BF = jnp.bfloat16
F32 = jnp.float32


LANES = 256
TILE = 256


def feature_tables(heads):
    left, right, scale = [-1], [-1], [1.0]
    for i in range(QK):
        left.append(i), right.append(-1), scale.append(1.0)
    for i in range(QK):
        for j in range(i, QK):
            left.append(i), right.append(j), scale.append(1.0 if i < j else 0.7071067811865476)
    padding = LANES - len(left)
    left, right, scale = left + [-2] * padding, right + [-2] * padding, scale + [0.0] * padding
    both = np.array(left + right)
    pick = np.zeros((heads * QK, heads, 2 * LANES), np.float32)
    for h in range(heads):
        pick[h * QK : (h + 1) * QK, h] = 0.5 * (np.arange(QK)[:, None] == both[None, :])
    ones = (both == -1).astype(np.float32)[None]
    own = np.zeros((8, heads * QK), np.float32)
    for h in range(heads):
        own[h, h * QK : (h + 1) * QK] = 0.25
    return (
        jnp.asarray(pick.reshape(heads * QK, -1), BF),
        jnp.asarray(ones),
        jnp.asarray(np.array(scale, np.float32)[None]),
        jnp.asarray(own, BF),
    )


def nt(a, b):
    return lax.dot_general(a, b, (((1,), (1,)), ((), ())), preferred_element_type=F32)


def tn(a, b):
    return lax.dot_general(a, b, (((0,), (0,)), ((), ())), preferred_element_type=F32)


def nn(a, b):
    return lax.dot_general(a, b, (((1,), (0,)), ((), ())), preferred_element_type=F32)


class Marks:
    def __init__(self, marks, b, block):
        t = lax.broadcasted_iota(jnp.int32, (block, 1), 0)
        first, second, third = marks[b, 0], marks[b, 1], marks[b, 2]
        low = jnp.where(t >= first, first, 0)
        low = jnp.where(t >= second, second, low)
        self.low = jnp.where(t >= third, block, low)
        self.padding = jnp.where(t >= third, 1.0, 0.0).astype(F32)
        self.use = jnp.where(t < marks[b, 3], 1.0, 0.0).astype(F32)
        self.tail = jnp.where(t >= marks[b, 4], 1.0, 0.0).astype(F32)

    def mask(self, at, count):
        t = lax.broadcasted_iota(jnp.int32, (TILE, count), 0) + at
        s = lax.broadcasted_iota(jnp.int32, (TILE, count), 1)
        return (s <= t) & (s >= self.low[at : at + TILE])


def sides(x, pick, ones, h):
    both = nn(x, pick[:, 2 * LANES * h : 2 * LANES * (h + 1)]) + ones
    return both[:, :LANES], both[:, LANES:]


def head_cols(ref, h):
    return ref[:, HEAD_V * h : HEAD_V * (h + 1)]


def output_grads(do_ref, o_ref, den_ref, h):
    do, o, den = head_cols(do_ref, h), head_cols(o_ref, h).astype(F32), head_cols(den_ref, h)
    do = do.astype(F32)
    inverse = 1.0 / den
    dnum = (do * inverse).astype(BF)
    dden = -jnp.sum(do * o, axis=1, keepdims=True) * inverse
    return dnum, dden


def state_kernel(marks, k_ref, v_ref, pick, ones, scale, out_ref, *, heads, block):
    m = Marks(marks, pl.program_id(0), block)
    k = k_ref[...]
    for h in range(heads):
        left, right = sides(k, pick, ones[...], h)
        feat = (left * right * (scale[...] * m.tail)).astype(BF)
        v = head_cols(v_ref, h)
        out_ref[0, h] = tn(feat, jnp.concatenate([v, jnp.ones_like(v)], 1))[:NFEAT]


def grad_state_kernel(
    marks, q_ref, do_ref, o_ref, den_ref, pick, ones, scale, out_ref, *, heads, block
):
    m = Marks(marks, pl.program_id(0), block)
    q = q_ref[...]
    for h in range(heads):
        left, right = sides(q, pick, ones[...], h)
        feat = (left * right * (scale[...] * m.use)).astype(BF)
        dnum, dden = output_grads(do_ref, o_ref, den_ref, h)
        out_ref[0, h] = tn(feat, jnp.concatenate([dnum, dden.astype(BF)], 1))[:NFEAT]


def mixer_kernel(
    marks, q_ref, k_ref, v_ref, s_ref, pick, ones, scale, own, o_ref, den_ref, *, heads, block
):
    m = Marks(marks, pl.program_id(0), block)
    q, k = q_ref[...], k_ref[...]
    for h in range(heads):
        q_own = q * own[h : h + 1, :]
        left, right = sides(q, pick, ones[...], h)
        feat = (left * right * scale[...]).astype(BF)
        before = nn(feat, s_ref[0, h]) * m.use
        v = head_cols(v_ref, h)
        v_one = jnp.concatenate([v, jnp.ones_like(v)], 1)
        for at in range(0, block, TILE):
            count = at + TILE
            prod = nt(q_own[at:count], k[:count])
            score = 1.0 + prod + 0.5 * prod * prod
            score = jnp.where(m.mask(at, count), score, 0.0).astype(BF)
            both = nn(score, v_one[:count]) + before[at:count]
            den = both[:, HEAD_V:] + m.padding[at:count]
            here = (slice(at, count), slice(HEAD_V * h, HEAD_V * (h + 1)))
            o_ref[here] = (both[:, :HEAD_V] / den).astype(BF)
            den_ref[here] = den


def mixer_back_kernel(
    marks,
    q_ref,
    k_ref,
    v_ref,
    do_ref,
    o_ref,
    den_ref,
    s_ref,
    g_ref,
    pick,
    ones,
    scale,
    own,
    dq_ref,
    dk_ref,
    dv_ref,
    dq,
    dk,
    dv,
    *,
    heads,
    block,
):
    m = Marks(marks, pl.program_id(0), block)
    q, k = q_ref[...], k_ref[...]
    first_lane = lax.broadcasted_iota(jnp.int32, (block, HEAD_V), 1) == 0
    dq[...] = jnp.zeros_like(dq)
    dk[...] = jnp.zeros_like(dk)
    for h in range(heads):
        table = pick[:, 2 * LANES * h : 2 * LANES * (h + 1)]
        q_own, k_own = q * own[h : h + 1, :], k * own[h : h + 1, :]
        v = head_cols(v_ref, h)
        dnum, dden = output_grads(do_ref, o_ref, den_ref, h)
        state, carried = s_ref[0, h], g_ref[0, h]

        left, right = sides(q, pick, ones[...], h)
        wide = jnp.concatenate([dnum, jnp.where(first_lane, dden, 0.0).astype(BF)], 1)
        dfeat = nt(wide, state) * (scale[...] * m.use)
        pulled = jnp.concatenate([(dfeat * right).astype(BF), (dfeat * left).astype(BF)], 1)
        dq[...] += nt(pulled, table)

        left, right = sides(k, pick, ones[...], h)
        wide = jnp.concatenate([v, jnp.where(first_lane, 1.0, 0.0).astype(BF)], 1)
        dfeat = nt(wide, carried) * (scale[...] * m.tail)
        pulled = jnp.concatenate([(dfeat * right).astype(BF), (dfeat * left).astype(BF)], 1)
        dk[...] += nt(pulled, table)
        feat = (left * right * (scale[...] * m.tail)).astype(BF)
        dv[...] = nn(feat, carried[:, :HEAD_V])

        for at in range(0, block, TILE):
            count = at + TILE
            prod = nt(q_own[at:count], k[:count])
            one = 1.0 + prod
            mask = m.mask(at, count)
            score = jnp.where(mask, one + 0.5 * prod * prod, 0.0).astype(BF)
            dscore = nt(dnum[at:count], v[:count]) + dden[at:count, :1]
            dprod = jnp.where(mask, dscore * one, 0.0).astype(BF)
            dq[at:count] += nn(dprod, k_own[:count])
            dk[:count] += tn(dprod, q_own[at:count])
            dv[:count] += tn(score, dnum[at:count])
        dv_ref[:, HEAD_V * h : HEAD_V * (h + 1)] = dv[...].astype(BF)
    dq_ref[...] = dq[...].astype(BF)
    dk_ref[...] = dk[...].astype(BF)


def mixer_calls(heads, block, blocks):
    tables = feature_tables(heads)
    narrow = pl.BlockSpec((block, heads * QK), lambda b, marks: (b, 0))
    wide = pl.BlockSpec((block, heads * HEAD_V), lambda b, marks: (b, 0))
    local = pl.BlockSpec((1, heads, NFEAT, 2 * HEAD_V), lambda b, marks: (b, 0, 0, 0))
    state = pl.BlockSpec((1, heads, LANES, 2 * HEAD_V), lambda b, marks: (b, 0, 0, 0))
    fixed = [pl.BlockSpec(t.shape, lambda b, marks: (0, 0)) for t in tables]
    rows = block * blocks

    def call(kernel, specs, used, outs, scratch, cost):
        def run(marks, *args):
            return pl.pallas_call(
                functools.partial(kernel, heads=heads, block=block),
                grid_spec=pltpu.PrefetchScalarGridSpec(
                    num_scalar_prefetch=1,
                    grid=(blocks,),
                    in_specs=specs + fixed[:used],
                    out_specs=[o[0] for o in outs],
                    scratch_shapes=scratch,
                ),
                out_shape=[jax.ShapeDtypeStruct(*o[1:]) for o in outs],
                cost_estimate=pl.CostEstimate(
                    flops=cost * rows * heads, bytes_accessed=rows * heads * 1500, transcendentals=0
                ),
                compiler_params=pltpu.CompilerParams(vmem_limit_bytes=48 * 2**20),
            )(marks, *args, *tables[:used])

        return run

    local_out = (local, (blocks, heads, NFEAT, 2 * HEAD_V), F32)
    wide_b, wide_f = (wide, (rows, heads * HEAD_V), BF), (wide, (rows, heads * HEAD_V), F32)
    narrow_b = (narrow, (rows, heads * QK), BF)
    scratch = [
        pltpu.VMEM((block, heads * QK), F32),
        pltpu.VMEM((block, heads * QK), F32),
        pltpu.VMEM((block, HEAD_V), F32),
    ]
    return (
        call(state_kernel, [narrow, wide], 3, [local_out], [], 500000),
        call(mixer_kernel, [narrow, narrow, wide, state], 4, [wide_b, wide_f], [], 1000000),
        call(grad_state_kernel, [narrow, wide, wide, wide], 3, [local_out], [], 500000),
        call(
            mixer_back_kernel,
            [narrow, narrow, wide, wide, wide, wide, state, state],
            4,
            [narrow_b, narrow_b, wide_b],
            scratch,
            2500000,
        ),
    )


def dot(a, b, ca=1, cb=0):
    return lax.dot_general(a, b, (((ca,), (cb,)), ((), ())), preferred_element_type=F32)


def tie(*values):
    return lax.optimization_barrier(values)


def place_kernel(offsets, *refs, axis):
    *pieces, out, sems = refs
    copies = []
    for i, piece in enumerate(pieces):
        size = piece.shape[axis]
        span = pl.ds(pl.multiple_of(offsets[i], size), size)
        target = out.at[span] if axis == 0 else out.at[:, span]
        copies.append(pltpu.make_async_copy(piece, target, sems.at[i]))
    for copy in copies:
        copy.start()
    for copy in copies:
        copy.wait()


def place(pieces, offsets, axis):
    shape = list(pieces[0].shape)
    shape[axis] = sum(p.shape[axis] for p in pieces)
    size = int(np.prod(shape)) * pieces[0].dtype.itemsize
    return pl.pallas_call(
        functools.partial(place_kernel, axis=axis),
        grid_spec=pltpu.PrefetchScalarGridSpec(
            num_scalar_prefetch=1,
            grid=(),
            in_specs=[pl.BlockSpec(memory_space=pltpu.VMEM)] * len(pieces),
            out_specs=pl.BlockSpec(memory_space=pl.ANY),
            scratch_shapes=[pltpu.SemaphoreType.DMA((len(pieces),))],
        ),
        compiler_params=pltpu.CompilerParams(vmem_limit_bytes=32 * 2**20),
        out_shape=jax.ShapeDtypeStruct(tuple(shape), pieces[0].dtype),
        cost_estimate=pl.CostEstimate(flops=0, bytes_accessed=2 * size, transcendentals=0),
    )(jnp.stack(offsets).astype(jnp.int32), *pieces)


def widen_kernel(where, *refs, group):
    *shares, out = refs
    count, core = (len(shares) + 1) // 2, where[1]
    piece = shares[0].shape[2]
    for d in range(count):
        plane = lax.rem(where[0] + count - d, count)
        batch, part = plane // group, lax.rem(plane, group)
        for j in range(CORES):
            got = shares[d][j].astype(F32)
            if d:
                got = got + shares[2 * count - 1 - d][j].astype(F32)
            k = core if j == 0 else 1 - core
            at = pl.multiple_of((k * group + part) * piece, piece)
            out[batch, :, pl.ds(at, piece)] = got


def widen(shares, feat_rank, core, micro, group, width):
    _, block, piece = shares[0].shape
    tile = 128
    return pl.pallas_call(
        functools.partial(widen_kernel, group=group),
        grid_spec=pltpu.PrefetchScalarGridSpec(
            num_scalar_prefetch=1,
            grid=(block // tile,),
            in_specs=[pl.BlockSpec((CORES, tile, piece), lambda i, w: (0, i, 0))] * len(shares),
            out_specs=pl.BlockSpec((micro, tile, width), lambda i, w: (0, i, 0)),
        ),
        out_shape=jax.ShapeDtypeStruct((micro, block, width), F32),
        compiler_params=pltpu.CompilerParams(vmem_limit_bytes=48 * 2**20),
    )(jnp.stack([feat_rank, core]).astype(jnp.int32), *shares)


def on_device(
    tokens,
    cotangent,
    lengths,
    w_query,
    w_key,
    w_value,
    w_output,
    w_gate,
    w_up,
    w_down,
    gain_mixer,
    gain_mlp,
):
    micro, block, width = tokens.shape
    seq_count, feat_count = lax.axis_size("seq"), lax.axis_size("feat")
    seq_rank, feat_rank = lax.axis_index("seq"), lax.axis_index("feat")
    group = feat_count // micro
    ranks = CORES * group
    chips = seq_count // CORES
    chip, core = seq_rank // CORES, seq_rank % CORES
    batch, part = feat_rank // group, feat_rank % group
    rank = core * group + part
    rows = CORES * block
    piece = width // ranks
    heads = HEADS // ranks

    def move(value, target):
        pairs = []
        for s in range(seq_count):
            for f in range(feat_count):
                there = target(s // CORES, s % CORES, f // group, f % group)
                if there is not None:
                    c2, k2, m2, l2 = there
                    pairs.append(
                        (s * feat_count + f, (c2 * CORES + k2) * feat_count + m2 * group + l2)
                    )
        return lax.ppermute(value, ("seq", "feat"), pairs)

    def to_core(value):
        return move(value, lambda c, k, m, l: (c, 1 - k, m, l))

    def to_part(value, d):
        return move(value, lambda c, k, m, l: (c, k, m, l ^ d))

    def to_chip(value, mask):
        return move(value, lambda c, k, m, l: (c ^ mask, k, m, l))

    def shift_chip(value, d):
        return move(value, lambda c, k, m, l: (c + d, k, m, l) if 0 <= c + d < chips else None)

    def spread(value):
        return (
            move(value, lambda c, k, m, l: (c, m, k, l)),
            move(value, lambda c, k, m, l: (c, m, 1 - k, l)),
        )

    def unspread(same, other):
        return (
            move(same, lambda c, k, m, l: (c, m, k, l)),
            move(other, lambda c, k, m, l: (c, 1 - m, k, l)),
        )

    def ordered(first_if_zero, second_if_zero, bit, axis):
        return jnp.where(
            bit == 0,
            jnp.concatenate([first_if_zero, second_if_zero], axis),
            jnp.concatenate([second_if_zero, first_if_zero], axis),
        )

    chip_groups = [[c * CORES + k for c in range(chips)] for k in range(CORES)]

    def gather_chips(owns, axis):
        size = owns[0].shape[axis]
        bits = [1 << i for i in range(chips.bit_length() - 1)]
        pieces, offsets = [], []
        for own, order, k in zip(owns, (bits, bits[::-1]), (batch, 1 - batch)):
            held = {0: own}
            for bit in order:
                for mask in list(held):
                    held[mask | bit] = to_chip(held[mask], bit)
            for mask, got in held.items():
                pieces.append(got)
                offsets.append(((chip ^ mask) * CORES + k) * size)
        return place(pieces, offsets, axis)

    def gather_chips_bulk(owns, axis):
        size = owns[0].shape[axis]
        both = place(list(owns), [batch * size, (1 - batch) * size], axis)
        return lax.all_gather(
            both, "seq", axis=axis, tiled=True, axis_index_groups=chip_groups
        )

    def sum_chips(value, axis):
        return lax.psum_scatter(
            value, "seq", scatter_dimension=axis, tiled=True, axis_index_groups=chip_groups
        )

    def send_halves(mine, axis):
        size = mine.shape[axis] // CORES
        same = lax.dynamic_slice_in_dim(mine, batch * size, size, axis)
        other = lax.dynamic_slice_in_dim(mine, (1 - batch) * size, size, axis)
        return unspread(same, other)

    def add(halves):
        return halves[0].astype(F32) + halves[1].astype(F32)

    def send_parts(own):
        return [to_part(own, d) for d in range(1, group)]

    def gather_ranks(own, arrived):
        found = []
        for d, here in enumerate([own, *arrived]):
            found.append((core * group + (part ^ d), here))
            found.append(((1 - core) * group + (part ^ d), to_core(here)))
        return found

    def reduce_begin(partial):
        totals = []
        for d in range(group - 1, -1, -1):
            away = to_core(partial((1 - core) * group + (part ^ d)).astype(BF))
            total = partial(core * group + (part ^ d)) + away.astype(F32)
            totals.append(total.astype(BF) if d else total)
        return totals[-1], totals[-2::-1]

    def reduce_send(totals):
        return [to_part(total, d + 1) for d, total in enumerate(totals)]

    def reduce_end(own, arrived):
        return sum((got.astype(F32) for got in arrived), own)

    def sum_ranks(value):
        for d in [1 << i for i in range(group.bit_length() - 1)]:
            value = value + to_part(value, d)
        return value + to_core(value)

    def row_piece(value, r):
        return lax.dynamic_slice_in_dim(value, r * piece, piece, 0)

    def column_piece(value, r):
        return lax.dynamic_slice_in_dim(value, r * piece, piece, 1)

    def chip_tokens(value):
        own = lax.dynamic_index_in_dim(value, batch, 0, False)
        return place([own, to_core(own)], [core * block, (1 - core) * block], 0)

    tokens_c = chip_tokens(tokens)
    grad_out = chip_tokens(cotangent)

    def half(value, k):
        return lax.dynamic_slice_in_dim(value, k * block, block, 0)

    qk_width, v_width = heads * QK, heads * HEAD_V
    qkv_owns = spread(jnp.concatenate([w_query, w_key, w_value], 1))
    gains = lax.all_gather(jnp.stack([gain_mixer, gain_mlp]), "seq", axis=1, tiled=True)
    w_output, gains, *qkv_owns = tie(w_output, gains, *qkv_owns)
    gains = gains.astype(F32)
    mixer_gain, mlp_gain = gains[0], gains[1]
    output_owns = spread(w_output)
    qkv_full = gather_chips(qkv_owns, 0)

    bounds = jnp.cumsum(lax.dynamic_index_in_dim(lengths, batch, 0, False))

    def segment_of(p):
        return jnp.sum((p[..., None] >= bounds).astype(jnp.int32), axis=-1)

    start = chip * rows
    base = start + block * jnp.arange(CORES + 1, dtype=jnp.int32)
    edges = jnp.where(base == 0, -1, segment_of(base - 1))
    keep = (edges[1:] == edges[:-1]).astype(F32)
    base = base[:-1]
    ends = jnp.concatenate([jnp.zeros((1,), jnp.int32), bounds])
    open_end = jnp.where((edges[:-1] < 0) | (edges[:-1] > 2), 0, ends[edges[:-1] + 1] - base)
    tail_start = jnp.where(edges[1:] > 2, block, ends[edges[1:]] - base)
    marks = jnp.concatenate(
        [bounds[None, :] - base[:, None], open_end[:, None], tail_start[:, None]], 1
    ).astype(jnp.int32)

    tokens_f = tokens_c.astype(F32)
    inv_one = lax.rsqrt(jnp.mean(tokens_f * tokens_f, axis=-1, keepdims=True) + EPS)
    normed = (tokens_f * inv_one * mixer_gain).astype(BF)
    qkv = dot(normed, qkv_full).astype(BF)
    w_gate, qkv, *output_owns = tie(w_gate.T, qkv, *output_owns)
    gate_owns = spread(w_gate)
    output_full = gather_chips(output_owns, 0)

    query, keys = qkv[:, :qk_width], qkv[:, qk_width : 2 * qk_width]
    values = qkv[:, 2 * qk_width :]
    local_states, mixer, grad_states, mixer_back = mixer_calls(heads, block, CORES)

    def pack(state, total):
        total = jnp.pad(total, ((0, 0), (0, -NFEAT % HEAD_V))).reshape(-1, HEAD_V)
        return jnp.concatenate([state.reshape(-1, HEAD_V), total], 0).astype(BF)

    def unpack(flat):
        flat = flat.astype(F32)
        cut = heads * NFEAT
        return (
            flat[:cut].reshape(heads, NFEAT, HEAD_V),
            flat[cut:].reshape(heads, -1)[:, :NFEAT],
        )

    def scan_blocks(both, blocks_order, step, meanwhile):
        state, total = both[..., :HEAD_V], both[..., HEAD_V]
        at_end = (state[blocks_order[0]], total[blocks_order[0]])
        for i in blocks_order[1:]:
            carry_keep = keep[i]
            at_end = (
                state[i] + carry_keep * at_end[0],
                total[i] + carry_keep * at_end[1],
            )
        message = pack(*at_end)
        run = None
        arrived = [shift_chip(message, step * d) for d in range(1, chips)]
        *arrived, state, total, meanwhile = tie(*arrived, state, total, meanwhile)
        for d in range(1, chips):
            got = unpack(arrived[d - 1])
            other = chip - step * d
            if step > 0:
                same = edges[0] == segment_of((other + 1) * rows - 1)
            else:
                same = edges[CORES] == segment_of(other * rows - 1)
            weight = (same & (other >= 0) & (other < chips)).astype(F32)
            term = (weight * got[0], weight * got[1])
            run = term if run is None else (run[0] + term[0], run[1] + term[1])
        found = {}
        for i in blocks_order:
            found[i] = run
            run = (state[i] + keep[i] * run[0], total[i] + keep[i] * run[1])
        state, total = (jnp.stack([found[i][j] for i in range(CORES)]) for j in range(2))
        total = jnp.broadcast_to(total[..., None], state.shape)
        both = jnp.concatenate([state, total], -1).astype(BF)
        both = jnp.pad(both, ((0, 0), (0, 0), (0, LANES - NFEAT), (0, 0)))
        return both, meanwhile

    (local,) = local_states(marks, keys, values)
    states, gate_owns = scan_blocks(local, list(range(CORES)), 1, gate_owns)
    up_owns = spread(tie(w_up.T, states)[0])
    gate_full = gather_chips_bulk(gate_owns, 1)
    mixer_own, denom = mixer(marks, query, keys, values, states)

    arrived = send_parts(mixer_own)
    w_down, *up_owns = tie(w_down, *up_owns)
    down_owns = spread(w_down)
    up_full = gather_chips_bulk(up_owns, 1)
    mixer_parts = gather_ranks(mixer_own, arrived)
    branch_own = sum(dot(got, row_piece(output_full, r)) for r, got in mixer_parts).astype(BF)
    arrived = send_parts(branch_own)
    *arrived, gate_full, down_owns = tie(*arrived, gate_full, down_owns)
    down_full = gather_chips(down_owns, 1)
    branch_parts = gather_ranks(branch_own, arrived)
    branch = place([got for _, got in branch_parts], [r * piece for r, _ in branch_parts], 1)
    hidden_state = tokens_f + branch.astype(F32)
    inv_two = lax.rsqrt(jnp.mean(hidden_state * hidden_state, axis=-1, keepdims=True) + EPS)
    normed_two = (hidden_state * inv_two * mlp_gain).astype(BF)

    grad_hidden = dot(grad_out, down_full, 1, 1).astype(BF).astype(F32)
    gate = dot(normed_two, gate_full, 1, 1).astype(BF).astype(F32)
    upward = dot(normed_two, up_full, 1, 1).astype(BF).astype(F32)
    logistic = jax.nn.sigmoid(gate)
    activated = gate * logistic
    hidden = (activated * upward).astype(BF)
    grad_gate_f = grad_hidden * upward * logistic * (1.0 + gate * (1.0 - logistic))
    grad_up_f = grad_hidden * activated
    grad_gate_b, grad_up_b = grad_gate_f.astype(BF), grad_up_f.astype(BF)
    inner_two = sum_ranks(jnp.sum(grad_gate_f * gate + grad_up_f * upward, axis=1)) / width
    own, totals = reduce_begin(
        lambda r: dot(grad_gate_b, column_piece(gate_full, r))
        + dot(grad_up_b, column_piece(up_full, r))
    )
    inner_two, *totals = tie(inner_two, *totals)
    arrived = reduce_send(totals)
    up_sum = sum_chips(dot(grad_up_b, normed_two, 0, 0).astype(BF), 1)
    gate_sum = dot(grad_gate_b, normed_two, 0, 0).astype(BF)
    up_sum, gate_sum, *arrived = tie(up_sum, gate_sum, *arrived)
    normed_grad = reduce_end(own, arrived)
    gate_sum = sum_chips(gate_sum, 1)
    up_halves = send_halves(up_sum, 1)
    tokens_own = column_piece(tokens_c, rank).astype(F32)
    hidden_own = tokens_own + branch_own.astype(F32)
    scaled_two = hidden_own * inv_two
    mlp_gain_own = lax.dynamic_slice_in_dim(mlp_gain, rank * piece, piece, 0)
    hidden_grad = column_piece(grad_out, rank).astype(F32) + inv_two * (
        normed_grad * mlp_gain_own - scaled_two * inner_two[:, None]
    )
    grad_gain_mlp = jnp.sum(normed_grad * scaled_two, axis=0)
    branch_grad = hidden_grad.astype(BF)

    own, totals = reduce_begin(lambda r: dot(branch_grad, row_piece(output_full, r), 1, 1))
    arrived = reduce_send(totals)
    mlp_own, mlp_totals = reduce_begin(lambda r: dot(hidden, column_piece(down_full, r)))
    down_sum = dot(hidden, grad_out, 0, 0).astype(BF)
    arrived, mlp_own, mlp_totals, down_sum, gate_sum, up_halves = tie(
        arrived, mlp_own, mlp_totals, down_sum, gate_sum, up_halves
    )
    mixer_grad = reduce_end(own, arrived)
    mlp_arrived = reduce_send(mlp_totals)
    down_sum = sum_chips(down_sum, 1)
    gate_halves = send_halves(gate_sum, 1)
    output_sum = place(
        [dot(got, branch_grad, 0, 0).astype(BF) for _, got in mixer_parts],
        [r * piece for r, _ in mixer_parts],
        0,
    )
    output_sum = sum_chips(output_sum, 0)
    (grad_local,) = grad_states(marks, query, mixer_grad, mixer_own, denom)
    carried, gate_halves = scan_blocks(
        grad_local, list(range(CORES))[::-1], -1, gate_halves
    )
    grad_qkv = jnp.concatenate(
        mixer_back(
            marks, query, keys, values, mixer_grad, mixer_own, denom, states, carried
        ),
        1,
    )
    inner_one = jnp.sum(grad_qkv.astype(F32) * qkv.astype(F32), axis=1)
    inner_one = sum_ranks(inner_one) / width
    grad_qkv, mlp_arrived, down_sum = tie(grad_qkv, mlp_arrived, down_sum)
    mixed_own = (hidden_own + reduce_end(mlp_own, mlp_arrived)).astype(BF)
    mixed_halves = unspread(half(mixed_own, batch), half(mixed_own, 1 - batch))
    own, totals = reduce_begin(lambda r: dot(grad_qkv, row_piece(qkv_full, r), 1, 1))
    inner_one, *totals = tie(inner_one, *totals)
    arrived = reduce_send(totals)
    down_halves = send_halves(down_sum, 1)
    qkv_sum = dot(normed, grad_qkv, 0, 0).astype(BF)
    arrived, mixed_halves, down_halves, qkv_sum, output_sum = tie(
        arrived, mixed_halves, down_halves, qkv_sum, output_sum
    )
    input_normed = reduce_end(own, arrived)
    qkv_sum = sum_chips(qkv_sum, 0)
    mixed = ordered(mixed_halves[0][None], mixed_halves[1][None], core, 0)
    scaled_one = tokens_own * inv_one
    mixer_gain_own = lax.dynamic_slice_in_dim(mixer_gain, rank * piece, piece, 0)
    grad_gain_mixer = jnp.sum(input_normed * scaled_one, axis=0)
    input_own = (
        hidden_grad
        + inv_one * (input_normed * mixer_gain_own - scaled_one * inner_one[:, None])
    ).astype(BF)

    gain_grads = lax.dynamic_update_slice_in_dim(
        jnp.zeros((2, width), F32), jnp.stack([grad_gain_mixer, grad_gain_mlp]), rank * piece, 1
    )
    planes = [
        move(gain_grads, lambda c, k, m, l: (c, k, *divmod((m * group + l) ^ d, group)))
        for d in range(1, feat_count)
    ]
    other_half = to_core(half(input_own, 1 - core))
    input_own, other_half, *planes = tie(input_own, other_half, *planes)
    input_pair = jnp.stack([half(input_own, core), other_half])

    def step_plane(value, step, first):
        def target(c, k, m, l):
            here = m * group + l
            behind = here if step > 0 else feat_count - 1 - here
            if behind < first or behind == feat_count - 1:
                return None
            return (c, k, *divmod(here + step, group))

        return move(value, target)

    gain_grads = sum(planes, gain_grads)
    output_halves = send_halves(output_sum, 0)
    hops = [to_core] + [
        functools.partial(to_chip, mask=1 << i) for i in range(chips.bit_length() - 1)
    ]
    ups, downs = [input_pair], [input_pair]
    for d in range(feat_count - 1):
        up, down = step_plane(ups[-1], 1, d), step_plane(downs[-1], -1, d)
        if hops:
            up, down, gain_grads, got = tie(up, down, gain_grads, hops[0](gain_grads))
            gain_grads, hops = gain_grads + got, hops[1:]
        if d == 0:
            up, down, qkv_sum = tie(up, down, qkv_sum)
            qkv_halves = send_halves(qkv_sum, 0)
        if d == 1:
            up, down, output_halves = tie(up, down, output_halves)
        ups.append(up), downs.append(down)
    for hop in hops:
        gain_grads = gain_grads + hop(gain_grads)
    input_grad = widen(ups + downs[1:], feat_rank, core, micro, group, width)

    shard = width // seq_count
    gain_grads = lax.dynamic_slice_in_dim(gain_grads, seq_rank * shard, shard, 1)

    grad_qkv_w = add(qkv_halves)
    return (
        mixed,
        input_grad,
        grad_qkv_w[:, :qk_width],
        grad_qkv_w[:, qk_width : 2 * qk_width],
        grad_qkv_w[:, 2 * qk_width :],
        add(output_halves),
        add(gate_halves).T,
        add(up_halves).T,
        add(down_halves),
        gain_grads[0],
        gain_grads[1],
    )


def solution(mesh):
    in_specs = (
        P(None, "seq", None),
        P(None, "seq", None),
        P(),
        P("seq", "feat"),
        P("seq", "feat"),
        P("seq", "feat"),
        P("seq", "feat"),
        P("seq", "feat"),
        P("seq", "feat"),
        P("feat", "seq"),
        P("seq"),
        P("seq"),
    )
    out_specs = (
        P(None, "seq", "feat"),
        P(None, "seq", None),
        P("seq", "feat"),
        P("seq", "feat"),
        P("seq", "feat"),
        P("seq", "feat"),
        P("seq", "feat"),
        P("seq", "feat"),
        P("feat", "seq"),
        P("seq"),
        P("seq"),
    )
    return jax.shard_map(
        on_device, mesh=mesh, in_specs=in_specs, out_specs=out_specs, check_vma=False
    )
```

```python
import functools

import jax
import jax.numpy as jnp
import numpy as np
from jax import lax
from jax.experimental import pallas as pl
from jax.experimental.pallas import tpu as pltpu
from jax.sharding import PartitionSpec as P

HEADS = 16
HEAD_V = 128
QK = 16
NFEAT = 160
CORES = 2
EPS = 1e-05
BF = jnp.bfloat16
F32 = jnp.float32


LANES = 256
TILE = 256


def feature_tables(heads):
    left, right, scale = [-1], [-1], [1.0]
    for i in range(QK):
        left.append(i), right.append(-1), scale.append(1.0)
    for i in range(QK):
        for j in range(i, QK):
            left.append(i), right.append(j), scale.append(1.0 if i < j else 0.7071067811865476)
    padding = LANES - len(left)
    left, right, scale = left + [-2] * padding, right + [-2] * padding, scale + [0.0] * padding
    both = np.array(left + right)
    pick = np.zeros((heads * QK, heads, 2 * LANES), np.float32)
    for h in range(heads):
        pick[h * QK : (h + 1) * QK, h] = 0.5 * (np.arange(QK)[:, None] == both[None, :])
    ones = (both == -1).astype(np.float32)[None]
    own = np.zeros((8, heads * QK), np.float32)
    for h in range(heads):
        own[h, h * QK : (h + 1) * QK] = 0.25
    return (
        jnp.asarray(pick.reshape(heads * QK, -1), BF),
        jnp.asarray(ones),
        jnp.asarray(np.array(scale, np.float32)[None]),
        jnp.asarray(own, BF),
    )


def nt(a, b):
    return lax.dot_general(a, b, (((1,), (1,)), ((), ())), preferred_element_type=F32)


def tn(a, b):
    return lax.dot_general(a, b, (((0,), (0,)), ((), ())), preferred_element_type=F32)


def nn(a, b):
    return lax.dot_general(a, b, (((1,), (0,)), ((), ())), preferred_element_type=F32)


class Marks:
    def __init__(self, marks, b, block):
        t = lax.broadcasted_iota(jnp.int32, (block, 1), 0)
        first, second, third = marks[b, 0], marks[b, 1], marks[b, 2]
        low = jnp.where(t >= first, first, 0)
        low = jnp.where(t >= second, second, low)
        self.low = jnp.where(t >= third, block, low)
        self.padding = jnp.where(t >= third, 1.0, 0.0).astype(F32)
        self.use = jnp.where(t < marks[b, 3], 1.0, 0.0).astype(F32)
        self.tail = jnp.where(t >= marks[b, 4], 1.0, 0.0).astype(F32)

    def mask(self, at, count):
        t = lax.broadcasted_iota(jnp.int32, (TILE, count), 0) + at
        s = lax.broadcasted_iota(jnp.int32, (TILE, count), 1)
        return (s <= t) & (s >= self.low[at : at + TILE])


def sides(x, pick, ones, h):
    both = nn(x, pick[:, 2 * LANES * h : 2 * LANES * (h + 1)]) + ones
    return both[:, :LANES], both[:, LANES:]


def head_cols(ref, h):
    return ref[:, HEAD_V * h : HEAD_V * (h + 1)]


def output_grads(do_ref, o_ref, den_ref, h):
    do, o, den = head_cols(do_ref, h), head_cols(o_ref, h).astype(F32), head_cols(den_ref, h)
    do = do.astype(F32)
    inverse = 1.0 / den
    dnum = (do * inverse).astype(BF)
    dden = -jnp.sum(do * o, axis=1, keepdims=True) * inverse
    return dnum, dden


def state_kernel(marks, k_ref, v_ref, pick, ones, scale, out_ref, *, heads, block):
    m = Marks(marks, pl.program_id(0), block)
    k = k_ref[...]
    for h in range(heads):
        left, right = sides(k, pick, ones[...], h)
        feat = (left * right * (scale[...] * m.tail)).astype(BF)
        v = head_cols(v_ref, h)
        out_ref[0, h] = tn(feat, jnp.concatenate([v, jnp.ones_like(v)], 1))[:NFEAT]


def grad_state_kernel(
    marks, q_ref, do_ref, o_ref, den_ref, pick, ones, scale, out_ref, *, heads, block
):
    m = Marks(marks, pl.program_id(0), block)
    q = q_ref[...]
    for h in range(heads):
        left, right = sides(q, pick, ones[...], h)
        feat = (left * right * (scale[...] * m.use)).astype(BF)
        dnum, dden = output_grads(do_ref, o_ref, den_ref, h)
        out_ref[0, h] = tn(feat, jnp.concatenate([dnum, dden.astype(BF)], 1))[:NFEAT]


def mixer_kernel(
    marks, q_ref, k_ref, v_ref, s_ref, pick, ones, scale, own, o_ref, den_ref, *, heads, block
):
    m = Marks(marks, pl.program_id(0), block)
    q, k = q_ref[...], k_ref[...]
    for h in range(heads):
        q_own = q * own[h : h + 1, :]
        left, right = sides(q, pick, ones[...], h)
        feat = (left * right * scale[...]).astype(BF)
        before = nn(feat, s_ref[0, h]) * m.use
        v = head_cols(v_ref, h)
        v_one = jnp.concatenate([v, jnp.ones_like(v)], 1)
        for at in range(0, block, TILE):
            count = at + TILE
            prod = nt(q_own[at:count], k[:count])
            score = 1.0 + prod + 0.5 * prod * prod
            score = jnp.where(m.mask(at, count), score, 0.0).astype(BF)
            both = nn(score, v_one[:count]) + before[at:count]
            den = both[:, HEAD_V:] + m.padding[at:count]
            here = (slice(at, count), slice(HEAD_V * h, HEAD_V * (h + 1)))
            o_ref[here] = (both[:, :HEAD_V] / den).astype(BF)
            den_ref[here] = den


def mixer_back_kernel(
    marks,
    q_ref,
    k_ref,
    v_ref,
    do_ref,
    o_ref,
    den_ref,
    s_ref,
    g_ref,
    pick,
    ones,
    scale,
    own,
    dq_ref,
    dk_ref,
    dv_ref,
    dq,
    dk,
    dv,
    *,
    heads,
    block,
):
    m = Marks(marks, pl.program_id(0), block)
    q, k = q_ref[...], k_ref[...]
    first_lane = lax.broadcasted_iota(jnp.int32, (block, HEAD_V), 1) == 0
    dq[...] = jnp.zeros_like(dq)
    dk[...] = jnp.zeros_like(dk)
    for h in range(heads):
        table = pick[:, 2 * LANES * h : 2 * LANES * (h + 1)]
        q_own, k_own = q * own[h : h + 1, :], k * own[h : h + 1, :]
        v = head_cols(v_ref, h)
        dnum, dden = output_grads(do_ref, o_ref, den_ref, h)
        state, carried = s_ref[0, h], g_ref[0, h]

        left, right = sides(q, pick, ones[...], h)
        wide = jnp.concatenate([dnum, jnp.where(first_lane, dden, 0.0).astype(BF)], 1)
        dfeat = nt(wide, state) * (scale[...] * m.use)
        pulled = jnp.concatenate([(dfeat * right).astype(BF), (dfeat * left).astype(BF)], 1)
        dq[...] += nt(pulled, table)

        left, right = sides(k, pick, ones[...], h)
        wide = jnp.concatenate([v, jnp.where(first_lane, 1.0, 0.0).astype(BF)], 1)
        dfeat = nt(wide, carried) * (scale[...] * m.tail)
        pulled = jnp.concatenate([(dfeat * right).astype(BF), (dfeat * left).astype(BF)], 1)
        dk[...] += nt(pulled, table)
        feat = (left * right * (scale[...] * m.tail)).astype(BF)
        dv[...] = nn(feat, carried[:, :HEAD_V])

        for at in range(0, block, TILE):
            count = at + TILE
            prod = nt(q_own[at:count], k[:count])
            one = 1.0 + prod
            mask = m.mask(at, count)
            score = jnp.where(mask, one + 0.5 * prod * prod, 0.0).astype(BF)
            dscore = nt(dnum[at:count], v[:count]) + dden[at:count, :1]
            dprod = jnp.where(mask, dscore * one, 0.0).astype(BF)
            dq[at:count] += nn(dprod, k_own[:count])
            dk[:count] += tn(dprod, q_own[at:count])
            dv[:count] += tn(score, dnum[at:count])
        dv_ref[:, HEAD_V * h : HEAD_V * (h + 1)] = dv[...].astype(BF)
    dq_ref[...] = dq[...].astype(BF)
    dk_ref[...] = dk[...].astype(BF)


def mixer_calls(heads, block, blocks):
    tables = feature_tables(heads)
    narrow = pl.BlockSpec((block, heads * QK), lambda b, marks: (b, 0))
    wide = pl.BlockSpec((block, heads * HEAD_V), lambda b, marks: (b, 0))
    local = pl.BlockSpec((1, heads, NFEAT, 2 * HEAD_V), lambda b, marks: (b, 0, 0, 0))
    state = pl.BlockSpec((1, heads, LANES, 2 * HEAD_V), lambda b, marks: (b, 0, 0, 0))
    fixed = [pl.BlockSpec(t.shape, lambda b, marks: (0, 0)) for t in tables]
    rows = block * blocks

    def call(kernel, specs, used, outs, scratch, cost):
        def run(marks, *args):
            return pl.pallas_call(
                functools.partial(kernel, heads=heads, block=block),
                grid_spec=pltpu.PrefetchScalarGridSpec(
                    num_scalar_prefetch=1,
                    grid=(blocks,),
                    in_specs=specs + fixed[:used],
                    out_specs=[o[0] for o in outs],
                    scratch_shapes=scratch,
                ),
                out_shape=[jax.ShapeDtypeStruct(*o[1:]) for o in outs],
                cost_estimate=pl.CostEstimate(
                    flops=cost * rows * heads, bytes_accessed=rows * heads * 1500, transcendentals=0
                ),
                compiler_params=pltpu.CompilerParams(vmem_limit_bytes=48 * 2**20),
            )(marks, *args, *tables[:used])

        return run

    local_out = (local, (blocks, heads, NFEAT, 2 * HEAD_V), F32)
    wide_b, wide_f = (wide, (rows, heads * HEAD_V), BF), (wide, (rows, heads * HEAD_V), F32)
    narrow_b = (narrow, (rows, heads * QK), BF)
    scratch = [
        pltpu.VMEM((block, heads * QK), F32),
        pltpu.VMEM((block, heads * QK), F32),
        pltpu.VMEM((block, HEAD_V), F32),
    ]
    return (
        call(state_kernel, [narrow, wide], 3, [local_out], [], 500000),
        call(mixer_kernel, [narrow, narrow, wide, state], 4, [wide_b, wide_f], [], 1000000),
        call(grad_state_kernel, [narrow, wide, wide, wide], 3, [local_out], [], 500000),
        call(
            mixer_back_kernel,
            [narrow, narrow, wide, wide, wide, wide, state, state],
            4,
            [narrow_b, narrow_b, wide_b],
            scratch,
            2500000,
        ),
    )


def dot(a, b, ca=1, cb=0):
    return lax.dot_general(a, b, (((ca,), (cb,)), ((), ())), preferred_element_type=F32)


def tie(*values):
    return lax.optimization_barrier(values)


def place_kernel(offsets, *refs, axis):
    *pieces, out, sems = refs
    copies = []
    for i, piece in enumerate(pieces):
        size = piece.shape[axis]
        span = pl.ds(pl.multiple_of(offsets[i], size), size)
        target = out.at[span] if axis == 0 else out.at[:, span]
        copies.append(pltpu.make_async_copy(piece, target, sems.at[i]))
    for copy in copies:
        copy.start()
    for copy in copies:
        copy.wait()


def place(pieces, offsets, axis):
    shape = list(pieces[0].shape)
    shape[axis] = sum(p.shape[axis] for p in pieces)
    size = int(np.prod(shape)) * pieces[0].dtype.itemsize
    return pl.pallas_call(
        functools.partial(place_kernel, axis=axis),
        grid_spec=pltpu.PrefetchScalarGridSpec(
            num_scalar_prefetch=1,
            grid=(),
            in_specs=[pl.BlockSpec(memory_space=pltpu.VMEM)] * len(pieces),
            out_specs=pl.BlockSpec(memory_space=pl.ANY),
            scratch_shapes=[pltpu.SemaphoreType.DMA((len(pieces),))],
        ),
        compiler_params=pltpu.CompilerParams(vmem_limit_bytes=32 * 2**20),
        out_shape=jax.ShapeDtypeStruct(tuple(shape), pieces[0].dtype),
        cost_estimate=pl.CostEstimate(flops=0, bytes_accessed=2 * size, transcendentals=0),
    )(jnp.stack(offsets).astype(jnp.int32), *pieces)


def widen_kernel(where, *refs, group):
    *shares, out = refs
    count, core = (len(shares) + 1) // 2, where[1]
    piece = shares[0].shape[2]
    for d in range(count):
        plane = lax.rem(where[0] + count - d, count)
        batch, part = plane // group, lax.rem(plane, group)
        for j in range(CORES):
            got = shares[d][j].astype(F32)
            if d:
                got = got + shares[2 * count - 1 - d][j].astype(F32)
            k = core if j == 0 else 1 - core
            at = pl.multiple_of((k * group + part) * piece, piece)
            out[batch, :, pl.ds(at, piece)] = got


def widen(shares, feat_rank, core, micro, group, width):
    _, block, piece = shares[0].shape
    tile = 128
    return pl.pallas_call(
        functools.partial(widen_kernel, group=group),
        grid_spec=pltpu.PrefetchScalarGridSpec(
            num_scalar_prefetch=1,
            grid=(block // tile,),
            in_specs=[pl.BlockSpec((CORES, tile, piece), lambda i, w: (0, i, 0))] * len(shares),
            out_specs=pl.BlockSpec((micro, tile, width), lambda i, w: (0, i, 0)),
        ),
        out_shape=jax.ShapeDtypeStruct((micro, block, width), F32),
        compiler_params=pltpu.CompilerParams(vmem_limit_bytes=48 * 2**20),
    )(jnp.stack([feat_rank, core]).astype(jnp.int32), *shares)


def on_device(
    tokens,
    cotangent,
    lengths,
    w_query,
    w_key,
    w_value,
    w_output,
    w_gate,
    w_up,
    w_down,
    gain_mixer,
    gain_mlp,
):
    micro, block, width = tokens.shape
    seq_count, feat_count = lax.axis_size("seq"), lax.axis_size("feat")
    seq_rank, feat_rank = lax.axis_index("seq"), lax.axis_index("feat")
    group = feat_count // micro
    ranks = CORES * group
    chips = seq_count // CORES
    chip, core = seq_rank // CORES, seq_rank % CORES
    batch, part = feat_rank // group, feat_rank % group
    rank = core * group + part
    rows = CORES * block
    piece = width // ranks
    heads = HEADS // ranks

    def move(value, target):
        pairs = []
        for s in range(seq_count):
            for f in range(feat_count):
                here = (s // CORES, s % CORES, f // group, f % group)
                there = target(*here)
                if there is not None and there != here:
                    c2, k2, m2, l2 = there
                    pairs.append(
                        (s * feat_count + f, (c2 * CORES + k2) * feat_count + m2 * group + l2)
                    )
        return lax.ppermute(value, ("seq", "feat"), pairs)

    def to_core(value):
        return move(value, lambda c, k, m, l: (c, 1 - k, m, l))

    def to_part(value, d):
        return move(value, lambda c, k, m, l: (c, k, m, l ^ d))

    def to_chip(value, mask):
        return move(value, lambda c, k, m, l: (c ^ mask, k, m, l))

    def shift_chip(value, d):
        return move(value, lambda c, k, m, l: (c + d, k, m, l) if 0 <= c + d < chips else None)

    def spread(value):
        moved = move(value, lambda c, k, m, l: (c, m, k, l))
        other = move(value, lambda c, k, m, l: (c, m, 1 - k, l))
        return jnp.where(core == batch, value, moved), other

    def unspread(same, other):
        moved = move(same, lambda c, k, m, l: (c, m, k, l))
        other = move(other, lambda c, k, m, l: (c, 1 - m, k, l))
        return jnp.where(core == batch, same, moved), other

    def ordered(first_if_zero, second_if_zero, bit, axis):
        return jnp.where(
            bit == 0,
            jnp.concatenate([first_if_zero, second_if_zero], axis),
            jnp.concatenate([second_if_zero, first_if_zero], axis),
        )

    chip_groups = [[c * CORES + k for c in range(chips)] for k in range(CORES)]

    bits = [1 << i for i in range(chips.bit_length() - 1)]
    orders = (bits, bits[::-1])

    def all_hops(owns):
        helds = [{0: own} for own in owns]
        for held, order in zip(helds, orders):
            for bit in order:
                for mask in list(held):
                    held[mask | bit] = to_chip(held[mask], bit)
        return helds

    def straight(owns):
        return [
            {mask: to_chip(own, mask) if mask else own for mask in range(chips)} for own in owns
        ]

    def place_chips(helds, axis):
        size = helds[0][0].shape[axis]
        pieces, offsets = [], []
        for held, k in zip(helds, (batch, 1 - batch)):
            for mask, got in held.items():
                pieces.append(got)
                offsets.append(((chip ^ mask) * CORES + k) * size)
        return place(pieces, offsets, axis)

    def gather_chips_bulk(owns, axis):
        size = owns[0].shape[axis]
        both = place(list(owns), [batch * size, (1 - batch) * size], axis)
        return lax.all_gather(
            both, "seq", axis=axis, tiled=True, axis_index_groups=chip_groups
        )

    def sum_chips(value, axis):
        return lax.psum_scatter(
            value, "seq", scatter_dimension=axis, tiled=True, axis_index_groups=chip_groups
        )

    def send_halves(mine, axis):
        size = mine.shape[axis] // CORES
        same = lax.dynamic_slice_in_dim(mine, batch * size, size, axis)
        other = lax.dynamic_slice_in_dim(mine, (1 - batch) * size, size, axis)
        return unspread(same, other)

    def add(halves):
        return halves[0].astype(F32) + halves[1].astype(F32)

    def send_parts(own):
        return [to_part(own, d) for d in range(1, group)]

    def gather_ranks(own, arrived):
        found = []
        for d, here in enumerate([own, *arrived]):
            found.append((core * group + (part ^ d), here))
            found.append(((1 - core) * group + (part ^ d), to_core(here)))
        return found

    def reduce_part(partial, d):
        away = to_core(partial((1 - core) * group + (part ^ d)).astype(BF))
        return partial(core * group + (part ^ d)) + away.astype(F32)

    def reduce_away(partial):
        return [reduce_part(partial, d).astype(BF) for d in range(1, group)]

    def reduce_send(totals):
        return [to_part(total, d + 1) for d, total in enumerate(totals)]

    def reduce_end(own, arrived):
        return sum((got.astype(F32) for got in arrived), own)

    def sum_ranks(value):
        for d in [1 << i for i in range(group.bit_length() - 1)]:
            value = value + to_part(value, d)
        return value + to_core(value)

    def row_piece(value, r):
        return lax.dynamic_slice_in_dim(value, r * piece, piece, 0)

    def column_piece(value, r):
        return lax.dynamic_slice_in_dim(value, r * piece, piece, 1)

    def chip_tokens(value):
        own = lax.dynamic_index_in_dim(value, batch, 0, False)
        return place([own, to_core(own)], [core * block, (1 - core) * block], 0)

    tokens_c = chip_tokens(tokens)
    grad_out = chip_tokens(cotangent)

    def half(value, k):
        return lax.dynamic_slice_in_dim(value, k * block, block, 0)

    qk_width, v_width = heads * QK, heads * HEAD_V
    qkv_owns = spread(jnp.concatenate([w_query, w_key, w_value], 1))
    gains = lax.all_gather(jnp.stack([gain_mixer, gain_mlp]), "seq", axis=1, tiled=True)
    w_gate, gains, *qkv_owns = tie(w_gate.T, gains, *qkv_owns)
    gains = gains.astype(F32)
    mixer_gain, mlp_gain = gains[0], gains[1]
    gate_owns = spread(w_gate)
    qkv_full = place_chips(all_hops(qkv_owns), 0)

    bounds = jnp.cumsum(lax.dynamic_index_in_dim(lengths, batch, 0, False))

    def segment_of(p):
        return jnp.sum((p[..., None] >= bounds).astype(jnp.int32), axis=-1)

    start = chip * rows
    base = start + block * jnp.arange(CORES + 1, dtype=jnp.int32)
    edges = jnp.where(base == 0, -1, segment_of(base - 1))
    keep = (edges[1:] == edges[:-1]).astype(F32)
    base = base[:-1]
    ends = jnp.concatenate([jnp.zeros((1,), jnp.int32), bounds])
    open_end = jnp.where((edges[:-1] < 0) | (edges[:-1] > 2), 0, ends[edges[:-1] + 1] - base)
    tail_start = jnp.where(edges[1:] > 2, block, ends[edges[1:]] - base)
    marks = jnp.concatenate(
        [bounds[None, :] - base[:, None], open_end[:, None], tail_start[:, None]], 1
    ).astype(jnp.int32)

    tokens_f = tokens_c.astype(F32)
    inv_one = lax.rsqrt(jnp.mean(tokens_f * tokens_f, axis=-1, keepdims=True) + EPS)
    normed = (tokens_f * inv_one * mixer_gain).astype(BF)
    qkv = dot(normed, qkv_full).astype(BF)

    query, keys = qkv[:, :qk_width], qkv[:, qk_width : 2 * qk_width]
    values = qkv[:, 2 * qk_width :]
    local_states, mixer, grad_states, mixer_back = mixer_calls(heads, block, CORES)

    def pack(state, total):
        total = jnp.pad(total, ((0, 0), (0, -NFEAT % HEAD_V))).reshape(-1, HEAD_V)
        return jnp.concatenate([state.reshape(-1, HEAD_V), total], 0).astype(BF)

    def unpack(flat):
        flat = flat.astype(F32)
        cut = heads * NFEAT
        return (
            flat[:cut].reshape(heads, NFEAT, HEAD_V),
            flat[cut:].reshape(heads, -1)[:, :NFEAT],
        )

    def scan_blocks(both, blocks_order, step, meanwhile):
        state, total = both[..., :HEAD_V], both[..., HEAD_V]
        at_end = (state[blocks_order[0]], total[blocks_order[0]])
        for i in blocks_order[1:]:
            carry_keep = keep[i]
            at_end = (
                state[i] + carry_keep * at_end[0],
                total[i] + carry_keep * at_end[1],
            )
        message = pack(*at_end)
        run = None
        arrived = [shift_chip(message, step * d) for d in range(1, chips)]
        *arrived, state, total, meanwhile = tie(*arrived, state, total, meanwhile)
        for d in range(1, chips):
            got = unpack(arrived[d - 1])
            other = chip - step * d
            if step > 0:
                same = edges[0] == segment_of((other + 1) * rows - 1)
            else:
                same = edges[CORES] == segment_of(other * rows - 1)
            weight = (same & (other >= 0) & (other < chips)).astype(F32)
            term = (weight * got[0], weight * got[1])
            run = term if run is None else (run[0] + term[0], run[1] + term[1])
        found = {}
        for i in blocks_order:
            found[i] = run
            run = (state[i] + keep[i] * run[0], total[i] + keep[i] * run[1])
        state, total = (jnp.stack([found[i][j] for i in range(CORES)]) for j in range(2))
        total = jnp.broadcast_to(total[..., None], state.shape)
        both = jnp.concatenate([state, total], -1).astype(BF)
        both = jnp.pad(both, ((0, 0), (0, 0), (0, LANES - NFEAT), (0, 0)))
        return both, meanwhile

    (local,) = local_states(marks, keys, values)
    states, gate_owns = scan_blocks(local, list(range(CORES)), 1, gate_owns)
    w_output, gate_owns = tie(w_output, gate_owns)
    output_owns = spread(w_output)
    gate_full = gather_chips_bulk(gate_owns, 1)
    w_up, states = tie(w_up.T, states)
    up_owns = spread(w_up)
    mixer_own, denom = mixer(marks, query, keys, values, states)
    mixer_own, output_owns, up_owns = tie(mixer_own, output_owns, up_owns)

    arrived = send_parts(mixer_own)
    up_full = gather_chips_bulk(up_owns, 1)
    output_full = place_chips(all_hops(output_owns), 0)
    w_down, mixer_own = tie(w_down, mixer_own)
    down_owns = spread(w_down)
    mixer_parts = gather_ranks(mixer_own, arrived)
    branch_own = sum(dot(got, row_piece(output_full, r)) for r, got in mixer_parts).astype(BF)
    branch_own, down_owns = tie(branch_own, down_owns)
    arrived = send_parts(branch_own)
    downs = straight(down_owns)
    *arrived, gate_full = tie(*arrived, gate_full)
    branch_parts = gather_ranks(branch_own, arrived)
    branch = place([got for _, got in branch_parts], [r * piece for r, _ in branch_parts], 1)
    hidden_state = tokens_f + branch.astype(F32)
    inv_two = lax.rsqrt(jnp.mean(hidden_state * hidden_state, axis=-1, keepdims=True) + EPS)
    normed_two = (hidden_state * inv_two * mlp_gain).astype(BF)

    gate = dot(normed_two, gate_full, 1, 1).astype(BF)
    upward = dot(normed_two, up_full, 1, 1).astype(BF)
    downs, gate, upward = tie(downs, gate, upward)
    down_full = place_chips(downs, 1)
    gate, upward = gate.astype(F32), upward.astype(F32)
    grad_hidden = dot(grad_out, down_full, 1, 1).astype(BF).astype(F32)
    logistic = jax.nn.sigmoid(gate)
    activated = gate * logistic
    hidden = (activated * upward).astype(BF)
    grad_gate_f = grad_hidden * upward * logistic * (1.0 + gate * (1.0 - logistic))
    grad_up_f = grad_hidden * activated
    grad_gate_b, grad_up_b = grad_gate_f.astype(BF), grad_up_f.astype(BF)
    inner_two = sum_ranks(jnp.sum(grad_gate_f * gate + grad_up_f * upward, axis=1)) / width
    def hidden_part(grads, r):
        return dot(grads[0], column_piece(gate_full, r)) + dot(grads[1], column_piece(up_full, r))

    grads = (grad_gate_b, grad_up_b)
    totals = reduce_away(functools.partial(hidden_part, grads))
    inner_two, totals, grads = tie(inner_two, totals, grads)
    arrived = reduce_send(totals)
    own = reduce_part(functools.partial(hidden_part, grads), 0)
    up_sum = sum_chips(dot(grads[1], normed_two, 0, 0).astype(BF), 1)
    gate_sum = dot(grads[0], normed_two, 0, 0).astype(BF)
    own, gate_sum, arrived = tie(own, gate_sum, arrived)
    normed_grad = reduce_end(own, arrived)
    gate_sum = sum_chips(gate_sum, 1)
    tokens_own = column_piece(tokens_c, rank).astype(F32)
    hidden_own = tokens_own + branch_own.astype(F32)
    scaled_two = hidden_own * inv_two
    mlp_gain_own = lax.dynamic_slice_in_dim(mlp_gain, rank * piece, piece, 0)
    hidden_grad = column_piece(grad_out, rank).astype(F32) + inv_two * (
        normed_grad * mlp_gain_own - scaled_two * inner_two[:, None]
    )
    grad_gain_mlp = jnp.sum(normed_grad * scaled_two, axis=0)
    branch_grad = hidden_grad.astype(BF)

    def output_part(grad, r):
        return dot(grad, row_piece(output_full, r), 1, 1)

    totals = reduce_away(functools.partial(output_part, branch_grad))
    totals, branch_grad, hidden, up_sum = tie(totals, branch_grad, hidden, up_sum)
    arrived = reduce_send(totals)
    own = reduce_part(functools.partial(output_part, branch_grad), 0)

    def down_part(r):
        return dot(hidden, column_piece(down_full, r))

    mlp_totals, mlp_own = reduce_away(down_part), reduce_part(down_part, 0)
    down_sum = dot(hidden, grad_out, 0, 0).astype(BF)
    up_sum, down_sum = tie(up_sum, down_sum)
    up_halves = send_halves(up_sum, 1)
    arrived, own, mlp_own, mlp_totals, down_sum, gate_sum = tie(
        arrived, own, mlp_own, mlp_totals, down_sum, gate_sum
    )
    mixer_grad = reduce_end(own, arrived)
    mlp_arrived = reduce_send(mlp_totals)
    down_sum = sum_chips(down_sum, 1)
    gate_halves = send_halves(gate_sum, 1)
    (grad_local,) = grad_states(marks, query, mixer_grad, mixer_own, denom)
    grad_local, branch_grad = tie(grad_local, branch_grad)
    output_sum = place(
        [dot(got, branch_grad, 0, 0).astype(BF) for _, got in mixer_parts],
        [r * piece for r, _ in mixer_parts],
        0,
    )
    carried, (up_halves, output_sum) = scan_blocks(
        grad_local, list(range(CORES))[::-1], -1, (up_halves, output_sum)
    )
    carried, mlp_arrived, down_sum, output_sum = tie(
        carried, mlp_arrived, down_sum, output_sum
    )
    output_sum = sum_chips(output_sum, 0)
    grad_qkv = jnp.concatenate(
        mixer_back(
            marks, query, keys, values, mixer_grad, mixer_own, denom, states, carried
        ),
        1,
    )
    inner_one = jnp.sum(grad_qkv.astype(F32) * qkv.astype(F32), axis=1)
    inner_one = sum_ranks(inner_one) / width

    def input_part(grad, r):
        return dot(grad, row_piece(qkv_full, r), 1, 1)

    totals = reduce_away(functools.partial(input_part, grad_qkv))
    totals, grad_qkv, inner_one, gate_halves = tie(totals, grad_qkv, inner_one, gate_halves)
    arrived = reduce_send(totals)
    mixed_own = (hidden_own + reduce_end(mlp_own, mlp_arrived)).astype(BF)
    mixed_halves = unspread(half(mixed_own, batch), half(mixed_own, 1 - batch))
    down_halves = send_halves(down_sum, 1)
    own = reduce_part(functools.partial(input_part, grad_qkv), 0)
    qkv_sum = dot(normed, grad_qkv, 0, 0).astype(BF)
    arrived, own, mixed_halves, down_halves, qkv_sum, output_sum = tie(
        arrived, own, mixed_halves, down_halves, qkv_sum, output_sum
    )
    input_normed = reduce_end(own, arrived)
    qkv_sum = sum_chips(qkv_sum, 0)
    mixed = ordered(mixed_halves[0][None], mixed_halves[1][None], core, 0)
    scaled_one = tokens_own * inv_one
    mixer_gain_own = lax.dynamic_slice_in_dim(mixer_gain, rank * piece, piece, 0)
    grad_gain_mixer = jnp.sum(input_normed * scaled_one, axis=0)
    input_own = (
        hidden_grad
        + inv_one * (input_normed * mixer_gain_own - scaled_one * inner_one[:, None])
    ).astype(BF)

    gain_grads = lax.dynamic_update_slice_in_dim(
        jnp.zeros((2, width), F32), jnp.stack([grad_gain_mixer, grad_gain_mlp]), rank * piece, 1
    )
    planes = [
        move(gain_grads, lambda c, k, m, l: (c, k, *divmod((m * group + l) ^ d, group)))
        for d in range(1, feat_count)
    ]
    other_half = to_core(half(input_own, 1 - core))
    input_own, other_half, *planes = tie(input_own, other_half, *planes)
    input_pair = jnp.stack([half(input_own, core), other_half])

    def step_plane(value, step, first):
        def target(c, k, m, l):
            here = m * group + l
            behind = here if step > 0 else feat_count - 1 - here
            if behind < first or behind == feat_count - 1:
                return None
            return (c, k, *divmod(here + step, group))

        return move(value, target)

    gain_grads = sum(planes, gain_grads)
    output_halves = send_halves(output_sum, 0)
    hops = [to_core] + [
        functools.partial(to_chip, mask=1 << i) for i in range(chips.bit_length() - 1)
    ]
    ups, downs = [input_pair], [input_pair]
    for d in range(feat_count - 1):
        up, down = step_plane(ups[-1], 1, d), step_plane(downs[-1], -1, d)
        if hops:
            up, down, gain_grads, got = tie(up, down, gain_grads, hops[0](gain_grads))
            gain_grads, hops = gain_grads + got, hops[1:]
        if d == 0:
            up, down, qkv_sum = tie(up, down, qkv_sum)
            qkv_halves = send_halves(qkv_sum, 0)
        ups.append(up), downs.append(down)
    for hop in hops:
        gain_grads = gain_grads + hop(gain_grads)
    input_grad = widen(ups + downs[1:], feat_rank, core, micro, group, width)

    shard = width // seq_count
    gain_grads = lax.dynamic_slice_in_dim(gain_grads, seq_rank * shard, shard, 1)

    grad_qkv_w = add(qkv_halves)
    return (
        mixed,
        input_grad,
        grad_qkv_w[:, :qk_width],
        grad_qkv_w[:, qk_width : 2 * qk_width],
        grad_qkv_w[:, 2 * qk_width :],
        add(output_halves),
        add(gate_halves).T,
        add(up_halves).T,
        add(down_halves),
        gain_grads[0],
        gain_grads[1],
    )


def solution(mesh):
    in_specs = (
        P(None, "seq", None),
        P(None, "seq", None),
        P(),
        P("seq", "feat"),
        P("seq", "feat"),
        P("seq", "feat"),
        P("seq", "feat"),
        P("seq", "feat"),
        P("seq", "feat"),
        P("feat", "seq"),
        P("seq"),
        P("seq"),
    )
    out_specs = (
        P(None, "seq", "feat"),
        P(None, "seq", None),
        P("seq", "feat"),
        P("seq", "feat"),
        P("seq", "feat"),
        P("seq", "feat"),
        P("seq", "feat"),
        P("seq", "feat"),
        P("feat", "seq"),
        P("seq"),
        P("seq"),
    )
    return jax.shard_map(
        on_device, mesh=mesh, in_specs=in_specs, out_specs=out_specs, check_vma=False
    )
```

```python
import functools

import jax
import jax.numpy as jnp
import numpy as np
from jax import lax
from jax.experimental import pallas as pl
from jax.experimental.pallas import tpu as pltpu
from jax.sharding import PartitionSpec as P

HEADS = 16
HEAD_V = 128
QK = 16
NFEAT = 160
CORES = 2
EPS = 1e-05
BF = jnp.bfloat16
F32 = jnp.float32


LANES = 256
TILE = 256


def feature_tables(heads):
    left, right, scale = [-1], [-1], [1.0]
    for i in range(QK):
        left.append(i), right.append(-1), scale.append(1.0)
    for i in range(QK):
        for j in range(i, QK):
            left.append(i), right.append(j), scale.append(1.0 if i < j else 0.7071067811865476)
    padding = LANES - len(left)
    left, right, scale = left + [-2] * padding, right + [-2] * padding, scale + [0.0] * padding
    both = np.array(left + right)
    pick = np.zeros((heads * QK, heads, 2 * LANES), np.float32)
    for h in range(heads):
        pick[h * QK : (h + 1) * QK, h] = 0.5 * (np.arange(QK)[:, None] == both[None, :])
    ones = (both == -1).astype(np.float32)[None]
    own = np.zeros((8, heads * QK), np.float32)
    for h in range(heads):
        own[h, h * QK : (h + 1) * QK] = 0.25
    return (
        jnp.asarray(pick.reshape(heads * QK, -1), BF),
        jnp.asarray(ones),
        jnp.asarray(np.array(scale, np.float32)[None]),
        jnp.asarray(own, BF),
    )


def nt(a, b):
    return lax.dot_general(a, b, (((1,), (1,)), ((), ())), preferred_element_type=F32)


def tn(a, b):
    return lax.dot_general(a, b, (((0,), (0,)), ((), ())), preferred_element_type=F32)


def nn(a, b):
    return lax.dot_general(a, b, (((1,), (0,)), ((), ())), preferred_element_type=F32)


class Marks:
    def __init__(self, marks, b, block):
        t = lax.broadcasted_iota(jnp.int32, (block, 1), 0)
        first, second, third = marks[b, 0], marks[b, 1], marks[b, 2]
        low = jnp.where(t >= first, first, 0)
        low = jnp.where(t >= second, second, low)
        self.low = jnp.where(t >= third, block, low)
        self.padding = jnp.where(t >= third, 1.0, 0.0).astype(F32)
        self.use = jnp.where(t < marks[b, 3], 1.0, 0.0).astype(F32)
        self.tail = jnp.where(t >= marks[b, 4], 1.0, 0.0).astype(F32)

    def mask(self, at, count):
        t = lax.broadcasted_iota(jnp.int32, (TILE, count), 0) + at
        s = lax.broadcasted_iota(jnp.int32, (TILE, count), 1)
        return (s <= t) & (s >= self.low[at : at + TILE])


def sides(x, pick, ones, h):
    both = nn(x, pick[:, 2 * LANES * h : 2 * LANES * (h + 1)]) + ones
    return both[:, :LANES], both[:, LANES:]


def head_cols(ref, h):
    return ref[:, HEAD_V * h : HEAD_V * (h + 1)]


def output_grads(do_ref, o_ref, den_ref, h):
    do, o, den = head_cols(do_ref, h), head_cols(o_ref, h).astype(F32), head_cols(den_ref, h)
    do = do.astype(F32)
    inverse = 1.0 / den
    dnum = (do * inverse).astype(BF)
    dden = -jnp.sum(do * o, axis=1, keepdims=True) * inverse
    return dnum, dden


def state_kernel(marks, k_ref, v_ref, pick, ones, scale, out_ref, *, heads, block):
    m = Marks(marks, pl.program_id(0), block)
    k = k_ref[...]
    for h in range(heads):
        left, right = sides(k, pick, ones[...], h)
        feat = (left * right * (scale[...] * m.tail)).astype(BF)
        v = head_cols(v_ref, h)
        out_ref[0, h] = tn(feat, jnp.concatenate([v, jnp.ones_like(v)], 1))[:NFEAT]


def grad_state_kernel(
    marks, q_ref, do_ref, o_ref, den_ref, pick, ones, scale, out_ref, *, heads, block
):
    m = Marks(marks, pl.program_id(0), block)
    q = q_ref[...]
    for h in range(heads):
        left, right = sides(q, pick, ones[...], h)
        feat = (left * right * (scale[...] * m.use)).astype(BF)
        dnum, dden = output_grads(do_ref, o_ref, den_ref, h)
        out_ref[0, h] = tn(feat, jnp.concatenate([dnum, dden.astype(BF)], 1))[:NFEAT]


def mixer_kernel(
    marks, q_ref, k_ref, v_ref, s_ref, pick, ones, scale, own, o_ref, den_ref, *, heads, block
):
    m = Marks(marks, pl.program_id(0), block)
    q, k = q_ref[...], k_ref[...]
    for h in range(heads):
        q_own = q * own[h : h + 1, :]
        left, right = sides(q, pick, ones[...], h)
        feat = (left * right * scale[...]).astype(BF)
        before = nn(feat, s_ref[0, h]) * m.use
        v = head_cols(v_ref, h)
        v_one = jnp.concatenate([v, jnp.ones_like(v)], 1)
        for at in range(0, block, TILE):
            count = at + TILE
            prod = nt(q_own[at:count], k[:count])
            score = 1.0 + prod + 0.5 * prod * prod
            score = jnp.where(m.mask(at, count), score, 0.0).astype(BF)
            both = nn(score, v_one[:count]) + before[at:count]
            den = both[:, HEAD_V:] + m.padding[at:count]
            here = (slice(at, count), slice(HEAD_V * h, HEAD_V * (h + 1)))
            o_ref[here] = (both[:, :HEAD_V] / den).astype(BF)
            den_ref[here] = den


def mixer_back_kernel(
    marks,
    q_ref,
    k_ref,
    v_ref,
    do_ref,
    o_ref,
    den_ref,
    s_ref,
    g_ref,
    pick,
    ones,
    scale,
    own,
    dq_ref,
    dk_ref,
    dv_ref,
    dq,
    dk,
    dv,
    *,
    heads,
    block,
):
    m = Marks(marks, pl.program_id(0), block)
    q, k = q_ref[...], k_ref[...]
    first_lane = lax.broadcasted_iota(jnp.int32, (block, HEAD_V), 1) == 0
    dq[...] = jnp.zeros_like(dq)
    dk[...] = jnp.zeros_like(dk)
    for h in range(heads):
        table = pick[:, 2 * LANES * h : 2 * LANES * (h + 1)]
        q_own, k_own = q * own[h : h + 1, :], k * own[h : h + 1, :]
        v = head_cols(v_ref, h)
        dnum, dden = output_grads(do_ref, o_ref, den_ref, h)
        state, carried = s_ref[0, h], g_ref[0, h]

        left, right = sides(q, pick, ones[...], h)
        wide = jnp.concatenate([dnum, jnp.where(first_lane, dden, 0.0).astype(BF)], 1)
        dfeat = nt(wide, state) * (scale[...] * m.use)
        pulled = jnp.concatenate([(dfeat * right).astype(BF), (dfeat * left).astype(BF)], 1)
        dq[...] += nt(pulled, table)

        left, right = sides(k, pick, ones[...], h)
        wide = jnp.concatenate([v, jnp.where(first_lane, 1.0, 0.0).astype(BF)], 1)
        dfeat = nt(wide, carried) * (scale[...] * m.tail)
        pulled = jnp.concatenate([(dfeat * right).astype(BF), (dfeat * left).astype(BF)], 1)
        dk[...] += nt(pulled, table)
        feat = (left * right * (scale[...] * m.tail)).astype(BF)
        dv[...] = nn(feat, carried[:, :HEAD_V])

        for at in range(0, block, TILE):
            count = at + TILE
            prod = nt(q_own[at:count], k[:count])
            one = 1.0 + prod
            mask = m.mask(at, count)
            score = jnp.where(mask, one + 0.5 * prod * prod, 0.0).astype(BF)
            dscore = nt(dnum[at:count], v[:count]) + dden[at:count, :1]
            dprod = jnp.where(mask, dscore * one, 0.0).astype(BF)
            dq[at:count] += nn(dprod, k_own[:count])
            dk[:count] += tn(dprod, q_own[at:count])
            dv[:count] += tn(score, dnum[at:count])
        dv_ref[:, HEAD_V * h : HEAD_V * (h + 1)] = dv[...].astype(BF)
    dq_ref[...] = dq[...].astype(BF)
    dk_ref[...] = dk[...].astype(BF)


def mixer_calls(heads, block, blocks):
    tables = feature_tables(heads)
    narrow = pl.BlockSpec((block, heads * QK), lambda b, marks: (b, 0))
    wide = pl.BlockSpec((block, heads * HEAD_V), lambda b, marks: (b, 0))
    local = pl.BlockSpec((1, heads, NFEAT, 2 * HEAD_V), lambda b, marks: (b, 0, 0, 0))
    state = pl.BlockSpec((1, heads, LANES, 2 * HEAD_V), lambda b, marks: (b, 0, 0, 0))
    fixed = [pl.BlockSpec(t.shape, lambda b, marks: (0, 0)) for t in tables]
    rows = block * blocks

    def call(kernel, specs, used, outs, scratch, cost):
        def run(marks, *args):
            return pl.pallas_call(
                functools.partial(kernel, heads=heads, block=block),
                grid_spec=pltpu.PrefetchScalarGridSpec(
                    num_scalar_prefetch=1,
                    grid=(blocks,),
                    in_specs=specs + fixed[:used],
                    out_specs=[o[0] for o in outs],
                    scratch_shapes=scratch,
                ),
                out_shape=[jax.ShapeDtypeStruct(*o[1:]) for o in outs],
                cost_estimate=pl.CostEstimate(
                    flops=cost * rows * heads, bytes_accessed=rows * heads * 1500, transcendentals=0
                ),
                compiler_params=pltpu.CompilerParams(vmem_limit_bytes=48 * 2**20),
            )(marks, *args, *tables[:used])

        return run

    local_out = (local, (blocks, heads, NFEAT, 2 * HEAD_V), F32)
    wide_b, wide_f = (wide, (rows, heads * HEAD_V), BF), (wide, (rows, heads * HEAD_V), F32)
    narrow_b = (narrow, (rows, heads * QK), BF)
    scratch = [
        pltpu.VMEM((block, heads * QK), F32),
        pltpu.VMEM((block, heads * QK), F32),
        pltpu.VMEM((block, HEAD_V), F32),
    ]
    return (
        call(state_kernel, [narrow, wide], 3, [local_out], [], 500000),
        call(mixer_kernel, [narrow, narrow, wide, state], 4, [wide_b, wide_f], [], 1000000),
        call(grad_state_kernel, [narrow, wide, wide, wide], 3, [local_out], [], 500000),
        call(
            mixer_back_kernel,
            [narrow, narrow, wide, wide, wide, wide, state, state],
            4,
            [narrow_b, narrow_b, wide_b],
            scratch,
            2500000,
        ),
    )


def dot(a, b, ca=1, cb=0):
    return lax.dot_general(a, b, (((ca,), (cb,)), ((), ())), preferred_element_type=F32)


def tie(*values):
    return lax.optimization_barrier(values)


def place_kernel(offsets, *refs, axis):
    *pieces, out, sems = refs
    copies = []
    for i, piece in enumerate(pieces):
        size = piece.shape[axis]
        span = pl.ds(pl.multiple_of(offsets[i], size), size)
        target = out.at[span] if axis == 0 else out.at[:, span]
        copies.append(pltpu.make_async_copy(piece, target, sems.at[i]))
    for copy in copies:
        copy.start()
    for copy in copies:
        copy.wait()


def place(pieces, offsets, axis):
    shape = list(pieces[0].shape)
    shape[axis] = sum(p.shape[axis] for p in pieces)
    size = int(np.prod(shape)) * pieces[0].dtype.itemsize
    return pl.pallas_call(
        functools.partial(place_kernel, axis=axis),
        grid_spec=pltpu.PrefetchScalarGridSpec(
            num_scalar_prefetch=1,
            grid=(),
            in_specs=[pl.BlockSpec(memory_space=pltpu.VMEM)] * len(pieces),
            out_specs=pl.BlockSpec(memory_space=pl.ANY),
            scratch_shapes=[pltpu.SemaphoreType.DMA((len(pieces),))],
        ),
        compiler_params=pltpu.CompilerParams(vmem_limit_bytes=32 * 2**20),
        out_shape=jax.ShapeDtypeStruct(tuple(shape), pieces[0].dtype),
        cost_estimate=pl.CostEstimate(flops=0, bytes_accessed=2 * size, transcendentals=0),
    )(jnp.stack(offsets).astype(jnp.int32), *pieces)


def widen_kernel(where, *refs, group):
    *shares, out = refs
    count, core = (len(shares) + 1) // 2, where[1]
    piece = shares[0].shape[2]
    for d in range(count):
        plane = lax.rem(where[0] + count - d, count)
        batch, part = plane // group, lax.rem(plane, group)
        for j in range(CORES):
            got = shares[d][j].astype(F32)
            if d:
                got = got + shares[2 * count - 1 - d][j].astype(F32)
            k = core if j == 0 else 1 - core
            at = pl.multiple_of((k * group + part) * piece, piece)
            out[batch, :, pl.ds(at, piece)] = got


def widen(shares, feat_rank, core, micro, group, width):
    _, block, piece = shares[0].shape
    tile = 128
    return pl.pallas_call(
        functools.partial(widen_kernel, group=group),
        grid_spec=pltpu.PrefetchScalarGridSpec(
            num_scalar_prefetch=1,
            grid=(block // tile,),
            in_specs=[pl.BlockSpec((CORES, tile, piece), lambda i, w: (0, i, 0))] * len(shares),
            out_specs=pl.BlockSpec((micro, tile, width), lambda i, w: (0, i, 0)),
        ),
        out_shape=jax.ShapeDtypeStruct((micro, block, width), F32),
        compiler_params=pltpu.CompilerParams(vmem_limit_bytes=48 * 2**20),
    )(jnp.stack([feat_rank, core]).astype(jnp.int32), *shares)


def on_device(
    tokens,
    cotangent,
    lengths,
    w_query,
    w_key,
    w_value,
    w_output,
    w_gate,
    w_up,
    w_down,
    gain_mixer,
    gain_mlp,
):
    micro, block, width = tokens.shape
    seq_count, feat_count = lax.axis_size("seq"), lax.axis_size("feat")
    seq_rank, feat_rank = lax.axis_index("seq"), lax.axis_index("feat")
    group = feat_count // micro
    ranks = CORES * group
    chips = seq_count // CORES
    chip, core = seq_rank // CORES, seq_rank % CORES
    batch, part = feat_rank // group, feat_rank % group
    rank = core * group + part
    rows = CORES * block
    piece = width // ranks
    heads = HEADS // ranks

    def move(value, target):
        pairs = []
        for s in range(seq_count):
            for f in range(feat_count):
                here = (s // CORES, s % CORES, f // group, f % group)
                there = target(*here)
                if there is not None and there != here:
                    c2, k2, m2, l2 = there
                    pairs.append(
                        (s * feat_count + f, (c2 * CORES + k2) * feat_count + m2 * group + l2)
                    )
        return lax.ppermute(value, ("seq", "feat"), pairs)

    def to_core(value):
        return move(value, lambda c, k, m, l: (c, 1 - k, m, l))

    def to_part(value, d):
        return move(value, lambda c, k, m, l: (c, k, m, l ^ d))

    def to_chip(value, mask):
        return move(value, lambda c, k, m, l: (c ^ mask, k, m, l))

    def shift_chip(value, d):
        return move(value, lambda c, k, m, l: (c + d, k, m, l) if 0 <= c + d < chips else None)

    def spread(value):
        moved = move(value, lambda c, k, m, l: (c, m, k, l))
        other = move(value, lambda c, k, m, l: (c, m, 1 - k, l))
        return jnp.where(core == batch, value, moved), other

    def unspread(same, other):
        moved = move(same, lambda c, k, m, l: (c, m, k, l))
        other = move(other, lambda c, k, m, l: (c, 1 - m, k, l))
        return jnp.where(core == batch, same, moved), other

    def ordered(first_if_zero, second_if_zero, bit, axis):
        return jnp.where(
            bit == 0,
            jnp.concatenate([first_if_zero, second_if_zero], axis),
            jnp.concatenate([second_if_zero, first_if_zero], axis),
        )

    chip_groups = [[c * CORES + k for c in range(chips)] for k in range(CORES)]

    bits = [1 << i for i in range(chips.bit_length() - 1)]
    orders = (bits, bits[::-1])

    def all_hops(owns):
        helds = [{0: own} for own in owns]
        for held, order in zip(helds, orders):
            for bit in order:
                for mask in list(held):
                    held[mask | bit] = to_chip(held[mask], bit)
        return helds

    def straight(owns):
        return [
            {mask: to_chip(own, mask) if mask else own for mask in range(chips)} for own in owns
        ]

    def place_chips(helds, axis):
        size = helds[0][0].shape[axis]
        pieces, offsets = [], []
        for held, k in zip(helds, (batch, 1 - batch)):
            for mask, got in held.items():
                pieces.append(got)
                offsets.append(((chip ^ mask) * CORES + k) * size)
        return place(pieces, offsets, axis)

    def gather_chips_bulk(owns, axis):
        size = owns[0].shape[axis]
        both = place(list(owns), [batch * size, (1 - batch) * size], axis)
        return lax.all_gather(
            both, "seq", axis=axis, tiled=True, axis_index_groups=chip_groups
        )

    def sum_chips(value, axis):
        return lax.psum_scatter(
            value, "seq", scatter_dimension=axis, tiled=True, axis_index_groups=chip_groups
        )

    def send_halves(mine, axis):
        size = mine.shape[axis] // CORES
        same = lax.dynamic_slice_in_dim(mine, batch * size, size, axis)
        other = lax.dynamic_slice_in_dim(mine, (1 - batch) * size, size, axis)
        return unspread(same, other)

    def add(halves):
        return halves[0].astype(F32) + halves[1].astype(F32)

    def send_parts(own):
        return [to_part(own, d) for d in range(1, group)]

    def gather_ranks(own, arrived):
        found = []
        for d, here in enumerate([own, *arrived]):
            found.append((core * group + (part ^ d), here))
            found.append(((1 - core) * group + (part ^ d), to_core(here)))
        return found

    def reduce_part(partial, d):
        away = to_core(partial((1 - core) * group + (part ^ d)).astype(BF))
        return partial(core * group + (part ^ d)) + away.astype(F32)

    def reduce_away(partial):
        return [reduce_part(partial, d).astype(BF) for d in range(1, group)]

    def reduce_send(totals):
        return [to_part(total, d + 1) for d, total in enumerate(totals)]

    def reduce_end(own, arrived):
        return sum((got.astype(F32) for got in arrived), own)

    def sum_ranks(value):
        for d in [1 << i for i in range(group.bit_length() - 1)]:
            value = value + to_part(value, d)
        return value + to_core(value)

    def row_piece(value, r):
        return lax.dynamic_slice_in_dim(value, r * piece, piece, 0)

    def column_piece(value, r):
        return lax.dynamic_slice_in_dim(value, r * piece, piece, 1)

    def chip_tokens(value):
        own = lax.dynamic_index_in_dim(value, batch, 0, False)
        return place([own, to_core(own)], [core * block, (1 - core) * block], 0)

    tokens_c = chip_tokens(tokens)
    grad_out = chip_tokens(cotangent)

    def half(value, k):
        return lax.dynamic_slice_in_dim(value, k * block, block, 0)

    qk_width, v_width = heads * QK, heads * HEAD_V
    qkv_owns = spread(jnp.concatenate([w_query, w_key, w_value], 1))
    gains = lax.all_gather(jnp.stack([gain_mixer, gain_mlp]), "seq", axis=1, tiled=True)
    w_gate, gains, *qkv_owns = tie(w_gate.T, gains, *qkv_owns)
    gains = gains.astype(F32)
    mixer_gain, mlp_gain = gains[0], gains[1]
    gate_owns = spread(w_gate)
    qkv_full = place_chips(all_hops(qkv_owns), 0)

    bounds = jnp.cumsum(lax.dynamic_index_in_dim(lengths, batch, 0, False))

    def segment_of(p):
        return jnp.sum((p[..., None] >= bounds).astype(jnp.int32), axis=-1)

    start = chip * rows
    base = start + block * jnp.arange(CORES + 1, dtype=jnp.int32)
    edges = jnp.where(base == 0, -1, segment_of(base - 1))
    keep = (edges[1:] == edges[:-1]).astype(F32)
    base = base[:-1]
    ends = jnp.concatenate([jnp.zeros((1,), jnp.int32), bounds])
    open_end = jnp.where((edges[:-1] < 0) | (edges[:-1] > 2), 0, ends[edges[:-1] + 1] - base)
    tail_start = jnp.where(edges[1:] > 2, block, ends[edges[1:]] - base)
    marks = jnp.concatenate(
        [bounds[None, :] - base[:, None], open_end[:, None], tail_start[:, None]], 1
    ).astype(jnp.int32)

    tokens_f = tokens_c.astype(F32)
    inv_one = lax.rsqrt(jnp.mean(tokens_f * tokens_f, axis=-1, keepdims=True) + EPS)
    normed = (tokens_f * inv_one * mixer_gain).astype(BF)
    qkv = dot(normed, qkv_full).astype(BF)

    query, keys = qkv[:, :qk_width], qkv[:, qk_width : 2 * qk_width]
    values = qkv[:, 2 * qk_width :]
    local_states, mixer, grad_states, mixer_back = mixer_calls(heads, block, CORES)

    def pack(state, total):
        total = jnp.pad(total, ((0, 0), (0, -NFEAT % HEAD_V))).reshape(-1, HEAD_V)
        return jnp.concatenate([state.reshape(-1, HEAD_V), total], 0).astype(BF)

    def unpack(flat):
        flat = flat.astype(F32)
        cut = heads * NFEAT
        return (
            flat[:cut].reshape(heads, NFEAT, HEAD_V),
            flat[cut:].reshape(heads, -1)[:, :NFEAT],
        )

    def scan_blocks(both, blocks_order, step, meanwhile):
        state, total = both[..., :HEAD_V], both[..., HEAD_V]
        at_end = (state[blocks_order[0]], total[blocks_order[0]])
        for i in blocks_order[1:]:
            carry_keep = keep[i]
            at_end = (
                state[i] + carry_keep * at_end[0],
                total[i] + carry_keep * at_end[1],
            )
        message = pack(*at_end)
        run = None
        arrived = [shift_chip(message, step * d) for d in range(1, chips)]
        *arrived, state, total, meanwhile = tie(*arrived, state, total, meanwhile)
        for d in range(1, chips):
            got = unpack(arrived[d - 1])
            other = chip - step * d
            if step > 0:
                same = edges[0] == segment_of((other + 1) * rows - 1)
            else:
                same = edges[CORES] == segment_of(other * rows - 1)
            weight = (same & (other >= 0) & (other < chips)).astype(F32)
            term = (weight * got[0], weight * got[1])
            run = term if run is None else (run[0] + term[0], run[1] + term[1])
        found = {}
        for i in blocks_order:
            found[i] = run
            run = (state[i] + keep[i] * run[0], total[i] + keep[i] * run[1])
        state, total = (jnp.stack([found[i][j] for i in range(CORES)]) for j in range(2))
        total = jnp.broadcast_to(total[..., None], state.shape)
        both = jnp.concatenate([state, total], -1).astype(BF)
        both = jnp.pad(both, ((0, 0), (0, 0), (0, LANES - NFEAT), (0, 0)))
        return both, meanwhile

    (local,) = local_states(marks, keys, values)
    w_output, gate_owns, local = tie(w_output, gate_owns, local)
    output_owns = spread(w_output)
    states, output_owns = scan_blocks(local, list(range(CORES)), 1, output_owns)
    gate_full = gather_chips_bulk(gate_owns, 1)
    w_up, states = tie(w_up.T, states)
    up_owns = spread(w_up)
    mixer_own, denom = mixer(marks, query, keys, values, states)
    mixer_own, output_owns, up_owns = tie(mixer_own, output_owns, up_owns)

    arrived = send_parts(mixer_own)
    up_full = gather_chips_bulk(up_owns, 1)
    output_full = place_chips(all_hops(output_owns), 0)
    w_down, mixer_own = tie(w_down, mixer_own)
    down_owns = spread(w_down)
    mixer_parts = gather_ranks(mixer_own, arrived)
    branch_own = sum(dot(got, row_piece(output_full, r)) for r, got in mixer_parts).astype(BF)
    branch_own, down_owns = tie(branch_own, down_owns)
    arrived = send_parts(branch_own)
    downs = straight(down_owns)
    *arrived, gate_full = tie(*arrived, gate_full)
    branch_parts = gather_ranks(branch_own, arrived)
    branch = place([got for _, got in branch_parts], [r * piece for r, _ in branch_parts], 1)
    hidden_state = tokens_f + branch.astype(F32)
    inv_two = lax.rsqrt(jnp.mean(hidden_state * hidden_state, axis=-1, keepdims=True) + EPS)
    normed_two = (hidden_state * inv_two * mlp_gain).astype(BF)

    gate = dot(normed_two, gate_full, 1, 1).astype(BF)
    upward = dot(normed_two, up_full, 1, 1).astype(BF)
    hidden = jax.nn.silu(gate.astype(F32)) * upward.astype(F32)
    hidden = hidden.astype(BF)
    down_sum = dot(hidden, grad_out, 0, 0).astype(BF)
    downs, gate, upward, hidden, down_sum = tie(downs, gate, upward, hidden, down_sum)
    down_sum = sum_chips(down_sum, 1)
    down_full = place_chips(downs, 1)
    gate, upward = gate.astype(F32), upward.astype(F32)
    grad_hidden = dot(grad_out, down_full, 1, 1).astype(BF).astype(F32)
    logistic = jax.nn.sigmoid(gate)
    activated = gate * logistic
    grad_gate_f = grad_hidden * upward * logistic * (1.0 + gate * (1.0 - logistic))
    grad_up_f = grad_hidden * activated
    grad_gate_b, grad_up_b = grad_gate_f.astype(BF), grad_up_f.astype(BF)
    inner_two = sum_ranks(jnp.sum(grad_gate_f * gate + grad_up_f * upward, axis=1)) / width
    def hidden_part(grads, r):
        return dot(grads[0], column_piece(gate_full, r)) + dot(grads[1], column_piece(up_full, r))

    grads = (grad_gate_b, grad_up_b)
    totals = reduce_away(functools.partial(hidden_part, grads))
    inner_two, totals, grads = tie(inner_two, totals, grads)
    arrived = reduce_send(totals)
    own = reduce_part(functools.partial(hidden_part, grads), 0)
    up_sum = sum_chips(dot(grads[1], normed_two, 0, 0).astype(BF), 1)
    gate_sum = dot(grads[0], normed_two, 0, 0).astype(BF)
    own, gate_sum, arrived, down_sum = tie(own, gate_sum, arrived, down_sum)
    normed_grad = reduce_end(own, arrived)
    down_halves = send_halves(down_sum, 1)
    gate_sum = sum_chips(gate_sum, 1)
    tokens_own = column_piece(tokens_c, rank).astype(F32)
    hidden_own = tokens_own + branch_own.astype(F32)
    scaled_two = hidden_own * inv_two
    mlp_gain_own = lax.dynamic_slice_in_dim(mlp_gain, rank * piece, piece, 0)
    hidden_grad = column_piece(grad_out, rank).astype(F32) + inv_two * (
        normed_grad * mlp_gain_own - scaled_two * inner_two[:, None]
    )
    grad_gain_mlp = jnp.sum(normed_grad * scaled_two, axis=0)
    branch_grad = hidden_grad.astype(BF)

    def output_part(grad, r):
        return dot(grad, row_piece(output_full, r), 1, 1)

    totals = reduce_away(functools.partial(output_part, branch_grad))
    totals, branch_grad, hidden = tie(totals, branch_grad, hidden)
    arrived = reduce_send(totals)
    own = reduce_part(functools.partial(output_part, branch_grad), 0)

    def down_part(r):
        return dot(hidden, column_piece(down_full, r))

    mlp_totals, mlp_own = reduce_away(down_part), reduce_part(down_part, 0)
    arrived, own, mlp_own, mlp_totals, down_halves, up_sum = tie(
        arrived, own, mlp_own, mlp_totals, down_halves, up_sum
    )
    mixer_grad = reduce_end(own, arrived)
    mlp_arrived = reduce_send(mlp_totals)
    (grad_local,) = grad_states(marks, query, mixer_grad, mixer_own, denom)
    grad_local, branch_grad = tie(grad_local, branch_grad)
    output_sum = place(
        [dot(got, branch_grad, 0, 0).astype(BF) for _, got in mixer_parts],
        [r * piece for r, _ in mixer_parts],
        0,
    )
    carried, (mlp_arrived, output_sum) = scan_blocks(
        grad_local, list(range(CORES))[::-1], -1, (mlp_arrived, output_sum)
    )
    carried, output_sum, gate_sum, up_sum = tie(carried, output_sum, gate_sum, up_sum)
    up_halves = send_halves(up_sum, 1)
    output_sum = sum_chips(output_sum, 0)
    grad_qkv = mixer_back(
        marks, query, keys, values, mixer_grad, mixer_own, denom, states, carried
    )
    grad_qkv, up_halves, gate_sum = tie(grad_qkv, up_halves, gate_sum)
    gate_halves = send_halves(gate_sum, 1)
    grad_qkv = jnp.concatenate(grad_qkv, 1)
    inner_one = jnp.sum(grad_qkv.astype(F32) * qkv.astype(F32), axis=1)
    inner_one = sum_ranks(inner_one) / width

    def input_part(grad, r):
        return dot(grad, row_piece(qkv_full, r), 1, 1)

    totals = reduce_away(functools.partial(input_part, grad_qkv))
    totals, grad_qkv, inner_one, gate_halves = tie(totals, grad_qkv, inner_one, gate_halves)
    arrived = reduce_send(totals)
    mixed_own = (hidden_own + reduce_end(mlp_own, mlp_arrived)).astype(BF)
    mixed_halves = unspread(half(mixed_own, batch), half(mixed_own, 1 - batch))
    own = reduce_part(functools.partial(input_part, grad_qkv), 0)
    qkv_sum = dot(normed, grad_qkv, 0, 0).astype(BF)
    arrived, own, mixed_halves, qkv_sum, output_sum = tie(
        arrived, own, mixed_halves, qkv_sum, output_sum
    )
    input_normed = reduce_end(own, arrived)
    qkv_sum = sum_chips(qkv_sum, 0)
    mixed = ordered(mixed_halves[0][None], mixed_halves[1][None], core, 0)
    scaled_one = tokens_own * inv_one
    mixer_gain_own = lax.dynamic_slice_in_dim(mixer_gain, rank * piece, piece, 0)
    grad_gain_mixer = jnp.sum(input_normed * scaled_one, axis=0)
    input_own = (
        hidden_grad
        + inv_one * (input_normed * mixer_gain_own - scaled_one * inner_one[:, None])
    ).astype(BF)

    gain_grads = lax.dynamic_update_slice_in_dim(
        jnp.zeros((2, width), F32), jnp.stack([grad_gain_mixer, grad_gain_mlp]), rank * piece, 1
    )
    planes = [
        move(gain_grads, lambda c, k, m, l: (c, k, *divmod((m * group + l) ^ d, group)))
        for d in range(1, feat_count)
    ]
    other_half = to_core(half(input_own, 1 - core))
    input_own, other_half, *planes = tie(input_own, other_half, *planes)
    input_pair = jnp.stack([half(input_own, core), other_half])

    def step_plane(value, step, first):
        def target(c, k, m, l):
            here = m * group + l
            behind = here if step > 0 else feat_count - 1 - here
            if behind < first or behind == feat_count - 1:
                return None
            return (c, k, *divmod(here + step, group))

        return move(value, target)

    gain_grads = sum(planes, gain_grads)
    output_halves = send_halves(output_sum, 0)
    hops = [to_core] + [
        functools.partial(to_chip, mask=1 << i) for i in range(chips.bit_length() - 1)
    ]
    ups, downs = [input_pair], [input_pair]
    for d in range(feat_count - 1):
        up, down = step_plane(ups[-1], 1, d), step_plane(downs[-1], -1, d)
        if hops:
            up, down, gain_grads, got = tie(up, down, gain_grads, hops[0](gain_grads))
            gain_grads, hops = gain_grads + got, hops[1:]
        if d == 0:
            up, down, qkv_sum = tie(up, down, qkv_sum)
            qkv_halves = send_halves(qkv_sum, 0)
        ups.append(up), downs.append(down)
    for hop in hops:
        gain_grads = gain_grads + hop(gain_grads)
    input_grad = widen(ups + downs[1:], feat_rank, core, micro, group, width)

    shard = width // seq_count
    gain_grads = lax.dynamic_slice_in_dim(gain_grads, seq_rank * shard, shard, 1)

    grad_qkv_w = add(qkv_halves)
    return (
        mixed,
        input_grad,
        grad_qkv_w[:, :qk_width],
        grad_qkv_w[:, qk_width : 2 * qk_width],
        grad_qkv_w[:, 2 * qk_width :],
        add(output_halves),
        add(gate_halves).T,
        add(up_halves).T,
        add(down_halves),
        gain_grads[0],
        gain_grads[1],
    )


def solution(mesh):
    in_specs = (
        P(None, "seq", None),
        P(None, "seq", None),
        P(),
        P("seq", "feat"),
        P("seq", "feat"),
        P("seq", "feat"),
        P("seq", "feat"),
        P("seq", "feat"),
        P("seq", "feat"),
        P("feat", "seq"),
        P("seq"),
        P("seq"),
    )
    out_specs = (
        P(None, "seq", "feat"),
        P(None, "seq", None),
        P("seq", "feat"),
        P("seq", "feat"),
        P("seq", "feat"),
        P("seq", "feat"),
        P("seq", "feat"),
        P("seq", "feat"),
        P("feat", "seq"),
        P("seq"),
        P("seq"),
    )
    return jax.shard_map(
        on_device, mesh=mesh, in_specs=in_specs, out_specs=out_specs, check_vma=False
    )
```

```python
import functools

import jax
import jax.numpy as jnp
import numpy as np
from jax import lax
from jax.experimental import pallas as pl
from jax.experimental.pallas import tpu as pltpu
from jax.sharding import PartitionSpec as P

HEADS = 16
HEAD_V = 128
QK = 16
NFEAT = 160
CORES = 2
EPS = 1e-05
BF = jnp.bfloat16
F32 = jnp.float32


LANES = 256
TILE = 256


def feature_tables(heads):
    left, right, scale = [-1], [-1], [1.0]
    for i in range(QK):
        left.append(i), right.append(-1), scale.append(1.0)
    for i in range(QK):
        for j in range(i, QK):
            left.append(i), right.append(j), scale.append(1.0 if i < j else 0.7071067811865476)
    padding = LANES - len(left)
    left, right, scale = left + [-2] * padding, right + [-2] * padding, scale + [0.0] * padding
    both = np.array(left + right)
    pick = np.zeros((heads * QK, heads, 2 * LANES), np.float32)
    for h in range(heads):
        pick[h * QK : (h + 1) * QK, h] = 0.5 * (np.arange(QK)[:, None] == both[None, :])
    ones = (both == -1).astype(np.float32)[None]
    own = np.zeros((8, heads * QK), np.float32)
    for h in range(heads):
        own[h, h * QK : (h + 1) * QK] = 0.25
    return (
        jnp.asarray(pick.reshape(heads * QK, -1), BF),
        jnp.asarray(ones),
        jnp.asarray(np.array(scale, np.float32)[None]),
        jnp.asarray(own, BF),
    )


def nt(a, b):
    return lax.dot_general(a, b, (((1,), (1,)), ((), ())), preferred_element_type=F32)


def tn(a, b):
    return lax.dot_general(a, b, (((0,), (0,)), ((), ())), preferred_element_type=F32)


def nn(a, b):
    return lax.dot_general(a, b, (((1,), (0,)), ((), ())), preferred_element_type=F32)


class Marks:
    def __init__(self, marks, b, block):
        t = lax.broadcasted_iota(jnp.int32, (block, 1), 0)
        first, second, third = marks[b, 0], marks[b, 1], marks[b, 2]
        low = jnp.where(t >= first, first, 0)
        low = jnp.where(t >= second, second, low)
        self.low = jnp.where(t >= third, block, low)
        self.padding = jnp.where(t >= third, 1.0, 0.0).astype(F32)
        self.use = jnp.where(t < marks[b, 3], 1.0, 0.0).astype(F32)
        self.tail = jnp.where(t >= marks[b, 4], 1.0, 0.0).astype(F32)

    def mask(self, at, count):
        t = lax.broadcasted_iota(jnp.int32, (TILE, count), 0) + at
        s = lax.broadcasted_iota(jnp.int32, (TILE, count), 1)
        return (s <= t) & (s >= self.low[at : at + TILE])


def sides(x, pick, ones, h):
    both = nn(x, pick[:, 2 * LANES * h : 2 * LANES * (h + 1)]) + ones
    return both[:, :LANES], both[:, LANES:]


def head_cols(ref, h):
    return ref[:, HEAD_V * h : HEAD_V * (h + 1)]


def output_grads(do_ref, o_ref, den_ref, h):
    do, o, den = head_cols(do_ref, h), head_cols(o_ref, h).astype(F32), head_cols(den_ref, h)
    do = do.astype(F32)
    inverse = 1.0 / den
    dnum = (do * inverse).astype(BF)
    dden = -jnp.sum(do * o, axis=1, keepdims=True) * inverse
    return dnum, dden


def state_kernel(marks, k_ref, v_ref, pick, ones, scale, out_ref, *, heads, block):
    m = Marks(marks, pl.program_id(0), block)
    k = k_ref[...]
    for h in range(heads):
        left, right = sides(k, pick, ones[...], h)
        feat = (left * right * (scale[...] * m.tail)).astype(BF)
        v = head_cols(v_ref, h)
        out_ref[0, h] = tn(feat, jnp.concatenate([v, jnp.ones_like(v)], 1))[:NFEAT]


def grad_state_kernel(
    marks, q_ref, do_ref, o_ref, den_ref, pick, ones, scale, out_ref, *, heads, block
):
    m = Marks(marks, pl.program_id(0), block)
    q = q_ref[...]
    for h in range(heads):
        left, right = sides(q, pick, ones[...], h)
        feat = (left * right * (scale[...] * m.use)).astype(BF)
        dnum, dden = output_grads(do_ref, o_ref, den_ref, h)
        out_ref[0, h] = tn(feat, jnp.concatenate([dnum, dden.astype(BF)], 1))[:NFEAT]


def mixer_kernel(
    marks, q_ref, k_ref, v_ref, s_ref, pick, ones, scale, own, o_ref, den_ref, *, heads, block
):
    m = Marks(marks, pl.program_id(0), block)
    q, k = q_ref[...], k_ref[...]
    for h in range(heads):
        q_own = q * own[h : h + 1, :]
        left, right = sides(q, pick, ones[...], h)
        feat = (left * right * scale[...]).astype(BF)
        before = nn(feat, s_ref[0, h]) * m.use
        v = head_cols(v_ref, h)
        v_one = jnp.concatenate([v, jnp.ones_like(v)], 1)
        for at in range(0, block, TILE):
            count = at + TILE
            prod = nt(q_own[at:count], k[:count])
            score = 1.0 + prod + 0.5 * prod * prod
            score = jnp.where(m.mask(at, count), score, 0.0).astype(BF)
            both = nn(score, v_one[:count]) + before[at:count]
            den = both[:, HEAD_V:] + m.padding[at:count]
            here = (slice(at, count), slice(HEAD_V * h, HEAD_V * (h + 1)))
            o_ref[here] = (both[:, :HEAD_V] / den).astype(BF)
            den_ref[here] = den


def mixer_back_kernel(
    marks,
    q_ref,
    k_ref,
    v_ref,
    do_ref,
    o_ref,
    den_ref,
    s_ref,
    g_ref,
    pick,
    ones,
    scale,
    own,
    dq_ref,
    dk_ref,
    dv_ref,
    dq,
    dk,
    dv,
    *,
    heads,
    block,
):
    m = Marks(marks, pl.program_id(0), block)
    q, k = q_ref[...], k_ref[...]
    first_lane = lax.broadcasted_iota(jnp.int32, (block, HEAD_V), 1) == 0
    dq[...] = jnp.zeros_like(dq)
    dk[...] = jnp.zeros_like(dk)
    for h in range(heads):
        table = pick[:, 2 * LANES * h : 2 * LANES * (h + 1)]
        q_own, k_own = q * own[h : h + 1, :], k * own[h : h + 1, :]
        v = head_cols(v_ref, h)
        dnum, dden = output_grads(do_ref, o_ref, den_ref, h)
        state, carried = s_ref[0, h], g_ref[0, h]

        left, right = sides(q, pick, ones[...], h)
        wide = jnp.concatenate([dnum, jnp.where(first_lane, dden, 0.0).astype(BF)], 1)
        dfeat = nt(wide, state) * (scale[...] * m.use)
        pulled = jnp.concatenate([(dfeat * right).astype(BF), (dfeat * left).astype(BF)], 1)
        dq[...] += nt(pulled, table)

        left, right = sides(k, pick, ones[...], h)
        wide = jnp.concatenate([v, jnp.where(first_lane, 1.0, 0.0).astype(BF)], 1)
        dfeat = nt(wide, carried) * (scale[...] * m.tail)
        pulled = jnp.concatenate([(dfeat * right).astype(BF), (dfeat * left).astype(BF)], 1)
        dk[...] += nt(pulled, table)
        feat = (left * right * (scale[...] * m.tail)).astype(BF)
        dv[...] = nn(feat, carried[:, :HEAD_V])

        for at in range(0, block, TILE):
            count = at + TILE
            prod = nt(q_own[at:count], k[:count])
            one = 1.0 + prod
            mask = m.mask(at, count)
            score = jnp.where(mask, one + 0.5 * prod * prod, 0.0).astype(BF)
            dscore = nt(dnum[at:count], v[:count]) + dden[at:count, :1]
            dprod = jnp.where(mask, dscore * one, 0.0).astype(BF)
            dq[at:count] += nn(dprod, k_own[:count])
            dk[:count] += tn(dprod, q_own[at:count])
            dv[:count] += tn(score, dnum[at:count])
        dv_ref[:, HEAD_V * h : HEAD_V * (h + 1)] = dv[...].astype(BF)
    dq_ref[...] = dq[...].astype(BF)
    dk_ref[...] = dk[...].astype(BF)


def mixer_calls(heads, block, blocks):
    tables = feature_tables(heads)
    narrow = pl.BlockSpec((block, heads * QK), lambda b, marks: (b, 0))
    wide = pl.BlockSpec((block, heads * HEAD_V), lambda b, marks: (b, 0))
    local = pl.BlockSpec((1, heads, NFEAT, 2 * HEAD_V), lambda b, marks: (b, 0, 0, 0))
    state = pl.BlockSpec((1, heads, LANES, 2 * HEAD_V), lambda b, marks: (b, 0, 0, 0))
    fixed = [pl.BlockSpec(t.shape, lambda b, marks: (0, 0)) for t in tables]
    rows = block * blocks

    def call(kernel, specs, used, outs, scratch, cost):
        def run(marks, *args):
            return pl.pallas_call(
                functools.partial(kernel, heads=heads, block=block),
                grid_spec=pltpu.PrefetchScalarGridSpec(
                    num_scalar_prefetch=1,
                    grid=(blocks,),
                    in_specs=specs + fixed[:used],
                    out_specs=[o[0] for o in outs],
                    scratch_shapes=scratch,
                ),
                out_shape=[jax.ShapeDtypeStruct(*o[1:]) for o in outs],
                cost_estimate=pl.CostEstimate(
                    flops=cost * rows * heads, bytes_accessed=rows * heads * 1500, transcendentals=0
                ),
                compiler_params=pltpu.CompilerParams(vmem_limit_bytes=48 * 2**20),
            )(marks, *args, *tables[:used])

        return run

    local_out = (local, (blocks, heads, NFEAT, 2 * HEAD_V), F32)
    wide_b, wide_f = (wide, (rows, heads * HEAD_V), BF), (wide, (rows, heads * HEAD_V), F32)
    narrow_b = (narrow, (rows, heads * QK), BF)
    scratch = [
        pltpu.VMEM((block, heads * QK), F32),
        pltpu.VMEM((block, heads * QK), F32),
        pltpu.VMEM((block, HEAD_V), F32),
    ]
    return (
        call(state_kernel, [narrow, wide], 3, [local_out], [], 500000),
        call(mixer_kernel, [narrow, narrow, wide, state], 4, [wide_b, wide_f], [], 1000000),
        call(grad_state_kernel, [narrow, wide, wide, wide], 3, [local_out], [], 500000),
        call(
            mixer_back_kernel,
            [narrow, narrow, wide, wide, wide, wide, state, state],
            4,
            [narrow_b, narrow_b, wide_b],
            scratch,
            2500000,
        ),
    )


def dot(a, b, ca=1, cb=0):
    return lax.dot_general(a, b, (((ca,), (cb,)), ((), ())), preferred_element_type=F32)


def tie(*values):
    return lax.optimization_barrier(values)


def place_kernel(offsets, *refs, axis):
    *pieces, out, sems = refs
    copies = []
    for i, piece in enumerate(pieces):
        size = piece.shape[axis]
        span = pl.ds(pl.multiple_of(offsets[i], size), size)
        target = out.at[span] if axis == 0 else out.at[:, span]
        copies.append(pltpu.make_async_copy(piece, target, sems.at[i]))
    for copy in copies:
        copy.start()
    for copy in copies:
        copy.wait()


def place(pieces, offsets, axis):
    shape = list(pieces[0].shape)
    shape[axis] = sum(p.shape[axis] for p in pieces)
    size = int(np.prod(shape)) * pieces[0].dtype.itemsize
    return pl.pallas_call(
        functools.partial(place_kernel, axis=axis),
        grid_spec=pltpu.PrefetchScalarGridSpec(
            num_scalar_prefetch=1,
            grid=(),
            in_specs=[pl.BlockSpec(memory_space=pltpu.VMEM)] * len(pieces),
            out_specs=pl.BlockSpec(memory_space=pl.ANY),
            scratch_shapes=[pltpu.SemaphoreType.DMA((len(pieces),))],
        ),
        compiler_params=pltpu.CompilerParams(vmem_limit_bytes=32 * 2**20),
        out_shape=jax.ShapeDtypeStruct(tuple(shape), pieces[0].dtype),
        cost_estimate=pl.CostEstimate(flops=0, bytes_accessed=2 * size, transcendentals=0),
    )(jnp.stack(offsets).astype(jnp.int32), *pieces)


def widen_kernel(where, *refs, group):
    *shares, out = refs
    count, core = (len(shares) + 1) // 2, where[1]
    piece = shares[0].shape[2]
    for d in range(count):
        plane = lax.rem(where[0] + count - d, count)
        batch, part = plane // group, lax.rem(plane, group)
        for j in range(CORES):
            got = shares[d][j].astype(F32)
            if d:
                got = got + shares[2 * count - 1 - d][j].astype(F32)
            k = core if j == 0 else 1 - core
            at = pl.multiple_of((k * group + part) * piece, piece)
            out[batch, :, pl.ds(at, piece)] = got


def widen(shares, feat_rank, core, micro, group, width):
    _, block, piece = shares[0].shape
    tile = 128
    return pl.pallas_call(
        functools.partial(widen_kernel, group=group),
        grid_spec=pltpu.PrefetchScalarGridSpec(
            num_scalar_prefetch=1,
            grid=(block // tile,),
            in_specs=[pl.BlockSpec((CORES, tile, piece), lambda i, w: (0, i, 0))] * len(shares),
            out_specs=pl.BlockSpec((micro, tile, width), lambda i, w: (0, i, 0)),
        ),
        out_shape=jax.ShapeDtypeStruct((micro, block, width), F32),
        compiler_params=pltpu.CompilerParams(vmem_limit_bytes=48 * 2**20),
    )(jnp.stack([feat_rank, core]).astype(jnp.int32), *shares)


def on_device(
    tokens,
    cotangent,
    lengths,
    w_query,
    w_key,
    w_value,
    w_output,
    w_gate,
    w_up,
    w_down,
    gain_mixer,
    gain_mlp,
):
    micro, block, width = tokens.shape
    seq_count, feat_count = lax.axis_size("seq"), lax.axis_size("feat")
    seq_rank, feat_rank = lax.axis_index("seq"), lax.axis_index("feat")
    group = feat_count // micro
    ranks = CORES * group
    chips = seq_count // CORES
    chip, core = seq_rank // CORES, seq_rank % CORES
    batch, part = feat_rank // group, feat_rank % group
    rank = core * group + part
    rows = CORES * block
    piece = width // ranks
    heads = HEADS // ranks

    def move(value, target):
        pairs = []
        for s in range(seq_count):
            for f in range(feat_count):
                here = (s // CORES, s % CORES, f // group, f % group)
                there = target(*here)
                if there is not None and there != here:
                    c2, k2, m2, l2 = there
                    pairs.append(
                        (s * feat_count + f, (c2 * CORES + k2) * feat_count + m2 * group + l2)
                    )
        return lax.ppermute(value, ("seq", "feat"), pairs)

    def to_core(value):
        return move(value, lambda c, k, m, l: (c, 1 - k, m, l))

    def to_part(value, d):
        return move(value, lambda c, k, m, l: (c, k, m, l ^ d))

    def to_chip(value, mask):
        return move(value, lambda c, k, m, l: (c ^ mask, k, m, l))

    def shift_chip(value, d):
        return move(value, lambda c, k, m, l: (c + d, k, m, l) if 0 <= c + d < chips else None)

    def spread(value):
        moved = move(value, lambda c, k, m, l: (c, m, k, l))
        other = move(value, lambda c, k, m, l: (c, m, 1 - k, l))
        return jnp.where(core == batch, value, moved), other

    def unspread(same, other):
        moved = move(same, lambda c, k, m, l: (c, m, k, l))
        other = move(other, lambda c, k, m, l: (c, 1 - m, k, l))
        return jnp.where(core == batch, same, moved), other

    def ordered(first_if_zero, second_if_zero, bit, axis):
        return jnp.where(
            bit == 0,
            jnp.concatenate([first_if_zero, second_if_zero], axis),
            jnp.concatenate([second_if_zero, first_if_zero], axis),
        )

    chip_groups = [[c * CORES + k for c in range(chips)] for k in range(CORES)]

    bits = [1 << i for i in range(chips.bit_length() - 1)]
    orders = (bits, bits[::-1])

    def all_hops(owns):
        helds = [{0: own} for own in owns]
        for held, order in zip(helds, orders):
            for bit in order:
                for mask in list(held):
                    held[mask | bit] = to_chip(held[mask], bit)
        return helds

    def straight(owns):
        return [
            {mask: to_chip(own, mask) if mask else own for mask in range(chips)} for own in owns
        ]

    def place_chips(helds, axis):
        size = helds[0][0].shape[axis]
        pieces, offsets = [], []
        for held, k in zip(helds, (batch, 1 - batch)):
            for mask, got in held.items():
                pieces.append(got)
                offsets.append(((chip ^ mask) * CORES + k) * size)
        return place(pieces, offsets, axis)

    def gather_chips_bulk(owns, axis):
        size = owns[0].shape[axis]
        both = place(list(owns), [batch * size, (1 - batch) * size], axis)
        return lax.all_gather(
            both, "seq", axis=axis, tiled=True, axis_index_groups=chip_groups
        )

    def sum_chips(value, axis):
        return lax.psum_scatter(
            value, "seq", scatter_dimension=axis, tiled=True, axis_index_groups=chip_groups
        )

    def send_halves(mine, axis):
        size = mine.shape[axis] // CORES
        same = lax.dynamic_slice_in_dim(mine, batch * size, size, axis)
        other = lax.dynamic_slice_in_dim(mine, (1 - batch) * size, size, axis)
        return unspread(same, other)

    def add(halves):
        return halves[0].astype(F32) + halves[1].astype(F32)

    def send_parts(own):
        return [to_part(own, d) for d in range(1, group)]

    def gather_ranks(own, arrived):
        found = []
        for d, here in enumerate([own, *arrived]):
            found.append((core * group + (part ^ d), here))
            found.append(((1 - core) * group + (part ^ d), to_core(here)))
        return found

    def reduce_part(partial, d):
        away = to_core(partial((1 - core) * group + (part ^ d)).astype(BF))
        return partial(core * group + (part ^ d)) + away.astype(F32)

    def reduce_away(partial):
        return [reduce_part(partial, d).astype(BF) for d in range(1, group)]

    def reduce_send(totals):
        return [to_part(total, d + 1) for d, total in enumerate(totals)]

    def reduce_end(own, arrived):
        return sum((got.astype(F32) for got in arrived), own)

    def sum_ranks(value):
        for d in [1 << i for i in range(group.bit_length() - 1)]:
            value = value + to_part(value, d)
        return value + to_core(value)

    def row_piece(value, r):
        return lax.dynamic_slice_in_dim(value, r * piece, piece, 0)

    def column_piece(value, r):
        return lax.dynamic_slice_in_dim(value, r * piece, piece, 1)

    def chip_tokens(value):
        own = lax.dynamic_index_in_dim(value, batch, 0, False)
        return place([own, to_core(own)], [core * block, (1 - core) * block], 0)

    tokens_c = chip_tokens(tokens)
    grad_out = chip_tokens(cotangent)

    def half(value, k):
        return lax.dynamic_slice_in_dim(value, k * block, block, 0)

    qk_width, v_width = heads * QK, heads * HEAD_V
    qkv_owns = spread(jnp.concatenate([w_query, w_key, w_value], 1))
    gains = lax.all_gather(jnp.stack([gain_mixer, gain_mlp]), "seq", axis=1, tiled=True)
    w_output, gains, *qkv_owns = tie(w_output, gains, *qkv_owns)
    gains = gains.astype(F32)
    mixer_gain, mlp_gain = gains[0], gains[1]
    output_owns = spread(w_output)
    qkv_full = place_chips(all_hops(qkv_owns), 0)
    w_gate, qkv_full, output_owns = tie(w_gate.T, qkv_full, output_owns)
    gate_owns = spread(w_gate)

    bounds = jnp.cumsum(lax.dynamic_index_in_dim(lengths, batch, 0, False))

    def segment_of(p):
        return jnp.sum((p[..., None] >= bounds).astype(jnp.int32), axis=-1)

    start = chip * rows
    base = start + block * jnp.arange(CORES + 1, dtype=jnp.int32)
    edges = jnp.where(base == 0, -1, segment_of(base - 1))
    keep = (edges[1:] == edges[:-1]).astype(F32)
    base = base[:-1]
    ends = jnp.concatenate([jnp.zeros((1,), jnp.int32), bounds])
    open_end = jnp.where((edges[:-1] < 0) | (edges[:-1] > 2), 0, ends[edges[:-1] + 1] - base)
    tail_start = jnp.where(edges[1:] > 2, block, ends[edges[1:]] - base)
    marks = jnp.concatenate(
        [bounds[None, :] - base[:, None], open_end[:, None], tail_start[:, None]], 1
    ).astype(jnp.int32)

    tokens_f = tokens_c.astype(F32)
    inv_one = lax.rsqrt(jnp.mean(tokens_f * tokens_f, axis=-1, keepdims=True) + EPS)
    normed = (tokens_f * inv_one * mixer_gain).astype(BF)
    qkv = dot(normed, qkv_full).astype(BF)

    query, keys = qkv[:, :qk_width], qkv[:, qk_width : 2 * qk_width]
    values = qkv[:, 2 * qk_width :]
    local_states, mixer, grad_states, mixer_back = mixer_calls(heads, block, CORES)

    def pack(state, total):
        total = jnp.pad(total, ((0, 0), (0, -NFEAT % HEAD_V))).reshape(-1, HEAD_V)
        return jnp.concatenate([state.reshape(-1, HEAD_V), total], 0).astype(BF)

    def unpack(flat):
        cut = heads * NFEAT
        return (
            flat[:cut].reshape(heads, NFEAT, HEAD_V).astype(F32),
            flat[cut:].reshape(heads, -1)[:, :NFEAT].astype(F32),
        )

    def scan_blocks(both, blocks_order, step, meanwhile):
        state, total = both[..., :HEAD_V], both[..., HEAD_V]
        at_end = (state[blocks_order[0]], total[blocks_order[0]])
        for i in blocks_order[1:]:
            carry_keep = keep[i]
            at_end = (
                state[i] + carry_keep * at_end[0],
                total[i] + carry_keep * at_end[1],
            )
        message = pack(*at_end)
        run = None
        arrived = [shift_chip(message, step * d) for d in range(1, chips)]
        *arrived, state, total, meanwhile = tie(*arrived, state, total, meanwhile)
        for d in range(1, chips):
            got = unpack(arrived[d - 1])
            other = chip - step * d
            if step > 0:
                same = edges[0] == segment_of((other + 1) * rows - 1)
            else:
                same = edges[CORES] == segment_of(other * rows - 1)
            weight = (same & (other >= 0) & (other < chips)).astype(F32)
            term = (weight * got[0], weight * got[1])
            run = term if run is None else (run[0] + term[0], run[1] + term[1])
        found = {}
        for i in blocks_order:
            found[i] = run
            run = (state[i] + keep[i] * run[0], total[i] + keep[i] * run[1])
        state, total = (jnp.stack([found[i][j] for i in range(CORES)]) for j in range(2))
        total = jnp.broadcast_to(total[..., None], state.shape)
        both = jnp.concatenate([state, total], -1).astype(BF)
        both = jnp.pad(both, ((0, 0), (0, 0), (0, LANES - NFEAT), (0, 0)))
        return both, meanwhile

    (local,) = local_states(marks, keys, values)
    states, gate_owns = scan_blocks(local, list(range(CORES)), 1, gate_owns)
    w_up, states, output_owns = tie(w_up.T, states, output_owns)
    up_owns = spread(w_up)
    gate_full = gather_chips_bulk(gate_owns, 1)
    mixer_own, denom = mixer(marks, query, keys, values, states)
    mixer_own, up_owns = tie(mixer_own, up_owns)

    arrived = send_parts(mixer_own)
    up_full = gather_chips_bulk(up_owns, 1)
    output_full = place_chips(all_hops(output_owns), 0)
    w_down, mixer_own = tie(w_down, mixer_own)
    down_owns = spread(w_down)
    mixer_parts = gather_ranks(mixer_own, arrived)
    branch_own = sum(dot(got, row_piece(output_full, r)) for r, got in mixer_parts).astype(BF)
    branch_own, down_owns = tie(branch_own, down_owns)
    arrived = send_parts(branch_own)
    downs = straight(down_owns)
    *arrived, gate_full = tie(*arrived, gate_full)
    branch_parts = gather_ranks(branch_own, arrived)
    branch = place([got for _, got in branch_parts], [r * piece for r, _ in branch_parts], 1)
    hidden_state = tokens_f + branch.astype(F32)
    inv_two = lax.rsqrt(jnp.mean(hidden_state * hidden_state, axis=-1, keepdims=True) + EPS)
    normed_two = (hidden_state * inv_two * mlp_gain).astype(BF)

    gate = dot(normed_two, gate_full, 1, 1).astype(BF)
    upward = dot(normed_two, up_full, 1, 1).astype(BF)
    hidden = jax.nn.silu(gate.astype(F32)) * upward.astype(F32)
    hidden = hidden.astype(BF)
    down_sum = dot(hidden, grad_out, 0, 0).astype(BF)
    downs, gate, upward, hidden, down_sum = tie(downs, gate, upward, hidden, down_sum)
    down_sum = sum_chips(down_sum, 1)
    down_full = place_chips(downs, 1)
    gate, upward = gate.astype(F32), upward.astype(F32)
    grad_hidden = dot(grad_out, down_full, 1, 1).astype(BF).astype(F32)
    logistic = jax.nn.sigmoid(gate)
    activated = gate * logistic
    grad_gate_f = grad_hidden * upward * logistic * (1.0 + gate * (1.0 - logistic))
    grad_up_f = grad_hidden * activated
    grad_gate_b, grad_up_b = grad_gate_f.astype(BF), grad_up_f.astype(BF)
    inner_two = sum_ranks(jnp.sum(grad_gate_f * gate + grad_up_f * upward, axis=1)) / width
    def hidden_part(grads, r):
        return dot(grads[0], column_piece(gate_full, r)) + dot(grads[1], column_piece(up_full, r))

    grads = (grad_gate_b, grad_up_b)
    totals = reduce_away(functools.partial(hidden_part, grads))
    inner_two, totals, grads = tie(inner_two, totals, grads)
    arrived = reduce_send(totals)
    own = reduce_part(functools.partial(hidden_part, grads), 0)
    up_sum = sum_chips(dot(grads[1], normed_two, 0, 0).astype(BF), 1)
    gate_sum = dot(grads[0], normed_two, 0, 0).astype(BF)
    own, gate_sum, arrived, down_sum = tie(own, gate_sum, arrived, down_sum)
    normed_grad = reduce_end(own, arrived)
    down_halves = send_halves(down_sum, 1)
    gate_sum = sum_chips(gate_sum, 1)
    tokens_own = column_piece(tokens_c, rank).astype(F32)
    hidden_own = tokens_own + branch_own.astype(F32)
    scaled_two = hidden_own * inv_two
    mlp_gain_own = lax.dynamic_slice_in_dim(mlp_gain, rank * piece, piece, 0)
    hidden_grad = column_piece(grad_out, rank).astype(F32) + inv_two * (
        normed_grad * mlp_gain_own - scaled_two * inner_two[:, None]
    )
    grad_gain_mlp = jnp.sum(normed_grad * scaled_two, axis=0)
    branch_grad = hidden_grad.astype(BF)

    def output_part(grad, r):
        return dot(grad, row_piece(output_full, r), 1, 1)

    totals = reduce_away(functools.partial(output_part, branch_grad))
    totals, branch_grad, hidden = tie(totals, branch_grad, hidden)
    arrived = reduce_send(totals)
    own = reduce_part(functools.partial(output_part, branch_grad), 0)

    def down_part(r):
        return dot(hidden, column_piece(down_full, r))

    mlp_totals, mlp_own = reduce_away(down_part), reduce_part(down_part, 0)
    arrived, own, mlp_own, mlp_totals, down_halves, up_sum = tie(
        arrived, own, mlp_own, mlp_totals, down_halves, up_sum
    )
    mixer_grad = reduce_end(own, arrived)
    mlp_arrived = reduce_send(mlp_totals)
    (grad_local,) = grad_states(marks, query, mixer_grad, mixer_own, denom)
    grad_local, branch_grad = tie(grad_local, branch_grad)
    output_sum = place(
        [dot(got, branch_grad, 0, 0).astype(BF) for _, got in mixer_parts],
        [r * piece for r, _ in mixer_parts],
        0,
    )
    carried, (mlp_arrived, output_sum) = scan_blocks(
        grad_local, list(range(CORES))[::-1], -1, (mlp_arrived, output_sum)
    )
    carried, output_sum, gate_sum, up_sum = tie(carried, output_sum, gate_sum, up_sum)
    up_halves = send_halves(up_sum, 1)
    output_sum = sum_chips(output_sum, 0)
    grad_qkv = mixer_back(
        marks, query, keys, values, mixer_grad, mixer_own, denom, states, carried
    )
    grad_qkv, up_halves = tie(grad_qkv, up_halves)
    grad_qkv = jnp.concatenate(grad_qkv, 1)
    inner_one = jnp.sum(grad_qkv.astype(F32) * qkv.astype(F32), axis=1)
    inner_one = sum_ranks(inner_one) / width

    def input_part(grad, r):
        return dot(grad, row_piece(qkv_full, r), 1, 1)

    totals = reduce_away(functools.partial(input_part, grad_qkv))
    totals, grad_qkv, inner_one = tie(totals, grad_qkv, inner_one)
    arrived = reduce_send(totals)
    mixed_own = (hidden_own + reduce_end(mlp_own, mlp_arrived)).astype(BF)
    mixed_halves = unspread(half(mixed_own, batch), half(mixed_own, 1 - batch))
    own = reduce_part(functools.partial(input_part, grad_qkv), 0)
    qkv_sum = dot(normed, grad_qkv, 0, 0).astype(BF)
    arrived, own, mixed_halves, qkv_sum, output_sum = tie(
        arrived, own, mixed_halves, qkv_sum, output_sum
    )
    input_normed = reduce_end(own, arrived)
    qkv_sum = sum_chips(qkv_sum, 0)
    mixed = ordered(mixed_halves[0][None], mixed_halves[1][None], core, 0)
    scaled_one = tokens_own * inv_one
    mixer_gain_own = lax.dynamic_slice_in_dim(mixer_gain, rank * piece, piece, 0)
    grad_gain_mixer = jnp.sum(input_normed * scaled_one, axis=0)
    input_own = (
        hidden_grad
        + inv_one * (input_normed * mixer_gain_own - scaled_one * inner_one[:, None])
    ).astype(BF)

    gain_grads = lax.dynamic_update_slice_in_dim(
        jnp.zeros((2, width), F32), jnp.stack([grad_gain_mixer, grad_gain_mlp]), rank * piece, 1
    )
    other_half = to_core(half(input_own, 1 - core))
    input_own, other_half = tie(input_own, other_half)
    input_pair = jnp.stack([half(input_own, core), other_half])
    input_pair, gain_grads = tie(input_pair, gain_grads)
    planes = [
        move(gain_grads, lambda c, k, m, l: (c, k, *divmod((m * group + l) ^ d, group)))
        for d in range(1, feat_count)
    ]

    def step_plane(value, step, first):
        def target(c, k, m, l):
            here = m * group + l
            behind = here if step > 0 else feat_count - 1 - here
            if behind < first or behind == feat_count - 1:
                return None
            return (c, k, *divmod(here + step, group))

        return move(value, target)

    hops = [to_core] + [
        functools.partial(to_chip, mask=1 << i) for i in range(chips.bit_length() - 1)
    ]
    ups, downs = [input_pair], [input_pair]
    for d in range(feat_count - 1):
        up, down = step_plane(ups[-1], 1, d), step_plane(downs[-1], -1, d)
        if d == 0:
            up, down, planes, output_sum = tie(up, down, planes, output_sum)
            output_halves = send_halves(output_sum, 0)
            gain_grads = sum(planes, gain_grads)
        elif hops:
            up, down, gain_grads, got = tie(up, down, gain_grads, hops[0](gain_grads))
            gain_grads, hops = gain_grads + got, hops[1:]
        if d == feat_count - 3:
            up, down, gate_sum, qkv_sum = tie(up, down, gate_sum, qkv_sum)
            gate_halves, qkv_halves = send_halves(gate_sum, 1), send_halves(qkv_sum, 0)
        ups.append(up), downs.append(down)
    for hop in hops:
        gain_grads = gain_grads + hop(gain_grads)
    input_grad = widen(ups + downs[1:], feat_rank, core, micro, group, width)

    shard = width // seq_count
    gain_grads = lax.dynamic_slice_in_dim(gain_grads, seq_rank * shard, shard, 1)

    grad_qkv_w = add(qkv_halves)
    return (
        mixed,
        input_grad,
        grad_qkv_w[:, :qk_width],
        grad_qkv_w[:, qk_width : 2 * qk_width],
        grad_qkv_w[:, 2 * qk_width :],
        add(output_halves),
        add(gate_halves).T,
        add(up_halves).T,
        add(down_halves),
        gain_grads[0],
        gain_grads[1],
    )


def solution(mesh):
    in_specs = (
        P(None, "seq", None),
        P(None, "seq", None),
        P(),
        P("seq", "feat"),
        P("seq", "feat"),
        P("seq", "feat"),
        P("seq", "feat"),
        P("seq", "feat"),
        P("seq", "feat"),
        P("feat", "seq"),
        P("seq"),
        P("seq"),
    )
    out_specs = (
        P(None, "seq", "feat"),
        P(None, "seq", None),
        P("seq", "feat"),
        P("seq", "feat"),
        P("seq", "feat"),
        P("seq", "feat"),
        P("seq", "feat"),
        P("seq", "feat"),
        P("feat", "seq"),
        P("seq"),
        P("seq"),
    )
    return jax.shard_map(
        on_device, mesh=mesh, in_specs=in_specs, out_specs=out_specs, check_vma=False
    )
```

```python
import functools

import jax
import jax.numpy as jnp
import numpy as np
from jax import lax
from jax.experimental import pallas as pl
from jax.experimental.pallas import tpu as pltpu
from jax.sharding import PartitionSpec as P

HEADS = 16
HEAD_V = 128
QK = 16
NFEAT = 160
CORES = 2
EPS = 1e-05
BF = jnp.bfloat16
F32 = jnp.float32


LANES = 256
TILE = 256


def feature_tables(heads):
    left, right, scale = [-1], [-1], [1.0]
    for i in range(QK):
        left.append(i), right.append(-1), scale.append(1.0)
    for i in range(QK):
        for j in range(i, QK):
            left.append(i), right.append(j), scale.append(1.0 if i < j else 0.7071067811865476)
    padding = LANES - len(left)
    left, right, scale = left + [-2] * padding, right + [-2] * padding, scale + [0.0] * padding
    both = np.array(left + right)
    pick = np.zeros((heads * QK, heads, 2 * LANES), np.float32)
    for h in range(heads):
        pick[h * QK : (h + 1) * QK, h] = 0.5 * (np.arange(QK)[:, None] == both[None, :])
    ones = (both == -1).astype(np.float32)[None]
    own = np.zeros((8, heads * QK), np.float32)
    for h in range(heads):
        own[h, h * QK : (h + 1) * QK] = 0.25
    return (
        jnp.asarray(pick.reshape(heads * QK, -1), BF),
        jnp.asarray(ones),
        jnp.asarray(np.array(scale, np.float32)[None]),
        jnp.asarray(own, BF),
    )


def nt(a, b):
    return lax.dot_general(a, b, (((1,), (1,)), ((), ())), preferred_element_type=F32)


def tn(a, b):
    return lax.dot_general(a, b, (((0,), (0,)), ((), ())), preferred_element_type=F32)


def nn(a, b):
    return lax.dot_general(a, b, (((1,), (0,)), ((), ())), preferred_element_type=F32)


class Marks:
    def __init__(self, marks, b, block):
        t = lax.broadcasted_iota(jnp.int32, (block, 1), 0)
        first, second, third = marks[b, 0], marks[b, 1], marks[b, 2]
        low = jnp.where(t >= first, first, 0)
        low = jnp.where(t >= second, second, low)
        self.low = jnp.where(t >= third, block, low)
        self.padding = jnp.where(t >= third, 1.0, 0.0).astype(F32)
        self.use = jnp.where(t < marks[b, 3], 1.0, 0.0).astype(F32)
        self.tail = jnp.where(t >= marks[b, 4], 1.0, 0.0).astype(F32)

    def mask(self, at, count):
        t = lax.broadcasted_iota(jnp.int32, (TILE, count), 0) + at
        s = lax.broadcasted_iota(jnp.int32, (TILE, count), 1)
        return (s <= t) & (s >= self.low[at : at + TILE])


def sides(x, pick, ones, h):
    both = nn(x, pick[:, 2 * LANES * h : 2 * LANES * (h + 1)]) + ones
    return both[:, :LANES], both[:, LANES:]


def head_cols(ref, h):
    return ref[:, HEAD_V * h : HEAD_V * (h + 1)]


def output_grads(do_ref, o_ref, den_ref, h):
    do, o, den = head_cols(do_ref, h), head_cols(o_ref, h).astype(F32), head_cols(den_ref, h)
    do = do.astype(F32)
    inverse = 1.0 / den
    dnum = (do * inverse).astype(BF)
    dden = -jnp.sum(do * o, axis=1, keepdims=True) * inverse
    return dnum, dden


def state_kernel(marks, k_ref, v_ref, pick, ones, scale, out_ref, *, heads, block):
    m = Marks(marks, pl.program_id(0), block)
    k = k_ref[...]
    for h in range(heads):
        left, right = sides(k, pick, ones[...], h)
        feat = (left * right * (scale[...] * m.tail)).astype(BF)
        v = head_cols(v_ref, h)
        out_ref[0, h] = tn(feat, jnp.concatenate([v, jnp.ones_like(v)], 1))[:NFEAT]


def grad_state_kernel(
    marks, q_ref, do_ref, o_ref, den_ref, pick, ones, scale, out_ref, *, heads, block
):
    m = Marks(marks, pl.program_id(0), block)
    q = q_ref[...]
    for h in range(heads):
        left, right = sides(q, pick, ones[...], h)
        feat = (left * right * (scale[...] * m.use)).astype(BF)
        dnum, dden = output_grads(do_ref, o_ref, den_ref, h)
        out_ref[0, h] = tn(feat, jnp.concatenate([dnum, dden.astype(BF)], 1))[:NFEAT]


def mixer_kernel(
    marks, q_ref, k_ref, v_ref, s_ref, pick, ones, scale, own, o_ref, den_ref, *, heads, block
):
    m = Marks(marks, pl.program_id(0), block)
    q, k = q_ref[...], k_ref[...]
    for h in range(heads):
        q_own = q * own[h : h + 1, :]
        left, right = sides(q, pick, ones[...], h)
        feat = (left * right * scale[...]).astype(BF)
        before = nn(feat, s_ref[0, h]) * m.use
        v = head_cols(v_ref, h)
        v_one = jnp.concatenate([v, jnp.ones_like(v)], 1)
        for at in range(0, block, TILE):
            count = at + TILE
            prod = nt(q_own[at:count], k[:count])
            score = 1.0 + prod + 0.5 * prod * prod
            score = jnp.where(m.mask(at, count), score, 0.0).astype(BF)
            both = nn(score, v_one[:count]) + before[at:count]
            den = both[:, HEAD_V:] + m.padding[at:count]
            here = (slice(at, count), slice(HEAD_V * h, HEAD_V * (h + 1)))
            o_ref[here] = (both[:, :HEAD_V] / den).astype(BF)
            den_ref[here] = den


def mixer_back_kernel(
    marks,
    q_ref,
    k_ref,
    v_ref,
    do_ref,
    o_ref,
    den_ref,
    s_ref,
    g_ref,
    pick,
    ones,
    scale,
    own,
    dq_ref,
    dk_ref,
    dv_ref,
    dq,
    dk,
    dv,
    *,
    heads,
    block,
):
    m = Marks(marks, pl.program_id(0), block)
    q, k = q_ref[...], k_ref[...]
    first_lane = lax.broadcasted_iota(jnp.int32, (block, HEAD_V), 1) == 0
    dq[...] = jnp.zeros_like(dq)
    dk[...] = jnp.zeros_like(dk)
    for h in range(heads):
        table = pick[:, 2 * LANES * h : 2 * LANES * (h + 1)]
        q_own, k_own = q * own[h : h + 1, :], k * own[h : h + 1, :]
        v = head_cols(v_ref, h)
        dnum, dden = output_grads(do_ref, o_ref, den_ref, h)
        state, carried = s_ref[0, h], g_ref[0, h]

        left, right = sides(q, pick, ones[...], h)
        wide = jnp.concatenate([dnum, jnp.where(first_lane, dden, 0.0).astype(BF)], 1)
        dfeat = nt(wide, state) * (scale[...] * m.use)
        pulled = jnp.concatenate([(dfeat * right).astype(BF), (dfeat * left).astype(BF)], 1)
        dq[...] += nt(pulled, table)

        left, right = sides(k, pick, ones[...], h)
        wide = jnp.concatenate([v, jnp.where(first_lane, 1.0, 0.0).astype(BF)], 1)
        dfeat = nt(wide, carried) * (scale[...] * m.tail)
        pulled = jnp.concatenate([(dfeat * right).astype(BF), (dfeat * left).astype(BF)], 1)
        dk[...] += nt(pulled, table)
        feat = (left * right * (scale[...] * m.tail)).astype(BF)
        dv[...] = nn(feat, carried[:, :HEAD_V])

        for at in range(0, block, TILE):
            count = at + TILE
            prod = nt(q_own[at:count], k[:count])
            one = 1.0 + prod
            mask = m.mask(at, count)
            score = jnp.where(mask, one + 0.5 * prod * prod, 0.0).astype(BF)
            dscore = nt(dnum[at:count], v[:count]) + dden[at:count, :1]
            dprod = jnp.where(mask, dscore * one, 0.0).astype(BF)
            dq[at:count] += nn(dprod, k_own[:count])
            dk[:count] += tn(dprod, q_own[at:count])
            dv[:count] += tn(score, dnum[at:count])
        dv_ref[:, HEAD_V * h : HEAD_V * (h + 1)] = dv[...].astype(BF)
    dq_ref[...] = dq[...].astype(BF)
    dk_ref[...] = dk[...].astype(BF)


def mixer_calls(heads, block, blocks):
    tables = feature_tables(heads)
    narrow = pl.BlockSpec((block, heads * QK), lambda b, marks: (b, 0))
    wide = pl.BlockSpec((block, heads * HEAD_V), lambda b, marks: (b, 0))
    local = pl.BlockSpec((1, heads, NFEAT, 2 * HEAD_V), lambda b, marks: (b, 0, 0, 0))
    state = pl.BlockSpec((1, heads, LANES, 2 * HEAD_V), lambda b, marks: (b, 0, 0, 0))
    fixed = [pl.BlockSpec(t.shape, lambda b, marks: (0, 0)) for t in tables]
    rows = block * blocks

    def call(kernel, specs, used, outs, scratch, cost):
        def run(marks, *args):
            return pl.pallas_call(
                functools.partial(kernel, heads=heads, block=block),
                grid_spec=pltpu.PrefetchScalarGridSpec(
                    num_scalar_prefetch=1,
                    grid=(blocks,),
                    in_specs=specs + fixed[:used],
                    out_specs=[o[0] for o in outs],
                    scratch_shapes=scratch,
                ),
                out_shape=[jax.ShapeDtypeStruct(*o[1:]) for o in outs],
                cost_estimate=pl.CostEstimate(
                    flops=cost * rows * heads, bytes_accessed=rows * heads * 1500, transcendentals=0
                ),
                compiler_params=pltpu.CompilerParams(vmem_limit_bytes=48 * 2**20),
            )(marks, *args, *tables[:used])

        return run

    local_out = (local, (blocks, heads, NFEAT, 2 * HEAD_V), F32)
    wide_b, wide_f = (wide, (rows, heads * HEAD_V), BF), (wide, (rows, heads * HEAD_V), F32)
    narrow_b = (narrow, (rows, heads * QK), BF)
    scratch = [
        pltpu.VMEM((block, heads * QK), F32),
        pltpu.VMEM((block, heads * QK), F32),
        pltpu.VMEM((block, HEAD_V), F32),
    ]
    return (
        call(state_kernel, [narrow, wide], 3, [local_out], [], 500000),
        call(mixer_kernel, [narrow, narrow, wide, state], 4, [wide_b, wide_f], [], 1000000),
        call(grad_state_kernel, [narrow, wide, wide, wide], 3, [local_out], [], 500000),
        call(
            mixer_back_kernel,
            [narrow, narrow, wide, wide, wide, wide, state, state],
            4,
            [narrow_b, narrow_b, wide_b],
            scratch,
            2500000,
        ),
    )


def dot(a, b, ca=1, cb=0):
    return lax.dot_general(a, b, (((ca,), (cb,)), ((), ())), preferred_element_type=F32)


def tie(*values):
    return lax.optimization_barrier(values)


def place_kernel(offsets, *refs, axis):
    *pieces, out, sems = refs
    copies = []
    for i, piece in enumerate(pieces):
        size = piece.shape[axis]
        span = pl.ds(pl.multiple_of(offsets[i], size), size)
        target = out.at[span] if axis == 0 else out.at[:, span]
        copies.append(pltpu.make_async_copy(piece, target, sems.at[i]))
    for copy in copies:
        copy.start()
    for copy in copies:
        copy.wait()


def place(pieces, offsets, axis):
    shape = list(pieces[0].shape)
    shape[axis] = sum(p.shape[axis] for p in pieces)
    size = int(np.prod(shape)) * pieces[0].dtype.itemsize
    return pl.pallas_call(
        functools.partial(place_kernel, axis=axis),
        grid_spec=pltpu.PrefetchScalarGridSpec(
            num_scalar_prefetch=1,
            grid=(),
            in_specs=[pl.BlockSpec(memory_space=pltpu.VMEM)] * len(pieces),
            out_specs=pl.BlockSpec(memory_space=pl.ANY),
            scratch_shapes=[pltpu.SemaphoreType.DMA((len(pieces),))],
        ),
        compiler_params=pltpu.CompilerParams(vmem_limit_bytes=32 * 2**20),
        out_shape=jax.ShapeDtypeStruct(tuple(shape), pieces[0].dtype),
        cost_estimate=pl.CostEstimate(flops=0, bytes_accessed=2 * size, transcendentals=0),
    )(jnp.stack(offsets).astype(jnp.int32), *pieces)


def widen_kernel(where, *refs, group):
    *shares, out = refs
    count, core = (len(shares) + 1) // 2, where[1]
    piece = shares[0].shape[2]
    for d in range(count):
        plane = lax.rem(where[0] + count - d, count)
        batch, part = plane // group, lax.rem(plane, group)
        for j in range(CORES):
            got = shares[d][j].astype(F32)
            if d:
                got = got + shares[2 * count - 1 - d][j].astype(F32)
            k = core if j == 0 else 1 - core
            at = pl.multiple_of((k * group + part) * piece, piece)
            out[batch, :, pl.ds(at, piece)] = got


def widen(shares, feat_rank, core, micro, group, width):
    _, block, piece = shares[0].shape
    tile = 128
    return pl.pallas_call(
        functools.partial(widen_kernel, group=group),
        grid_spec=pltpu.PrefetchScalarGridSpec(
            num_scalar_prefetch=1,
            grid=(block // tile,),
            in_specs=[pl.BlockSpec((CORES, tile, piece), lambda i, w: (0, i, 0))] * len(shares),
            out_specs=pl.BlockSpec((micro, tile, width), lambda i, w: (0, i, 0)),
        ),
        out_shape=jax.ShapeDtypeStruct((micro, block, width), F32),
        compiler_params=pltpu.CompilerParams(vmem_limit_bytes=48 * 2**20),
    )(jnp.stack([feat_rank, core]).astype(jnp.int32), *shares)


def on_device(
    tokens,
    cotangent,
    lengths,
    w_query,
    w_key,
    w_value,
    w_output,
    w_gate,
    w_up,
    w_down,
    gain_mixer,
    gain_mlp,
):
    micro, block, width = tokens.shape
    seq_count, feat_count = lax.axis_size("seq"), lax.axis_size("feat")
    seq_rank, feat_rank = lax.axis_index("seq"), lax.axis_index("feat")
    group = feat_count // micro
    ranks = CORES * group
    chips = seq_count // CORES
    chip, core = seq_rank // CORES, seq_rank % CORES
    batch, part = feat_rank // group, feat_rank % group
    rank = core * group + part
    rows = CORES * block
    piece = width // ranks
    heads = HEADS // ranks

    def move(value, target):
        pairs = []
        for s in range(seq_count):
            for f in range(feat_count):
                here = (s // CORES, s % CORES, f // group, f % group)
                there = target(*here)
                if there is not None and there != here:
                    c2, k2, m2, l2 = there
                    pairs.append(
                        (s * feat_count + f, (c2 * CORES + k2) * feat_count + m2 * group + l2)
                    )
        return lax.ppermute(value, ("seq", "feat"), pairs)

    def to_core(value):
        return move(value, lambda c, k, m, l: (c, 1 - k, m, l))

    def to_part(value, d):
        return move(value, lambda c, k, m, l: (c, k, m, l ^ d))

    def to_chip(value, mask):
        return move(value, lambda c, k, m, l: (c ^ mask, k, m, l))

    def shift_chip(value, d):
        return move(value, lambda c, k, m, l: (c + d, k, m, l) if 0 <= c + d < chips else None)

    def spread(value):
        moved = move(value, lambda c, k, m, l: (c, m, k, l))
        other = move(value, lambda c, k, m, l: (c, m, 1 - k, l))
        return jnp.where(core == batch, value, moved), other

    def unspread(same, other):
        moved = move(same, lambda c, k, m, l: (c, m, k, l))
        other = move(other, lambda c, k, m, l: (c, 1 - m, k, l))
        return jnp.where(core == batch, same, moved), other

    def ordered(first_if_zero, second_if_zero, bit, axis):
        return jnp.where(
            bit == 0,
            jnp.concatenate([first_if_zero, second_if_zero], axis),
            jnp.concatenate([second_if_zero, first_if_zero], axis),
        )

    chip_groups = [[c * CORES + k for c in range(chips)] for k in range(CORES)]

    bits = [1 << i for i in range(chips.bit_length() - 1)]
    orders = (bits, bits[::-1])

    def all_hops(owns):
        helds = [{0: own} for own in owns]
        for held, order in zip(helds, orders):
            for bit in order:
                for mask in list(held):
                    held[mask | bit] = to_chip(held[mask], bit)
        return helds

    def straight(owns):
        return [
            {mask: to_chip(own, mask) if mask else own for mask in range(chips)} for own in owns
        ]

    def place_chips(helds, axis):
        size = helds[0][0].shape[axis]
        pieces, offsets = [], []
        for held, k in zip(helds, (batch, 1 - batch)):
            for mask, got in held.items():
                pieces.append(got)
                offsets.append(((chip ^ mask) * CORES + k) * size)
        return place(pieces, offsets, axis)

    def gather_chips_bulk(owns, axis):
        size = owns[0].shape[axis]
        both = place(list(owns), [batch * size, (1 - batch) * size], axis)
        return lax.all_gather(
            both, "seq", axis=axis, tiled=True, axis_index_groups=chip_groups
        )

    def sum_chips(value, axis):
        return lax.psum_scatter(
            value, "seq", scatter_dimension=axis, tiled=True, axis_index_groups=chip_groups
        )

    def send_halves(mine, axis):
        size = mine.shape[axis] // CORES
        same = lax.dynamic_slice_in_dim(mine, batch * size, size, axis)
        other = lax.dynamic_slice_in_dim(mine, (1 - batch) * size, size, axis)
        return unspread(same, other)

    def add(halves):
        return halves[0].astype(F32) + halves[1].astype(F32)

    def send_parts(own):
        return [to_part(own, d) for d in range(1, group)]

    def gather_ranks(own, arrived):
        found = []
        for d, here in enumerate([own, *arrived]):
            found.append((core * group + (part ^ d), here))
            found.append(((1 - core) * group + (part ^ d), to_core(here)))
        return found

    def reduce_part(partial, d):
        away = to_core(partial((1 - core) * group + (part ^ d)).astype(BF))
        return partial(core * group + (part ^ d)) + away.astype(F32)

    def reduce_away(partial):
        return [reduce_part(partial, d).astype(BF) for d in range(1, group)]

    def reduce_send(totals):
        return [to_part(total, d + 1) for d, total in enumerate(totals)]

    def reduce_end(own, arrived):
        return sum((got.astype(F32) for got in arrived), own)

    def sum_ranks(value):
        for d in [1 << i for i in range(group.bit_length() - 1)]:
            value = value + to_part(value, d)
        return value + to_core(value)

    def row_piece(value, r):
        return lax.dynamic_slice_in_dim(value, r * piece, piece, 0)

    def column_piece(value, r):
        return lax.dynamic_slice_in_dim(value, r * piece, piece, 1)

    def chip_tokens(value):
        own = lax.dynamic_index_in_dim(value, batch, 0, False)
        return place([own, to_core(own)], [core * block, (1 - core) * block], 0)

    tokens_c = chip_tokens(tokens)
    grad_out = chip_tokens(cotangent)

    def half(value, k):
        return lax.dynamic_slice_in_dim(value, k * block, block, 0)

    qk_width, v_width = heads * QK, heads * HEAD_V
    qkv_owns = spread(jnp.concatenate([w_query, w_key, w_value], 1))
    gains = lax.all_gather(jnp.stack([gain_mixer, gain_mlp]), "seq", axis=1, tiled=True)
    w_output, gains, *qkv_owns = tie(w_output, gains, *qkv_owns)
    gains = gains.astype(F32)
    mixer_gain, mlp_gain = gains[0], gains[1]
    output_owns = spread(w_output)
    qkv_full = place_chips(all_hops(qkv_owns), 0)
    w_gate, qkv_full, output_owns = tie(w_gate.T, qkv_full, output_owns)
    gate_owns = spread(w_gate)

    bounds = jnp.cumsum(lax.dynamic_index_in_dim(lengths, batch, 0, False))

    def segment_of(p):
        return jnp.sum((p[..., None] >= bounds).astype(jnp.int32), axis=-1)

    start = chip * rows
    base = start + block * jnp.arange(CORES + 1, dtype=jnp.int32)
    edges = jnp.where(base == 0, -1, segment_of(base - 1))
    keep = (edges[1:] == edges[:-1]).astype(F32)
    base = base[:-1]
    ends = jnp.concatenate([jnp.zeros((1,), jnp.int32), bounds])
    open_end = jnp.where((edges[:-1] < 0) | (edges[:-1] > 2), 0, ends[edges[:-1] + 1] - base)
    tail_start = jnp.where(edges[1:] > 2, block, ends[edges[1:]] - base)
    marks = jnp.concatenate(
        [bounds[None, :] - base[:, None], open_end[:, None], tail_start[:, None]], 1
    ).astype(jnp.int32)

    tokens_f = tokens_c.astype(F32)
    inv_one = lax.rsqrt(jnp.mean(tokens_f * tokens_f, axis=-1, keepdims=True) + EPS)
    normed = (tokens_f * inv_one * mixer_gain).astype(BF)
    qkv = dot(normed, qkv_full).astype(BF)

    query, keys = qkv[:, :qk_width], qkv[:, qk_width : 2 * qk_width]
    values = qkv[:, 2 * qk_width :]
    local_states, mixer, grad_states, mixer_back = mixer_calls(heads, block, CORES)

    def pack(state, total):
        total = jnp.pad(total, ((0, 0), (0, -NFEAT % HEAD_V))).reshape(-1, HEAD_V)
        return jnp.concatenate([state.reshape(-1, HEAD_V), total], 0).astype(BF)

    def unpack(flat):
        cut = heads * NFEAT
        return (
            flat[:cut].reshape(heads, NFEAT, HEAD_V).astype(F32),
            flat[cut:].reshape(heads, -1)[:, :NFEAT].astype(F32),
        )

    def scan_blocks(both, blocks_order, step, meanwhile):
        state, total = both[..., :HEAD_V], both[..., HEAD_V]
        at_end = (state[blocks_order[0]], total[blocks_order[0]])
        for i in blocks_order[1:]:
            carry_keep = keep[i]
            at_end = (
                state[i] + carry_keep * at_end[0],
                total[i] + carry_keep * at_end[1],
            )
        message = pack(*at_end)
        run = None
        arrived = [shift_chip(message, step * d) for d in range(1, chips)]
        *arrived, state, total, meanwhile = tie(*arrived, state, total, meanwhile)
        for d in range(1, chips):
            got = unpack(arrived[d - 1])
            other = chip - step * d
            if step > 0:
                same = edges[0] == segment_of((other + 1) * rows - 1)
            else:
                same = edges[CORES] == segment_of(other * rows - 1)
            weight = (same & (other >= 0) & (other < chips)).astype(F32)
            term = (weight * got[0], weight * got[1])
            run = term if run is None else (run[0] + term[0], run[1] + term[1])
        found = {}
        for i in blocks_order:
            found[i] = run
            run = (state[i] + keep[i] * run[0], total[i] + keep[i] * run[1])
        state, total = (jnp.stack([found[i][j] for i in range(CORES)]) for j in range(2))
        total = jnp.broadcast_to(total[..., None], state.shape)
        both = jnp.concatenate([state, total], -1).astype(BF)
        both = jnp.pad(both, ((0, 0), (0, 0), (0, LANES - NFEAT), (0, 0)))
        return both, meanwhile

    (local,) = local_states(marks, keys, values)
    states, gate_owns = scan_blocks(local, list(range(CORES)), 1, gate_owns)
    w_up, states, output_owns = tie(w_up.T, states, output_owns)
    up_owns = spread(w_up)
    gate_full = gather_chips_bulk(gate_owns, 1)
    mixer_own, denom = mixer(marks, query, keys, values, states)
    mixer_own, up_owns = tie(mixer_own, up_owns)

    arrived = send_parts(mixer_own)
    up_full = gather_chips_bulk(up_owns, 1)
    output_full = place_chips(all_hops(output_owns), 0)
    w_down, mixer_own = tie(w_down, mixer_own)
    down_owns = spread(w_down)
    mixer_parts = gather_ranks(mixer_own, arrived)
    branch_own = sum(dot(got, row_piece(output_full, r)) for r, got in mixer_parts).astype(BF)
    branch_own, down_owns = tie(branch_own, down_owns)
    arrived = send_parts(branch_own)
    downs = straight(down_owns)
    *arrived, gate_full = tie(*arrived, gate_full)
    branch_parts = gather_ranks(branch_own, arrived)
    branch = place([got for _, got in branch_parts], [r * piece for r, _ in branch_parts], 1)
    hidden_state = tokens_f + branch.astype(F32)
    inv_two = lax.rsqrt(jnp.mean(hidden_state * hidden_state, axis=-1, keepdims=True) + EPS)
    normed_two = (hidden_state * inv_two * mlp_gain).astype(BF)

    gate = dot(normed_two, gate_full, 1, 1).astype(BF)
    upward = dot(normed_two, up_full, 1, 1).astype(BF)
    hidden = jax.nn.silu(gate.astype(F32)) * upward.astype(F32)
    hidden = hidden.astype(BF)
    down_sum = dot(hidden, grad_out, 0, 0).astype(BF)
    downs, gate, upward, hidden, down_sum = tie(downs, gate, upward, hidden, down_sum)
    down_sum = sum_chips(down_sum, 1)
    down_full = place_chips(downs, 1)
    gate, upward = gate.astype(F32), upward.astype(F32)
    grad_hidden = dot(grad_out, down_full, 1, 1).astype(BF).astype(F32)
    logistic = jax.nn.sigmoid(gate)
    activated = gate * logistic
    grad_gate_f = grad_hidden * upward * logistic * (1.0 + gate * (1.0 - logistic))
    grad_up_f = grad_hidden * activated
    grad_gate_b, grad_up_b = grad_gate_f.astype(BF), grad_up_f.astype(BF)
    inner_two = sum_ranks(jnp.sum(grad_gate_f * gate + grad_up_f * upward, axis=1)) / width
    def hidden_part(grads, r):
        return dot(grads[0], column_piece(gate_full, r)) + dot(grads[1], column_piece(up_full, r))

    grads = (grad_gate_b, grad_up_b)
    totals = reduce_away(functools.partial(hidden_part, grads))
    inner_two, totals, grads = tie(inner_two, totals, grads)
    arrived = reduce_send(totals)
    own = reduce_part(functools.partial(hidden_part, grads), 0)
    up_sum = sum_chips(dot(grads[1], normed_two, 0, 0).astype(BF), 1)
    gate_sum = dot(grads[0], normed_two, 0, 0).astype(BF)
    own, gate_sum, arrived, down_sum = tie(own, gate_sum, arrived, down_sum)
    normed_grad = reduce_end(own, arrived)
    down_halves = send_halves(down_sum, 1)
    gate_sum = sum_chips(gate_sum, 1)
    tokens_own = column_piece(tokens_c, rank).astype(F32)
    hidden_own = tokens_own + branch_own.astype(F32)
    scaled_two = hidden_own * inv_two
    mlp_gain_own = lax.dynamic_slice_in_dim(mlp_gain, rank * piece, piece, 0)
    hidden_grad = column_piece(grad_out, rank).astype(F32) + inv_two * (
        normed_grad * mlp_gain_own - scaled_two * inner_two[:, None]
    )
    grad_gain_mlp = jnp.sum(normed_grad * scaled_two, axis=0)
    branch_grad = hidden_grad.astype(BF)

    def output_part(grad, r):
        return dot(grad, row_piece(output_full, r), 1, 1)

    totals = reduce_away(functools.partial(output_part, branch_grad))
    totals, branch_grad, hidden = tie(totals, branch_grad, hidden)
    arrived = reduce_send(totals)
    own = reduce_part(functools.partial(output_part, branch_grad), 0)

    def down_part(r):
        return dot(hidden, column_piece(down_full, r))

    mlp_totals, mlp_own = reduce_away(down_part), reduce_part(down_part, 0)
    arrived, own, mlp_own, mlp_totals, down_halves, up_sum = tie(
        arrived, own, mlp_own, mlp_totals, down_halves, up_sum
    )
    mixer_grad = reduce_end(own, arrived)
    mlp_arrived = reduce_send(mlp_totals)
    (grad_local,) = grad_states(marks, query, mixer_grad, mixer_own, denom)
    grad_local, branch_grad = tie(grad_local, branch_grad)
    output_sum = place(
        [dot(got, branch_grad, 0, 0).astype(BF) for _, got in mixer_parts],
        [r * piece for r, _ in mixer_parts],
        0,
    )
    carried, output_sum = scan_blocks(
        grad_local, list(range(CORES))[::-1], -1, output_sum
    )
    carried, output_sum, gate_sum, up_sum, mlp_arrived = tie(
        carried, output_sum, gate_sum, up_sum, mlp_arrived
    )
    up_halves = send_halves(up_sum, 1)
    output_sum = sum_chips(output_sum, 0)
    grad_qkv = mixer_back(
        marks, query, keys, values, mixer_grad, mixer_own, denom, states, carried
    )
    grad_qkv, up_halves = tie(grad_qkv, up_halves)
    grad_qkv = jnp.concatenate(grad_qkv, 1)
    inner_one = jnp.sum(grad_qkv.astype(F32) * qkv.astype(F32), axis=1)
    inner_one = sum_ranks(inner_one) / width

    def input_part(grad, r):
        return dot(grad, row_piece(qkv_full, r), 1, 1)

    totals = reduce_away(functools.partial(input_part, grad_qkv))
    totals, grad_qkv, inner_one = tie(totals, grad_qkv, inner_one)
    arrived = reduce_send(totals)
    mixed_own = (hidden_own + reduce_end(mlp_own, mlp_arrived)).astype(BF)
    mixed_halves = unspread(half(mixed_own, batch), half(mixed_own, 1 - batch))
    own = reduce_part(functools.partial(input_part, grad_qkv), 0)
    qkv_sum = dot(normed, grad_qkv, 0, 0).astype(BF)
    arrived, own, mixed_halves, qkv_sum, output_sum = tie(
        arrived, own, mixed_halves, qkv_sum, output_sum
    )
    input_normed = reduce_end(own, arrived)
    qkv_sum = sum_chips(qkv_sum, 0)
    mixed = ordered(mixed_halves[0][None], mixed_halves[1][None], core, 0)
    scaled_one = tokens_own * inv_one
    mixer_gain_own = lax.dynamic_slice_in_dim(mixer_gain, rank * piece, piece, 0)
    grad_gain_mixer = jnp.sum(input_normed * scaled_one, axis=0)
    input_own = (
        hidden_grad
        + inv_one * (input_normed * mixer_gain_own - scaled_one * inner_one[:, None])
    ).astype(BF)

    gain_grads = lax.dynamic_update_slice_in_dim(
        jnp.zeros((2, width), F32), jnp.stack([grad_gain_mixer, grad_gain_mlp]), rank * piece, 1
    )
    other_half = to_core(half(input_own, 1 - core))
    input_own, other_half = tie(input_own, other_half)
    input_pair = jnp.stack([half(input_own, core), other_half])
    input_pair, gain_grads = tie(input_pair, gain_grads)
    planes = [
        move(gain_grads, lambda c, k, m, l: (c, k, *divmod((m * group + l) ^ d, group)))
        for d in range(1, feat_count)
    ]

    def step_plane(value, step, first):
        def target(c, k, m, l):
            here = m * group + l
            behind = here if step > 0 else feat_count - 1 - here
            if behind < first or behind == feat_count - 1:
                return None
            return (c, k, *divmod(here + step, group))

        return move(value, target)

    hops = [to_core] + [
        functools.partial(to_chip, mask=1 << i) for i in range(chips.bit_length() - 1)
    ]
    ups, downs = [input_pair], [input_pair]
    for d in range(feat_count - 1):
        up, down = step_plane(ups[-1], 1, d), step_plane(downs[-1], -1, d)
        if d == 0:
            up, down, planes, output_sum = tie(up, down, planes, output_sum)
            output_halves = send_halves(output_sum, 0)
            gain_grads = sum(planes, gain_grads)
        elif hops:
            up, down, gain_grads, got = tie(up, down, gain_grads, hops[0](gain_grads))
            gain_grads, hops = gain_grads + got, hops[1:]
        if d == feat_count - 3:
            up, down, gate_sum, qkv_sum = tie(up, down, gate_sum, qkv_sum)
            gate_halves, qkv_halves = send_halves(gate_sum, 1), send_halves(qkv_sum, 0)
        ups.append(up), downs.append(down)
    for hop in hops:
        gain_grads = gain_grads + hop(gain_grads)
    input_grad = widen(ups + downs[1:], feat_rank, core, micro, group, width)
    input_grad, gate_halves = tie(input_grad, gate_halves)

    shard = width // seq_count
    gain_grads = lax.dynamic_slice_in_dim(gain_grads, seq_rank * shard, shard, 1)

    grad_qkv_w = add(qkv_halves)
    return (
        mixed,
        input_grad,
        grad_qkv_w[:, :qk_width],
        grad_qkv_w[:, qk_width : 2 * qk_width],
        grad_qkv_w[:, 2 * qk_width :],
        add(output_halves),
        add(gate_halves).T,
        add(up_halves).T,
        add(down_halves),
        gain_grads[0],
        gain_grads[1],
    )


def solution(mesh):
    in_specs = (
        P(None, "seq", None),
        P(None, "seq", None),
        P(),
        P("seq", "feat"),
        P("seq", "feat"),
        P("seq", "feat"),
        P("seq", "feat"),
        P("seq", "feat"),
        P("seq", "feat"),
        P("feat", "seq"),
        P("seq"),
        P("seq"),
    )
    out_specs = (
        P(None, "seq", "feat"),
        P(None, "seq", None),
        P("seq", "feat"),
        P("seq", "feat"),
        P("seq", "feat"),
        P("seq", "feat"),
        P("seq", "feat"),
        P("seq", "feat"),
        P("feat", "seq"),
        P("seq"),
        P("seq"),
    )
    return jax.shard_map(
        on_device, mesh=mesh, in_specs=in_specs, out_specs=out_specs, check_vma=False
    )
```

```python
import functools

import jax
import jax.numpy as jnp
import numpy as np
from jax import lax
from jax.experimental import pallas as pl
from jax.experimental.pallas import tpu as pltpu
from jax.sharding import PartitionSpec as P

HEADS = 16
HEAD_V = 128
QK = 16
NFEAT = 160
CORES = 2
EPS = 1e-05
BF = jnp.bfloat16
F32 = jnp.float32


LANES = 256
TILE = 256


def feature_tables(heads):
    left, right, scale = [-1], [-1], [1.0]
    for i in range(QK):
        left.append(i), right.append(-1), scale.append(1.0)
    for i in range(QK):
        for j in range(i, QK):
            left.append(i), right.append(j), scale.append(1.0 if i < j else 0.7071067811865476)
    padding = LANES - len(left)
    left, right, scale = left + [-2] * padding, right + [-2] * padding, scale + [0.0] * padding
    both = np.array(left + right)
    pick = np.zeros((heads * QK, heads, 2 * LANES), np.float32)
    for h in range(heads):
        pick[h * QK : (h + 1) * QK, h] = 0.5 * (np.arange(QK)[:, None] == both[None, :])
    ones = (both == -1).astype(np.float32)[None]
    own = np.zeros((8, heads * QK), np.float32)
    for h in range(heads):
        own[h, h * QK : (h + 1) * QK] = 0.25
    return (
        jnp.asarray(pick.reshape(heads * QK, -1), BF),
        jnp.asarray(ones),
        jnp.asarray(np.array(scale, np.float32)[None]),
        jnp.asarray(own, BF),
    )


def nt(a, b):
    return lax.dot_general(a, b, (((1,), (1,)), ((), ())), preferred_element_type=F32)


def tn(a, b):
    return lax.dot_general(a, b, (((0,), (0,)), ((), ())), preferred_element_type=F32)


def nn(a, b):
    return lax.dot_general(a, b, (((1,), (0,)), ((), ())), preferred_element_type=F32)


class Marks:
    def __init__(self, marks, b, block):
        t = lax.broadcasted_iota(jnp.int32, (block, 1), 0)
        first, second, third = marks[b, 0], marks[b, 1], marks[b, 2]
        low = jnp.where(t >= first, first, 0)
        low = jnp.where(t >= second, second, low)
        self.low = jnp.where(t >= third, block, low)
        self.padding = jnp.where(t >= third, 1.0, 0.0).astype(F32)
        self.use = jnp.where(t < marks[b, 3], 1.0, 0.0).astype(F32)
        self.tail = jnp.where(t >= marks[b, 4], 1.0, 0.0).astype(F32)

    def mask(self, at, count):
        t = lax.broadcasted_iota(jnp.int32, (TILE, count), 0) + at
        s = lax.broadcasted_iota(jnp.int32, (TILE, count), 1)
        return (s <= t) & (s >= self.low[at : at + TILE])


def sides(x, pick, ones, h):
    both = nn(x, pick[:, 2 * LANES * h : 2 * LANES * (h + 1)]) + ones
    return both[:, :LANES], both[:, LANES:]


def head_cols(ref, h):
    return ref[:, HEAD_V * h : HEAD_V * (h + 1)]


def output_grads(do_ref, o_ref, den_ref, h):
    do, o, den = head_cols(do_ref, h), head_cols(o_ref, h).astype(F32), head_cols(den_ref, h)
    do = do.astype(F32)
    inverse = 1.0 / den
    dnum = (do * inverse).astype(BF)
    dden = -jnp.sum(do * o, axis=1, keepdims=True) * inverse
    return dnum, dden


def state_kernel(marks, k_ref, v_ref, pick, ones, scale, out_ref, *, heads, block):
    m = Marks(marks, pl.program_id(0), block)
    k = k_ref[...]
    for h in range(heads):
        left, right = sides(k, pick, ones[...], h)
        feat = (left * right * (scale[...] * m.tail)).astype(BF)
        v = head_cols(v_ref, h)
        out_ref[0, h] = tn(feat, jnp.concatenate([v, jnp.ones_like(v)], 1))[:NFEAT]


def grad_state_kernel(
    marks, q_ref, do_ref, o_ref, den_ref, pick, ones, scale, out_ref, *, heads, block
):
    m = Marks(marks, pl.program_id(0), block)
    q = q_ref[...]
    for h in range(heads):
        left, right = sides(q, pick, ones[...], h)
        feat = (left * right * (scale[...] * m.use)).astype(BF)
        dnum, dden = output_grads(do_ref, o_ref, den_ref, h)
        out_ref[0, h] = tn(feat, jnp.concatenate([dnum, dden.astype(BF)], 1))[:NFEAT]


def mixer_kernel(
    marks, q_ref, k_ref, v_ref, s_ref, pick, ones, scale, own, o_ref, den_ref, *, heads, block
):
    m = Marks(marks, pl.program_id(0), block)
    q, k = q_ref[...], k_ref[...]
    for h in range(heads):
        q_own = q * own[h : h + 1, :]
        left, right = sides(q, pick, ones[...], h)
        feat = (left * right * scale[...]).astype(BF)
        before = nn(feat, s_ref[0, h]) * m.use
        v = head_cols(v_ref, h)
        v_one = jnp.concatenate([v, jnp.ones_like(v)], 1)
        for at in range(0, block, TILE):
            count = at + TILE
            prod = nt(q_own[at:count], k[:count])
            score = 1.0 + prod + 0.5 * prod * prod
            score = jnp.where(m.mask(at, count), score, 0.0).astype(BF)
            both = nn(score, v_one[:count]) + before[at:count]
            den = both[:, HEAD_V:] + m.padding[at:count]
            here = (slice(at, count), slice(HEAD_V * h, HEAD_V * (h + 1)))
            o_ref[here] = (both[:, :HEAD_V] / den).astype(BF)
            den_ref[here] = den


def mixer_back_kernel(
    marks,
    q_ref,
    k_ref,
    v_ref,
    do_ref,
    o_ref,
    den_ref,
    s_ref,
    g_ref,
    pick,
    ones,
    scale,
    own,
    dq_ref,
    dk_ref,
    dv_ref,
    dq,
    dk,
    dv,
    *,
    heads,
    block,
):
    m = Marks(marks, pl.program_id(0), block)
    q, k = q_ref[...], k_ref[...]
    first_lane = lax.broadcasted_iota(jnp.int32, (block, HEAD_V), 1) == 0
    dq[...] = jnp.zeros_like(dq)
    dk[...] = jnp.zeros_like(dk)
    for h in range(heads):
        table = pick[:, 2 * LANES * h : 2 * LANES * (h + 1)]
        q_own, k_own = q * own[h : h + 1, :], k * own[h : h + 1, :]
        v = head_cols(v_ref, h)
        dnum, dden = output_grads(do_ref, o_ref, den_ref, h)
        state, carried = s_ref[0, h], g_ref[0, h]

        left, right = sides(q, pick, ones[...], h)
        wide = jnp.concatenate([dnum, jnp.where(first_lane, dden, 0.0).astype(BF)], 1)
        dfeat = nt(wide, state) * (scale[...] * m.use)
        pulled = jnp.concatenate([(dfeat * right).astype(BF), (dfeat * left).astype(BF)], 1)
        dq[...] += nt(pulled, table)

        left, right = sides(k, pick, ones[...], h)
        wide = jnp.concatenate([v, jnp.where(first_lane, 1.0, 0.0).astype(BF)], 1)
        dfeat = nt(wide, carried) * (scale[...] * m.tail)
        pulled = jnp.concatenate([(dfeat * right).astype(BF), (dfeat * left).astype(BF)], 1)
        dk[...] += nt(pulled, table)
        feat = (left * right * (scale[...] * m.tail)).astype(BF)
        dv[...] = nn(feat, carried[:, :HEAD_V])

        for at in range(0, block, TILE):
            count = at + TILE
            prod = nt(q_own[at:count], k[:count])
            one = 1.0 + prod
            mask = m.mask(at, count)
            score = jnp.where(mask, one + 0.5 * prod * prod, 0.0).astype(BF)
            dscore = nt(dnum[at:count], v[:count]) + dden[at:count, :1]
            dprod = jnp.where(mask, dscore * one, 0.0).astype(BF)
            dq[at:count] += nn(dprod, k_own[:count])
            dk[:count] += tn(dprod, q_own[at:count])
            dv[:count] += tn(score, dnum[at:count])
        dv_ref[:, HEAD_V * h : HEAD_V * (h + 1)] = dv[...].astype(BF)
    dq_ref[...] = dq[...].astype(BF)
    dk_ref[...] = dk[...].astype(BF)


def mixer_calls(heads, block, blocks):
    tables = feature_tables(heads)
    narrow = pl.BlockSpec((block, heads * QK), lambda b, marks: (b, 0))
    wide = pl.BlockSpec((block, heads * HEAD_V), lambda b, marks: (b, 0))
    local = pl.BlockSpec((1, heads, NFEAT, 2 * HEAD_V), lambda b, marks: (b, 0, 0, 0))
    state = pl.BlockSpec((1, heads, LANES, 2 * HEAD_V), lambda b, marks: (b, 0, 0, 0))
    fixed = [pl.BlockSpec(t.shape, lambda b, marks: (0, 0)) for t in tables]
    rows = block * blocks

    def call(kernel, specs, used, outs, scratch, cost):
        def run(marks, *args):
            return pl.pallas_call(
                functools.partial(kernel, heads=heads, block=block),
                grid_spec=pltpu.PrefetchScalarGridSpec(
                    num_scalar_prefetch=1,
                    grid=(blocks,),
                    in_specs=specs + fixed[:used],
                    out_specs=[o[0] for o in outs],
                    scratch_shapes=scratch,
                ),
                out_shape=[jax.ShapeDtypeStruct(*o[1:]) for o in outs],
                cost_estimate=pl.CostEstimate(
                    flops=cost * rows * heads, bytes_accessed=rows * heads * 1500, transcendentals=0
                ),
                compiler_params=pltpu.CompilerParams(vmem_limit_bytes=48 * 2**20),
            )(marks, *args, *tables[:used])

        return run

    local_out = (local, (blocks, heads, NFEAT, 2 * HEAD_V), F32)
    wide_b, wide_f = (wide, (rows, heads * HEAD_V), BF), (wide, (rows, heads * HEAD_V), F32)
    narrow_b = (narrow, (rows, heads * QK), BF)
    scratch = [
        pltpu.VMEM((block, heads * QK), F32),
        pltpu.VMEM((block, heads * QK), F32),
        pltpu.VMEM((block, HEAD_V), F32),
    ]
    return (
        call(state_kernel, [narrow, wide], 3, [local_out], [], 500000),
        call(mixer_kernel, [narrow, narrow, wide, state], 4, [wide_b, wide_f], [], 1000000),
        call(grad_state_kernel, [narrow, wide, wide, wide], 3, [local_out], [], 500000),
        call(
            mixer_back_kernel,
            [narrow, narrow, wide, wide, wide, wide, state, state],
            4,
            [narrow_b, narrow_b, wide_b],
            scratch,
            2500000,
        ),
    )


def dot(a, b, ca=1, cb=0):
    return lax.dot_general(a, b, (((ca,), (cb,)), ((), ())), preferred_element_type=F32)


def tie(*values):
    return lax.optimization_barrier(values)


def place_kernel(offsets, *refs, axis):
    *pieces, out, sems = refs
    copies = []
    for i, piece in enumerate(pieces):
        size = piece.shape[axis]
        span = pl.ds(pl.multiple_of(offsets[i], size), size)
        target = out.at[span] if axis == 0 else out.at[:, span]
        copies.append(pltpu.make_async_copy(piece, target, sems.at[i]))
    for copy in copies:
        copy.start()
    for copy in copies:
        copy.wait()


def place(pieces, offsets, axis):
    shape = list(pieces[0].shape)
    shape[axis] = sum(p.shape[axis] for p in pieces)
    size = int(np.prod(shape)) * pieces[0].dtype.itemsize
    return pl.pallas_call(
        functools.partial(place_kernel, axis=axis),
        grid_spec=pltpu.PrefetchScalarGridSpec(
            num_scalar_prefetch=1,
            grid=(),
            in_specs=[pl.BlockSpec(memory_space=pltpu.VMEM)] * len(pieces),
            out_specs=pl.BlockSpec(memory_space=pl.ANY),
            scratch_shapes=[pltpu.SemaphoreType.DMA((len(pieces),))],
        ),
        compiler_params=pltpu.CompilerParams(vmem_limit_bytes=32 * 2**20),
        out_shape=jax.ShapeDtypeStruct(tuple(shape), pieces[0].dtype),
        cost_estimate=pl.CostEstimate(flops=0, bytes_accessed=2 * size, transcendentals=0),
    )(jnp.stack(offsets).astype(jnp.int32), *pieces)


def widen_kernel(where, *refs, group):
    *shares, out = refs
    count, core = (len(shares) + 1) // 2, where[1]
    piece = shares[0].shape[2]
    for d in range(count):
        plane = lax.rem(where[0] + count - d, count)
        batch, part = plane // group, lax.rem(plane, group)
        for j in range(CORES):
            got = shares[d][j].astype(F32)
            if d:
                got = got + shares[2 * count - 1 - d][j].astype(F32)
            k = core if j == 0 else 1 - core
            at = pl.multiple_of((k * group + part) * piece, piece)
            out[batch, :, pl.ds(at, piece)] = got


def widen(shares, feat_rank, core, micro, group, width):
    _, block, piece = shares[0].shape
    tile = 128
    return pl.pallas_call(
        functools.partial(widen_kernel, group=group),
        grid_spec=pltpu.PrefetchScalarGridSpec(
            num_scalar_prefetch=1,
            grid=(block // tile,),
            in_specs=[pl.BlockSpec((CORES, tile, piece), lambda i, w: (0, i, 0))] * len(shares),
            out_specs=pl.BlockSpec((micro, tile, width), lambda i, w: (0, i, 0)),
        ),
        out_shape=jax.ShapeDtypeStruct((micro, block, width), F32),
        cost_estimate=pl.CostEstimate(
            flops=0, bytes_accessed=8 * micro * block * width, transcendentals=0
        ),
        compiler_params=pltpu.CompilerParams(vmem_limit_bytes=48 * 2**20),
    )(jnp.stack([feat_rank, core]).astype(jnp.int32), *shares)


def on_device(
    tokens,
    cotangent,
    lengths,
    w_query,
    w_key,
    w_value,
    w_output,
    w_gate,
    w_up,
    w_down,
    gain_mixer,
    gain_mlp,
):
    micro, block, width = tokens.shape
    seq_count, feat_count = lax.axis_size("seq"), lax.axis_size("feat")
    seq_rank, feat_rank = lax.axis_index("seq"), lax.axis_index("feat")
    group = feat_count // micro
    ranks = CORES * group
    chips = seq_count // CORES
    chip, core = seq_rank // CORES, seq_rank % CORES
    batch, part = feat_rank // group, feat_rank % group
    rank = core * group + part
    rows = CORES * block
    piece = width // ranks
    heads = HEADS // ranks

    def move(value, target):
        pairs = []
        for s in range(seq_count):
            for f in range(feat_count):
                here = (s // CORES, s % CORES, f // group, f % group)
                there = target(*here)
                if there is not None and there != here:
                    c2, k2, m2, l2 = there
                    pairs.append(
                        (s * feat_count + f, (c2 * CORES + k2) * feat_count + m2 * group + l2)
                    )
        return lax.ppermute(value, ("seq", "feat"), pairs)

    def to_core(value):
        return move(value, lambda c, k, m, l: (c, 1 - k, m, l))

    def to_part(value, d):
        return move(value, lambda c, k, m, l: (c, k, m, l ^ d))

    def to_chip(value, mask):
        return move(value, lambda c, k, m, l: (c ^ mask, k, m, l))

    def shift_chip(value, d):
        return move(value, lambda c, k, m, l: (c + d, k, m, l) if 0 <= c + d < chips else None)

    def spread(value):
        moved = move(value, lambda c, k, m, l: (c, m, k, l))
        other = move(value, lambda c, k, m, l: (c, m, 1 - k, l))
        return jnp.where(core == batch, value, moved), other

    def unspread(same, other):
        moved = move(same, lambda c, k, m, l: (c, m, k, l))
        other = move(other, lambda c, k, m, l: (c, 1 - m, k, l))
        return jnp.where(core == batch, same, moved), other

    def ordered(first_if_zero, second_if_zero, bit, axis):
        return jnp.where(
            bit == 0,
            jnp.concatenate([first_if_zero, second_if_zero], axis),
            jnp.concatenate([second_if_zero, first_if_zero], axis),
        )

    chip_groups = [[c * CORES + k for c in range(chips)] for k in range(CORES)]

    bits = [1 << i for i in range(chips.bit_length() - 1)]
    orders = (bits, bits[::-1])

    def all_hops(owns):
        helds = [{0: own} for own in owns]
        for held, order in zip(helds, orders):
            for bit in order:
                for mask in list(held):
                    held[mask | bit] = to_chip(held[mask], bit)
        return helds

    def straight(owns):
        return [
            {mask: to_chip(own, mask) if mask else own for mask in range(chips)} for own in owns
        ]

    def place_chips(helds, axis):
        size = helds[0][0].shape[axis]
        pieces, offsets = [], []
        for held, k in zip(helds, (batch, 1 - batch)):
            for mask, got in held.items():
                pieces.append(got)
                offsets.append(((chip ^ mask) * CORES + k) * size)
        return place(pieces, offsets, axis)

    def gather_chips_bulk(owns, axis):
        size = owns[0].shape[axis]
        both = place(list(owns), [batch * size, (1 - batch) * size], axis)
        return lax.all_gather(
            both, "seq", axis=axis, tiled=True, axis_index_groups=chip_groups
        )

    def sum_chips(value, axis):
        return lax.psum_scatter(
            value, "seq", scatter_dimension=axis, tiled=True, axis_index_groups=chip_groups
        )

    def send_halves(mine, axis):
        size = mine.shape[axis] // CORES
        same = lax.dynamic_slice_in_dim(mine, batch * size, size, axis)
        other = lax.dynamic_slice_in_dim(mine, (1 - batch) * size, size, axis)
        return unspread(same, other)

    def add(halves):
        return halves[0].astype(F32) + halves[1].astype(F32)

    def send_parts(own):
        return [to_part(own, d) for d in range(1, group)]

    def gather_ranks(own, arrived):
        found = []
        for d, here in enumerate([own, *arrived]):
            found.append((core * group + (part ^ d), here))
            found.append(((1 - core) * group + (part ^ d), to_core(here)))
        return found

    def reduce_part(partial, d):
        away = to_core(partial((1 - core) * group + (part ^ d)).astype(BF))
        return partial(core * group + (part ^ d)) + away.astype(F32)

    def reduce_away(partial):
        return [reduce_part(partial, d).astype(BF) for d in range(1, group)]

    def reduce_send(totals):
        return [to_part(total, d + 1) for d, total in enumerate(totals)]

    def reduce_end(own, arrived):
        return sum((got.astype(F32) for got in arrived), own)

    def sum_ranks(value):
        for d in [1 << i for i in range(group.bit_length() - 1)]:
            value = value + to_part(value, d)
        return value + to_core(value)

    def row_piece(value, r):
        return lax.dynamic_slice_in_dim(value, r * piece, piece, 0)

    def column_piece(value, r):
        return lax.dynamic_slice_in_dim(value, r * piece, piece, 1)

    def chip_tokens(value):
        own = lax.dynamic_index_in_dim(value, batch, 0, False)
        return place([own, to_core(own)], [core * block, (1 - core) * block], 0)

    tokens_c = chip_tokens(tokens)
    grad_out = chip_tokens(cotangent)

    def half(value, k):
        return lax.dynamic_slice_in_dim(value, k * block, block, 0)

    qk_width, v_width = heads * QK, heads * HEAD_V
    qkv_owns = spread(jnp.concatenate([w_query, w_key, w_value], 1))
    gains = lax.all_gather(jnp.stack([gain_mixer, gain_mlp]), "seq", axis=1, tiled=True)
    w_output, gains, *qkv_owns = tie(w_output, gains, *qkv_owns)
    gains = gains.astype(F32)
    mixer_gain, mlp_gain = gains[0], gains[1]
    output_owns = spread(w_output)
    qkv_full = place_chips(all_hops(qkv_owns), 0)
    w_gate, qkv_full, output_owns = tie(w_gate.T, qkv_full, output_owns)
    gate_owns = spread(w_gate)

    bounds = jnp.cumsum(lax.dynamic_index_in_dim(lengths, batch, 0, False))

    def segment_of(p):
        return jnp.sum((p[..., None] >= bounds).astype(jnp.int32), axis=-1)

    start = chip * rows
    base = start + block * jnp.arange(CORES + 1, dtype=jnp.int32)
    edges = jnp.where(base == 0, -1, segment_of(base - 1))
    keep = (edges[1:] == edges[:-1]).astype(F32)
    base = base[:-1]
    ends = jnp.concatenate([jnp.zeros((1,), jnp.int32), bounds])
    open_end = jnp.where((edges[:-1] < 0) | (edges[:-1] > 2), 0, ends[edges[:-1] + 1] - base)
    tail_start = jnp.where(edges[1:] > 2, block, ends[edges[1:]] - base)
    marks = jnp.concatenate(
        [bounds[None, :] - base[:, None], open_end[:, None], tail_start[:, None]], 1
    ).astype(jnp.int32)

    tokens_f = tokens_c.astype(F32)
    inv_one = lax.rsqrt(jnp.mean(tokens_f * tokens_f, axis=-1, keepdims=True) + EPS)
    normed = (tokens_f * inv_one * mixer_gain).astype(BF)
    qkv = dot(normed, qkv_full).astype(BF)

    query, keys = qkv[:, :qk_width], qkv[:, qk_width : 2 * qk_width]
    values = qkv[:, 2 * qk_width :]
    local_states, mixer, grad_states, mixer_back = mixer_calls(heads, block, CORES)

    def pack(state, total):
        total = jnp.pad(total, ((0, 0), (0, -NFEAT % HEAD_V))).reshape(-1, HEAD_V)
        return jnp.concatenate([state.reshape(-1, HEAD_V), total], 0).astype(BF)

    def unpack(flat):
        cut = heads * NFEAT
        return (
            flat[:cut].reshape(heads, NFEAT, HEAD_V).astype(F32),
            flat[cut:].reshape(heads, -1)[:, :NFEAT].astype(F32),
        )

    def scan_blocks(both, blocks_order, step, meanwhile):
        state, total = both[..., :HEAD_V], both[..., HEAD_V]
        at_end = (state[blocks_order[0]], total[blocks_order[0]])
        for i in blocks_order[1:]:
            carry_keep = keep[i]
            at_end = (
                state[i] + carry_keep * at_end[0],
                total[i] + carry_keep * at_end[1],
            )
        message = pack(*at_end)
        run = None
        arrived = [shift_chip(message, step * d) for d in range(1, chips)]
        *arrived, state, total, meanwhile = tie(*arrived, state, total, meanwhile)
        for d in range(1, chips):
            got = unpack(arrived[d - 1])
            other = chip - step * d
            if step > 0:
                same = edges[0] == segment_of((other + 1) * rows - 1)
            else:
                same = edges[CORES] == segment_of(other * rows - 1)
            weight = (same & (other >= 0) & (other < chips)).astype(F32)
            term = (weight * got[0], weight * got[1])
            run = term if run is None else (run[0] + term[0], run[1] + term[1])
        found = {}
        for i in blocks_order:
            found[i] = run
            run = (state[i] + keep[i] * run[0], total[i] + keep[i] * run[1])
        state, total = (jnp.stack([found[i][j] for i in range(CORES)]) for j in range(2))
        total = jnp.broadcast_to(total[..., None], state.shape)
        both = jnp.concatenate([state, total], -1).astype(BF)
        both = jnp.pad(both, ((0, 0), (0, 0), (0, LANES - NFEAT), (0, 0)))
        return both, meanwhile

    (local,) = local_states(marks, keys, values)
    states, gate_owns = scan_blocks(local, list(range(CORES)), 1, gate_owns)
    w_up, states, output_owns = tie(w_up.T, states, output_owns)
    up_owns = spread(w_up)
    gate_full = gather_chips_bulk(gate_owns, 1)
    mixer_own, denom = mixer(marks, query, keys, values, states)
    mixer_own, up_owns = tie(mixer_own, up_owns)

    arrived = send_parts(mixer_own)
    up_full = gather_chips_bulk(up_owns, 1)
    output_full = place_chips(all_hops(output_owns), 0)
    w_down, mixer_own = tie(w_down, mixer_own)
    down_owns = spread(w_down)
    mixer_parts = gather_ranks(mixer_own, arrived)
    branch_own = sum(dot(got, row_piece(output_full, r)) for r, got in mixer_parts).astype(BF)
    branch_own, down_owns = tie(branch_own, down_owns)
    arrived = send_parts(branch_own)
    downs = straight(down_owns)
    *arrived, gate_full = tie(*arrived, gate_full)
    branch_parts = gather_ranks(branch_own, arrived)
    branch = place([got for _, got in branch_parts], [r * piece for r, _ in branch_parts], 1)
    hidden_state = tokens_f + branch.astype(F32)
    inv_two = lax.rsqrt(jnp.mean(hidden_state * hidden_state, axis=-1, keepdims=True) + EPS)
    normed_two = (hidden_state * inv_two * mlp_gain).astype(BF)

    gate = dot(normed_two, gate_full, 1, 1).astype(BF)
    upward = dot(normed_two, up_full, 1, 1).astype(BF)
    hidden = jax.nn.silu(gate.astype(F32)) * upward.astype(F32)
    hidden = hidden.astype(BF)
    down_sum = dot(hidden, grad_out, 0, 0).astype(BF)
    downs, gate, upward, hidden, down_sum = tie(downs, gate, upward, hidden, down_sum)
    down_sum = sum_chips(down_sum, 1)
    down_full = place_chips(downs, 1)
    gate, upward = gate.astype(F32), upward.astype(F32)
    grad_hidden = dot(grad_out, down_full, 1, 1).astype(BF).astype(F32)
    logistic = jax.nn.sigmoid(gate)
    activated = gate * logistic
    grad_gate_f = grad_hidden * upward * logistic * (1.0 + gate * (1.0 - logistic))
    grad_up_f = grad_hidden * activated
    grad_gate_b, grad_up_b = grad_gate_f.astype(BF), grad_up_f.astype(BF)
    inner_two = sum_ranks(jnp.sum(grad_gate_f * gate + grad_up_f * upward, axis=1)) / width
    def hidden_part(grads, r):
        return dot(grads[0], column_piece(gate_full, r)) + dot(grads[1], column_piece(up_full, r))

    grads = (grad_gate_b, grad_up_b)
    totals = reduce_away(functools.partial(hidden_part, grads))
    inner_two, totals, grads = tie(inner_two, totals, grads)
    arrived = reduce_send(totals)
    own = reduce_part(functools.partial(hidden_part, grads), 0)
    up_sum = sum_chips(dot(grads[1], normed_two, 0, 0).astype(BF), 1)
    gate_sum = dot(grads[0], normed_two, 0, 0).astype(BF)
    own, gate_sum, arrived, down_sum = tie(own, gate_sum, arrived, down_sum)
    normed_grad = reduce_end(own, arrived)
    down_halves = send_halves(down_sum, 1)
    gate_sum = sum_chips(gate_sum, 1)
    tokens_own = column_piece(tokens_c, rank).astype(F32)
    hidden_own = tokens_own + branch_own.astype(F32)
    scaled_two = hidden_own * inv_two
    mlp_gain_own = lax.dynamic_slice_in_dim(mlp_gain, rank * piece, piece, 0)
    hidden_grad = column_piece(grad_out, rank).astype(F32) + inv_two * (
        normed_grad * mlp_gain_own - scaled_two * inner_two[:, None]
    )
    grad_gain_mlp = jnp.sum(normed_grad * scaled_two, axis=0)
    branch_grad = hidden_grad.astype(BF)

    def output_part(grad, r):
        return dot(grad, row_piece(output_full, r), 1, 1)

    totals = reduce_away(functools.partial(output_part, branch_grad))
    totals, branch_grad, hidden = tie(totals, branch_grad, hidden)
    arrived = reduce_send(totals)
    own = reduce_part(functools.partial(output_part, branch_grad), 0)

    def down_part(r):
        return dot(hidden, column_piece(down_full, r))

    mlp_totals, mlp_own = reduce_away(down_part), reduce_part(down_part, 0)
    arrived, own, mlp_own, mlp_totals, down_halves, up_sum = tie(
        arrived, own, mlp_own, mlp_totals, down_halves, up_sum
    )
    mixer_grad = reduce_end(own, arrived)
    mlp_arrived = reduce_send(mlp_totals)
    (grad_local,) = grad_states(marks, query, mixer_grad, mixer_own, denom)
    grad_local, branch_grad = tie(grad_local, branch_grad)
    output_sum = place(
        [dot(got, branch_grad, 0, 0).astype(BF) for _, got in mixer_parts],
        [r * piece for r, _ in mixer_parts],
        0,
    )
    carried, (mlp_arrived, output_sum) = scan_blocks(
        grad_local, list(range(CORES))[::-1], -1, (mlp_arrived, output_sum)
    )
    carried, output_sum, gate_sum, up_sum = tie(carried, output_sum, gate_sum, up_sum)
    up_halves = send_halves(up_sum, 1)
    output_sum = sum_chips(output_sum, 0)
    grad_qkv = mixer_back(
        marks, query, keys, values, mixer_grad, mixer_own, denom, states, carried
    )
    grad_qkv, up_halves = tie(grad_qkv, up_halves)
    grad_qkv = jnp.concatenate(grad_qkv, 1)
    inner_one = jnp.sum(grad_qkv.astype(F32) * qkv.astype(F32), axis=1)
    inner_one = sum_ranks(inner_one) / width

    def input_part(grad, r):
        return dot(grad, row_piece(qkv_full, r), 1, 1)

    totals = reduce_away(functools.partial(input_part, grad_qkv))
    totals, grad_qkv, inner_one = tie(totals, grad_qkv, inner_one)
    arrived = reduce_send(totals)
    mixed_own = (hidden_own + reduce_end(mlp_own, mlp_arrived)).astype(BF)
    mixed_halves = unspread(half(mixed_own, batch), half(mixed_own, 1 - batch))
    own = reduce_part(functools.partial(input_part, grad_qkv), 0)
    qkv_sum = dot(normed, grad_qkv, 0, 0).astype(BF)
    arrived, own, mixed_halves, qkv_sum, output_sum = tie(
        arrived, own, mixed_halves, qkv_sum, output_sum
    )
    input_normed = reduce_end(own, arrived)
    qkv_sum = sum_chips(qkv_sum, 0)
    mixed = ordered(mixed_halves[0][None], mixed_halves[1][None], core, 0)
    scaled_one = tokens_own * inv_one
    mixer_gain_own = lax.dynamic_slice_in_dim(mixer_gain, rank * piece, piece, 0)
    grad_gain_mixer = jnp.sum(input_normed * scaled_one, axis=0)
    input_own = (
        hidden_grad
        + inv_one * (input_normed * mixer_gain_own - scaled_one * inner_one[:, None])
    ).astype(BF)

    gain_grads = lax.dynamic_update_slice_in_dim(
        jnp.zeros((2, width), F32), jnp.stack([grad_gain_mixer, grad_gain_mlp]), rank * piece, 1
    )
    other_half = to_core(half(input_own, 1 - core))
    input_own, other_half = tie(input_own, other_half)
    input_pair = jnp.stack([half(input_own, core), other_half])
    input_pair, gain_grads = tie(input_pair, gain_grads)
    planes = [
        move(gain_grads, lambda c, k, m, l: (c, k, *divmod((m * group + l) ^ d, group)))
        for d in range(1, feat_count)
    ]

    def step_plane(value, step, first):
        def target(c, k, m, l):
            here = m * group + l
            behind = here if step > 0 else feat_count - 1 - here
            if behind < first or behind == feat_count - 1:
                return None
            return (c, k, *divmod(here + step, group))

        return move(value, target)

    hops = [to_core] + [
        functools.partial(to_chip, mask=1 << i) for i in range(chips.bit_length() - 1)
    ]
    ups, downs = [input_pair], [input_pair]
    for d in range(feat_count - 1):
        up, down = step_plane(ups[-1], 1, d), step_plane(downs[-1], -1, d)
        if d == 0:
            up, down, planes, output_sum = tie(up, down, planes, output_sum)
            output_halves = send_halves(output_sum, 0)
            gain_grads = sum(planes, gain_grads)
        elif hops:
            up, down, gain_grads, got = tie(up, down, gain_grads, hops[0](gain_grads))
            gain_grads, hops = gain_grads + got, hops[1:]
        if d == feat_count - 3:
            up, down, gate_sum, qkv_sum = tie(up, down, gate_sum, qkv_sum)
            gate_halves, qkv_halves = send_halves(gate_sum, 1), send_halves(qkv_sum, 0)
        ups.append(up), downs.append(down)
    for hop in hops:
        gain_grads = gain_grads + hop(gain_grads)
    input_grad = widen(ups + downs[1:], feat_rank, core, micro, group, width)

    shard = width // seq_count
    gain_grads = lax.dynamic_slice_in_dim(gain_grads, seq_rank * shard, shard, 1)

    grad_qkv_w = add(qkv_halves)
    return (
        mixed,
        input_grad,
        grad_qkv_w[:, :qk_width],
        grad_qkv_w[:, qk_width : 2 * qk_width],
        grad_qkv_w[:, 2 * qk_width :],
        add(output_halves),
        add(gate_halves).T,
        add(up_halves).T,
        add(down_halves),
        gain_grads[0],
        gain_grads[1],
    )


def solution(mesh):
    in_specs = (
        P(None, "seq", None),
        P(None, "seq", None),
        P(),
        P("seq", "feat"),
        P("seq", "feat"),
        P("seq", "feat"),
        P("seq", "feat"),
        P("seq", "feat"),
        P("seq", "feat"),
        P("feat", "seq"),
        P("seq"),
        P("seq"),
    )
    out_specs = (
        P(None, "seq", "feat"),
        P(None, "seq", None),
        P("seq", "feat"),
        P("seq", "feat"),
        P("seq", "feat"),
        P("seq", "feat"),
        P("seq", "feat"),
        P("seq", "feat"),
        P("feat", "seq"),
        P("seq"),
        P("seq"),
    )
    return jax.shard_map(
        on_device, mesh=mesh, in_specs=in_specs, out_specs=out_specs, check_vma=False
    )
```
